32 devices in a mesh: groups: 2 (over y), curve: 4 (over z), cross: 2 (over x), sub: 2 (over core).
Axes of the slice: x: 2, y: 2, z: 4, core: 2. Of those that a mesh axis runs over, the one named last changes fastest.
Arguments:
- node_features: bfloat16 [512, 8192], P('sub', ('groups', 'curve', 'cross')), parts along dimension 1, may hold values from -6 to 6
- inward_weight: bfloat16 [2, 512, 1024], P(None, 'sub'), may hold values from -0.1875 to 0.1875
- outward_weight: bfloat16 [2, 512, 512], P(None, 'sub'), may hold values from -0.25 to 0.25
- coarse_weight: bfloat16 [512, 512], P('sub'), may hold values from -0.25 to 0.25
- tile_index: int32 [64, 3], P(('groups', 'curve', 'cross')), parts along dimension 0, may hold values from 0 to 5, as said below
- tile_mask: int32 [64, 3, 128, 128], P(('groups', 'curve', 'cross')), parts along dimension 0, may hold values from 0 to 1, as said below
- send_rows: int32 [16, 2, 128], P(('groups', 'curve', 'cross')), parts along dimension 0, may hold values from 0 to 511, as said below
- parent: int32 [8192], P(('groups', 'curve', 'cross')), parts along dimension 0, may hold values from 0 to 1023, as said below
- cotangent: bfloat16 [512, 8192], P('sub', ('groups', 'curve', 'cross')), parts along dimension 1, may hold values from -6 to 6
Outputs:
- new_features: bfloat16 [512, 8192], P('sub', ('groups', 'curve', 'cross')), parts along dimension 1
- feature_grad: float32 [512, 8192], P('sub', ('groups', 'curve', 'cross')), parts along dimension 1
- grad_inward: float32 [4, 512, 1024], P('groups', 'sub', ('curve', 'cross')), parts along dimension 0
- grad_outward: float32 [4, 512, 512], P('groups', 'sub', ('curve', 'cross')), parts along dimension 0
- grad_coarse: float32 [1024, 512], P(('groups', 'sub'), ('curve', 'cross')), parts along dimension 0
The draws below stay inside these ranges and needn't reach their ends.
There are 2 independent parts, one for each index of `groups`. The reference program is written for one: setup_inputs(seed, part) draws one part's arguments, and reference() takes and returns one part's arrays. A program takes and returns all parts, laid end to end along the dimension named above; an argument that names none is the same for every part. Nothing has to cross between parts.
Inputs may be any that keep to these rules, and one draw needn't show every extreme that they name: `tile_index`: slot 0 of block t names the block itself (t % 4), slot 1 the block before it, or 4 (the rows received from the previous domain) for a domain's first block; the 3 slots of a block name different sources. Values 4 and 5 stand for the rows received from the previous and the next domain. tile_mask[t, 0, r, r] is 1 for every block and row. `send_rows`: the 128 entries of one row are distinct; row 0 lies in the last 256 rows of a domain, row 1 in the first 256. Domain o owns coarse nodes o * 128 to (o + 1) * 128 - 1. The parent of a cell of domain p is owned by domain p, p - 1, p + 1, p - 2 or p + 2. At most 32 cells of domain p have parents owned by each of p - 2, p - 1, p + 1 and p + 2, and exactly 32 by p + 1 for every domain but the last.
All inputs are finite; a program needn't handle non-finite values.
Results may differ from the reference program's by a relative error of at most 0.0068.
Values may be sent and summed in bfloat16 or wider, within the bound.
No kernel may reach another device: no remote copies, remote signals or barrier semaphores. Data moves between devices by JAX's collectives and lax.ppermute only.
A program may use at most 64 MiB of HBM per device.

```python
import jax
import jax.numpy as jnp
from jax import lax

D = 512
HID = 512
LAYERS = 2
K = 3
BLOCK = 128
NB = 4
ROWS_DEV = 512
COARSE_DEV = 128
DOMAINS = 8
CELLS = 4096
NBLK = 32
CAP = 32
COARSE = 1024


def draw_tile_index(key, part):
    key = jax.random.fold_in(key, 1)
    local_block = (jnp.arange(NBLK) % NB).astype(jnp.int32)
    own_slot = local_block
    previous = jnp.where(local_block > 0, local_block - 1, NB).astype(jnp.int32)
    drawn = jax.random.randint(key, (NBLK,), 0, NB)
    lower_slot = jnp.minimum(own_slot, previous)
    upper_slot = jnp.maximum(own_slot, previous)
    third_slot = drawn + (drawn >= lower_slot).astype(jnp.int32)
    third_slot = third_slot + (third_slot >= upper_slot).astype(jnp.int32)
    return jnp.stack([own_slot, previous, third_slot], axis=1).astype(jnp.int32)


def draw_tile_mask(key, part):
    key = jax.random.fold_in(key, 2)
    drawn = jax.random.randint(key, (NBLK, K, BLOCK, BLOCK), 0, 16)
    present = (drawn == 0).astype(jnp.int32)
    diagonal = jnp.arange(BLOCK)[:, None] == jnp.arange(BLOCK)[None, :]
    first_slot = (jnp.arange(K) == 0)[:, None, None] & diagonal[None]
    return jnp.where(first_slot[None], 1, present).astype(jnp.int32)


def draw_send_rows(key, part):
    key = jax.random.fold_in(key, 3)
    domain_keys = jax.random.split(key, DOMAINS * 2)

    def choose_rows(subkey):
        return jax.random.permutation(subkey, 2 * BLOCK)[:BLOCK]
    chosen = jax.vmap(choose_rows)(domain_keys).reshape(DOMAINS, 2, BLOCK)
    offset = jnp.array([ROWS_DEV - 2 * BLOCK, 0], jnp.int32)
    return (chosen + offset[None, :, None]).astype(jnp.int32)


def draw_parent(key, part):
    key = jax.random.fold_in(key, 4)
    count_key, order_key, label_key = jax.random.split(key, 3)
    domain_ids = jnp.arange(DOMAINS).astype(jnp.int32)
    drawn = jax.random.randint(count_key, (DOMAINS, 3), CAP // 2, CAP + 1).astype(jnp.int32)
    up_one = jnp.where(domain_ids + 1 < DOMAINS, CAP, 0).astype(jnp.int32)
    down_one = jnp.where(domain_ids >= 1, drawn[:, 0], 0).astype(jnp.int32)
    up_two = jnp.where(domain_ids + 2 < DOMAINS, drawn[:, 1], 0).astype(jnp.int32)
    down_two = jnp.where(domain_ids >= 2, drawn[:, 2], 0).astype(jnp.int32)
    ends = jnp.cumsum(jnp.stack([up_one, down_one, up_two, down_two], axis=1), axis=1)
    position = jnp.arange(ROWS_DEV).astype(jnp.int32)[None, :]
    offset = jnp.where(position < ends[:, 0:1], 1, jnp.where(position < ends[:, 1:2], -1, jnp.where(position < ends[:, 2:3], 2, jnp.where(position < ends[:, 3:4], -2, 0)))).astype(jnp.int32)

    def shuffle(subkey):
        return jax.random.permutation(subkey, ROWS_DEV).astype(jnp.int32)
    order = jax.vmap(shuffle)(jax.random.split(order_key, DOMAINS))
    shuffled = jnp.take_along_axis(offset, order, axis=1)
    owner_ids = domain_ids[:, None] + shuffled
    within = jax.random.randint(label_key, (DOMAINS, ROWS_DEV), 0, COARSE_DEV).astype(jnp.int32)
    return (owner_ids * COARSE_DEV + within).reshape(CELLS).astype(jnp.int32)


def level_of(key, dims, shards, least, high):
    def one(dim, blocks):
        draws = jax.random.uniform(jax.random.fold_in(jax.random.fold_in(key, 6), dim), (blocks,), jnp.float32, least / len(shards), high / len(shards))
        return jnp.repeat(jnp.exp(draws), dims[dim] // blocks).reshape((-1,) + (1,) * (len(dims) - dim - 1))

    gain = one(*shards[0])
    for cut in shards[1:]:
        gain = gain * one(*cut)
    return gain


def normal_values(stream_key, extent, deviation, limit, cuts=(), kind=jnp.bfloat16):
    values = jax.random.normal(stream_key, extent, jnp.float32) * deviation
    if len(cuts) > 0:
        values = level_of(stream_key, extent, cuts, -0.22, 0.18) * values
    return jnp.clip(values, min=-limit, max=limit).astype(kind)


def setup_inputs(seed: int = 0, part: int = 0) -> dict:
    key_list = jax.random.split(jax.random.key(seed), 10)
    part_splits = jax.random.split(jax.random.fold_in(key_list[9], part), 10)
    return {
        "node_features": normal_values(part_splits[0], (D, CELLS), 1.0, 6.0, ((0, 2), (1, 8))),
        "inward_weight": normal_values(key_list[1], (LAYERS, HID, 2 * D), (2 * D) ** -0.5, 0.1875, ((1, 2),)),
        "outward_weight": normal_values(key_list[2], (LAYERS, D, HID), HID ** -0.5, 0.25, ((1, 2),)),
        "coarse_weight": normal_values(key_list[3], (D, D), D ** -0.5, 0.25, ((0, 2),)),
        "tile_index": draw_tile_index(jax.random.fold_in(jax.random.fold_in(key_list[9], part), 71), part),
        "tile_mask": draw_tile_mask(jax.random.fold_in(jax.random.fold_in(key_list[9], part), 71), part),
        "send_rows": draw_send_rows(jax.random.fold_in(jax.random.fold_in(key_list[9], part), 71), part),
        "parent": draw_parent(jax.random.fold_in(jax.random.fold_in(key_list[9], part), 71), part),
        "cotangent": normal_values(part_splits[8], (D, CELLS), 1.0, 6.0, ((0, 2), (1, 8))),
    }


def silu_slope(preact):
    sigmoid_value = jax.nn.sigmoid(preact)
    return sigmoid_value * (1.0 + preact * (1.0 - sigmoid_value))


def neighbour_sources(features, send_rows):
    feature_count = features.shape[0]
    by_domain = features.reshape(feature_count, DOMAINS, ROWS_DEV)

    def choose_rows(column):
        take_index = jnp.broadcast_to(send_rows[None, :, column, :], (feature_count, DOMAINS, BLOCK))
        return jnp.take_along_axis(by_domain, take_index, axis=2)

    zeros_rim = jnp.zeros((feature_count, 1, BLOCK), features.dtype)
    from_before = jnp.concatenate([zeros_rim, choose_rows(0)[:, :-1]], axis=1)
    from_after = jnp.concatenate([choose_rows(1)[:, 1:], zeros_rim], axis=1)
    combined = jnp.concatenate([by_domain, from_before, from_after], axis=2)
    return jnp.moveaxis(combined.reshape(feature_count, DOMAINS, NB + 2, BLOCK), 1, 0)


def aggregate(features, tile_index, tile_mask, send_rows):
    sources = neighbour_sources(features, send_rows)
    slot_index = tile_index.reshape(DOMAINS, NB, K)
    tile_bits = tile_mask.reshape(DOMAINS, NB, K, BLOCK, BLOCK)

    def per_domain(operands):
        source_blocks, slots, bits = operands
        picked = source_blocks[:, slots, :].astype(jnp.float32)
        weights = bits.astype(jnp.float32)
        summed = jnp.einsum("fbkc,bkrc->fbr", picked, weights)
        degree = jnp.sum(weights, axis=(1, 3))
        return (summed / degree[None]).astype(jnp.bfloat16)

    result = lax.map(per_domain, (sources, slot_index, tile_bits))
    return jnp.moveaxis(result, 0, 1).reshape(features.shape[0], CELLS)


def aggregate_back(scaled, tile_index, tile_mask, send_rows):
    feature_count = scaled.shape[0]
    by_domain = jnp.moveaxis(scaled.reshape(feature_count, DOMAINS, NB, BLOCK), 1, 0)
    slot_index = tile_index.reshape(DOMAINS, NB, K)
    tile_bits = tile_mask.reshape(DOMAINS, NB, K, BLOCK, BLOCK)

    def per_domain(operands):
        gradient, slots, bits = operands
        contrib = jnp.einsum("fbr,bkrc->fbkc", gradient.astype(jnp.float32), bits.astype(jnp.float32))
        onehot = (slots[:, :, None] == jnp.arange(NB + 2)).astype(jnp.float32)
        return jnp.einsum("fbkc,bkj->fjc", contrib, onehot, precision=lax.Precision.HIGHEST)

    result = lax.map(per_domain, (by_domain, slot_index, tile_bits))
    own_part = jnp.moveaxis(result[:, :, :NB], 0, 1).reshape(feature_count, DOMAINS, ROWS_DEV)
    to_before = lax.optimization_barrier(result[:, :, NB].astype(jnp.bfloat16)).astype(jnp.float32)
    to_after = lax.optimization_barrier(result[:, :, NB + 1].astype(jnp.bfloat16)).astype(jnp.float32)
    zeros_rim = jnp.zeros((1, feature_count, BLOCK), jnp.float32)
    from_after = jnp.concatenate([to_before[1:], zeros_rim], axis=0)
    from_before = jnp.concatenate([zeros_rim, to_after[:-1]], axis=0)
    domain_ids = jnp.broadcast_to(jnp.arange(DOMAINS)[:, None], (DOMAINS, BLOCK))
    own_part = own_part.at[:, domain_ids, send_rows[:, 0]].add(jnp.moveaxis(from_after, 0, 1))
    own_part = own_part.at[:, domain_ids, send_rows[:, 1]].add(jnp.moveaxis(from_before, 0, 1))
    return own_part.reshape(feature_count, CELLS)


def reference(node_features, inward_weight, outward_weight, coarse_weight, tile_index, tile_mask, send_rows, parent, cotangent):
    grad_scale = float(CELLS) ** -0.5
    degree = jnp.sum(tile_mask, axis=(1, 3)).astype(jnp.float32).reshape(CELLS)

    def forward_layer(features, layer_id):
        aggregated = aggregate(features, tile_index, tile_mask, send_rows)
        preact = jnp.dot(inward_weight[layer_id, :, :D], features, preferred_element_type=jnp.float32) + jnp.dot(inward_weight[layer_id, :, D:], aggregated, preferred_element_type=jnp.float32)
        hidden = jax.nn.silu(preact).astype(jnp.bfloat16)
        output = jnp.dot(outward_weight[layer_id], hidden, preferred_element_type=jnp.float32)
        updated = (features.astype(jnp.float32) + output).astype(jnp.bfloat16)
        return updated, (features, aggregated, preact, hidden)

    def backward_layer(incoming, stored, layer_id):
        features, aggregated, preact, hidden = stored
        hidden_grad = jnp.dot(outward_weight[layer_id].T, incoming, preferred_element_type=jnp.float32)
        preact_grad = (hidden_grad * silu_slope(preact)).astype(jnp.bfloat16)
        joined = jnp.concatenate([features, aggregated], axis=0)
        inward = jnp.dot(preact_grad, joined.T, preferred_element_type=jnp.float32) * grad_scale
        outward = jnp.dot(incoming, hidden.T, preferred_element_type=jnp.float32) * grad_scale
        input_grad = jnp.dot(inward_weight[layer_id].T, preact_grad, preferred_element_type=jnp.float32)
        scaled = (input_grad[D:] / degree[None]).astype(jnp.bfloat16)
        combined = incoming.astype(jnp.float32) + input_grad[:D] + aggregate_back(scaled, tile_index, tile_mask, send_rows)
        return combined, inward, outward

    first_out, first_stored = forward_layer(node_features, 0)
    node_count = jnp.maximum(jax.ops.segment_sum(jnp.ones((CELLS,), jnp.float32), parent, num_segments=COARSE), 1.0)
    pooled = jax.ops.segment_sum(first_out.T.astype(jnp.float32), parent, num_segments=COARSE)
    coarse = (pooled / node_count[:, None]).T.astype(jnp.bfloat16)
    coarse_pre = jnp.dot(coarse_weight, coarse, preferred_element_type=jnp.float32)
    correction = jax.nn.silu(coarse_pre).astype(jnp.bfloat16)
    lifted = (first_out.astype(jnp.float32) + correction[:, parent].astype(jnp.float32)).astype(jnp.bfloat16)
    final_out, second_stored = forward_layer(lifted, 1)

    second_grad, second_inward, second_outward = backward_layer(cotangent, second_stored, 1)
    lifted_grad = second_grad.astype(jnp.bfloat16)
    correction_grad = jax.ops.segment_sum(lifted_grad.T.astype(jnp.float32), parent, num_segments=COARSE).T
    pooled_grad = (correction_grad * silu_slope(coarse_pre)).astype(jnp.bfloat16)
    coarse_grad = jnp.dot(coarse_weight.T, pooled_grad, preferred_element_type=jnp.float32)
    spread_grad = (coarse_grad / node_count[None]).astype(jnp.bfloat16)
    weight_grad = jnp.dot(pooled_grad, coarse.T, preferred_element_type=jnp.float32) * grad_scale
    first_back = (lifted_grad.astype(jnp.float32) + spread_grad[:, parent].astype(jnp.float32)).astype(jnp.bfloat16)
    feature_grad, first_inward, first_outward = backward_layer(first_back, first_stored, 0)
    return final_out, feature_grad, jnp.stack([first_inward, second_inward]), jnp.stack([first_outward, second_outward]), weight_grad
```

```python
import jax
import jax.numpy as jnp
from jax import lax
from jax.experimental import pallas as pl
from jax.experimental.pallas import tpu as pltpu
from jax.sharding import PartitionSpec as P

BF = jnp.bfloat16
F32 = jnp.float32
I32 = jnp.int32
DOM = ("curve", "cross")
LINE = ("curve", "cross", "sub")
NN = (((1,), (0,)), ((), ()))
NT = (((1,), (1,)), ((), ()))
TN = (((0,), (0,)), ((), ()))


def dot(a, b, dims=NN):
    return lax.dot_general(a, b, dims, preferred_element_type=F32)


def sds(shape, dtype):
    return jax.ShapeDtypeStruct(shape, dtype)


def call(body, outs, scalars, arrays, name, flops=0, scratch=()):
    scalars, arrays = list(scalars), list(arrays)
    moved = sum(a.size * a.dtype.itemsize for a in arrays) + sum(
        o.size * o.dtype.itemsize for o in outs
    )
    return pl.pallas_call(
        body,
        out_shape=tuple(outs),
        in_specs=[pl.BlockSpec(memory_space=pltpu.SMEM)] * len(scalars)
        + [pl.BlockSpec(memory_space=pltpu.VMEM)] * len(arrays),
        out_specs=tuple(pl.BlockSpec(memory_space=pltpu.VMEM) for _ in outs),
        scratch_shapes=list(scratch),
        compiler_params=pltpu.CompilerParams(vmem_limit_bytes=40 * 2**20),
        cost_estimate=pl.CostEstimate(flops=flops, bytes_accessed=moved, transcendentals=0),
        name=name,
    )(*scalars, *arrays)


def shifted(value, steps):
    count = lax.axis_size(DOM)
    first, last = (max(0, -steps), min(count, count - steps))
    return lax.ppermute(value, DOM, [(s, s + steps) for s in range(first, last)])


def two_way(value, steps):
    count = lax.axis_size(DOM)
    pairs = [(2 * p, 2 * (p + steps)) for p in range(count - steps)]
    pairs += [(2 * p + 1, 2 * (p - steps) + 1) for p in range(steps, count)]
    return lax.ppermute(value, LINE, pairs)


def gather(value):
    return lax.all_gather(value, "sub", axis=0, tiled=True)


def sigmoid(v):
    return 1.0 / (1.0 + jnp.exp(-v))


def slope_of(v):
    s = sigmoid(v)
    return s * (1.0 + v * (1.0 - s))


def wide(col, width):
    return jnp.concatenate([col] * (width // col.shape[1]), axis=1)


def k_halo(rows_ref, x_ref, next_ref, prev_ref):
    x = x_ref[...]
    n = x.shape[1]
    at = lax.broadcasted_iota(I32, (n, rows_ref.shape[1]), 0)
    next_ref[...] = dot(x, (at == rows_ref[0:1, :]).astype(BF)).astype(BF)
    prev_ref[...] = dot(x, (at == rows_ref[1:2, :]).astype(BF)).astype(BF)


def k_prep(tile_ref, me_ref, mask_ref, rows_ref, rowc_ref, par_ref, parc_ref,
           adj_ref, adjt_ref, inv_ref, hott_ref, hot_ref, slot_ref, slott_ref,
           pick_ref, place_ref, tags_ref, ocount_ref):
    blocks, k_slots, length, _ = mask_ref.shape
    n = adj_ref.shape[0]
    nodes = hott_ref.shape[0]
    slots = slot_ref.shape[0]
    cap = slots // 4
    adj_ref[...] = jnp.zeros(adj_ref.shape, BF)
    adjt_ref[...] = jnp.zeros(adjt_ref.shape, BF)
    for b in range(blocks):
        degree = jnp.zeros((length, 1), F32)
        for k in range(k_slots):
            bits = mask_ref[b, k].astype(F32)
            start = pl.multiple_of(tile_ref[b, k] * length, length)
            adj_ref[b * length:(b + 1) * length, pl.ds(start, length)] = bits.astype(BF)
            adjt_ref[pl.ds(start, length), b * length:(b + 1) * length] = bits.T.astype(BF)
            degree = degree + jnp.sum(bits, axis=1, keepdims=True)
        inv_ref[b * length:(b + 1) * length, :] = jnp.broadcast_to(1.0 / degree, (length, 128))
    base = me_ref[0] * nodes
    rel_row = par_ref[...] - base
    rel_col = parc_ref[...] - base
    hott = (lax.broadcasted_iota(I32, (nodes, n), 0) == rel_row).astype(F32)
    hott_ref[...] = hott.astype(BF)
    ocount_ref[...] = jnp.broadcast_to(jnp.sum(hott, axis=1, keepdims=True), (nodes, 128))
    hot_ref[...] = (lax.broadcasted_iota(I32, (n, nodes), 1) == rel_col).astype(F32).astype(BF)

    def offsets(shape, dim):
        j = lax.broadcasted_iota(I32, shape, dim)
        off = jnp.where(j < cap, 1, jnp.where(j < 2 * cap, -1, jnp.where(j < 3 * cap, 2, -2)))
        start = jnp.where(j < cap, 0, jnp.where(j < 2 * cap, cap, jnp.where(j < 3 * cap, 2 * cap, 3 * cap)))
        return off * nodes, (j - start).astype(F32)

    i0 = lax.broadcasted_iota(I32, (n, n), 0)
    i1 = lax.broadcasted_iota(I32, (n, n), 1)
    off, rank_want = offsets((slots, n), 0)
    node = rel_row - off
    chosen = ((node >= 0) & (node < nodes)).astype(F32)
    rank = dot(chosen.astype(BF), (i0 < i1).astype(F32).astype(BF))
    slot_ref[...] = jnp.where(rank == rank_want, chosen, 0.0).astype(BF)
    off, rank_want = offsets((n, slots), 1)
    node = rel_col - off
    chosen = ((node >= 0) & (node < nodes)).astype(F32)
    rank = dot((i0 > i1).astype(F32).astype(BF), chosen.astype(BF))
    fits = jnp.where(rank == rank_want, chosen, 0.0)
    slott_ref[...] = fits.astype(BF)
    tags = jnp.sum(fits * (node + 1).astype(F32), axis=0, keepdims=True)
    tags_ref[...] = jnp.broadcast_to(tags, tags_ref.shape).astype(BF)
    width = rows_ref.shape[1]
    at1 = lax.broadcasted_iota(I32, (width, n), 1)
    at0 = lax.broadcasted_iota(I32, (n, width), 0)
    for c in range(2):
        pick_ref[c * width:(c + 1) * width, :] = (at1 == rowc_ref[:, c:c + 1]).astype(F32).astype(BF)
        place_ref[:, c * width:(c + 1) * width] = (at0 == rows_ref[c:c + 1, :]).astype(F32).astype(BF)


def forward(xc, src, adj_ref, inv_ref, wx_ref, wa_ref, wo_ref):
    width = xc.shape[1]
    agg = (dot(adj_ref[...], src) * wide(inv_ref[...], width)).astype(BF)
    pre = dot(xc, wx_ref[...], NT) + dot(agg, wa_ref[...], NT)
    hid = (pre * sigmoid(pre)).astype(BF)
    out = (xc.astype(F32) + dot(hid, wo_ref[...], NT)).astype(BF)
    return agg, pre, hid, out


def send_slots(sub, values, slot_ref, one_ref, two_ref):
    cap = slot_ref.shape[0] // 4
    a = pl.multiple_of(sub * cap, cap)
    one_ref[0:cap, :] = dot(slot_ref[pl.ds(a, cap), :], values).astype(BF)
    two_ref[0:cap, :] = dot(slot_ref[pl.ds(a + 2 * cap, cap), :], values).astype(BF)


def k_first(me_ref, x_ref, before_ref, after_ref, adj_ref, inv_ref, wx_ref, wa_ref, wo_ref,
            slot_ref, tags_ref,
            xc_ref, agg_ref, pre_ref, hid_ref, first_ref, one_ref, two_ref, src):
    n = x_ref.shape[1]
    rim = before_ref.shape[1]
    xc = x_ref[...].T
    xc_ref[...] = xc
    src[0:n, :] = xc
    src[n:n + rim, :] = before_ref[...].T
    src[n + rim:, :] = after_ref[...].T
    agg, pre, hid, out = forward(xc, src[...], adj_ref, inv_ref, wx_ref, wa_ref, wo_ref)
    agg_ref[...] = agg
    pre_ref[...] = pre
    hid_ref[...] = hid
    first_ref[...] = out
    send_slots(me_ref[1], out, slot_ref, one_ref, two_ref)
    cap = slot_ref.shape[0] // 4
    pad = wide(tags_ref[...], one_ref.shape[1])
    one_ref[cap:, :] = pad
    two_ref[cap:, :] = pad


def k_own(hott_ref, v_ref, pre_ref, pool_ref, slope_ref):
    pool_ref[...] = dot(hott_ref[...], v_ref[...])
    slope_ref[...] = slope_of(pre_ref[...])


def k_pool(hott_ref, v_ref, pool_ref):
    pool_ref[...] = dot(hott_ref[...], v_ref[...])


def k_cot(ct_ref, wo_ref, ctc_ref, hg_ref):
    ctc = ct_ref[...].T
    ctc_ref[...] = ctc
    hg_ref[...] = dot(ctc, wo_ref[...])


def arrived_of(one_ref, two_ref, cap, rows):
    return jnp.concatenate(
        [one_ref[0:cap, :], one_ref[rows:rows + cap, :], two_ref[0:cap, :], two_ref[rows:rows + cap, :]],
        axis=0,
    )


def send_answers(sub, hits, values, one_ref, two_ref):
    cap = hits.shape[1] // 4
    ans = dot(hits.T, values).astype(BF)
    one_ref[...] = jnp.where(sub == 0, ans[cap:2 * cap], ans[0:cap])
    two_ref[...] = jnp.where(sub == 0, ans[3 * cap:], ans[2 * cap:3 * cap])


def k_coarse(me_ref, pool_ref, ocount_ref, one_ref, two_ref, cw_ref,
             hits_ref, icount_ref, coarse_ref, cpre_ref, corr_ref, out1_ref, out2_ref):
    nodes, width = pool_ref.shape
    cap = out1_ref.shape[0]
    rows = one_ref.shape[0] // 2
    slots = 4 * cap
    lane = lax.broadcasted_iota(I32, (1, slots), 1)
    t = [r[o + cap:o + cap + 1, 0:slots].astype(F32) for r in (one_ref, two_ref) for o in (0, rows)]
    tags = jnp.where(lane < cap, t[0], jnp.where(lane < 2 * cap, t[1], jnp.where(lane < 3 * cap, t[2], t[3])))
    node = (lax.broadcasted_iota(I32, (nodes, slots), 0) + 1).astype(F32)
    hits = (node == tags).astype(F32)
    count = jnp.maximum(ocount_ref[...] + jnp.sum(hits, axis=1, keepdims=True), 1.0)
    icount = 1.0 / count
    hits_ref[...] = hits
    icount_ref[...] = icount
    hb = hits.astype(BF)
    total = pool_ref[...] + dot(hb, arrived_of(one_ref, two_ref, cap, rows))
    coarse = (total * wide(icount, width)).astype(BF)
    cpre = dot(coarse, cw_ref[...], NT)
    corr = (cpre * sigmoid(cpre)).astype(BF)
    coarse_ref[...] = coarse
    cpre_ref[...] = cpre
    corr_ref[...] = corr
    ans = dot(hits.T.astype(BF), corr).astype(BF)
    sub = me_ref[1]
    out1_ref[...] = jnp.where(sub == 0, ans[cap:2 * cap], ans[0:cap])
    out2_ref[...] = jnp.where(sub == 0, ans[3 * cap:], ans[2 * cap:3 * cap])


def spread_back(first, hot_ref, slott_ref, corr, one_ref, two_ref):
    cap = one_ref.shape[0] // 2
    returned = jnp.concatenate(
        [one_ref[cap:, :], one_ref[0:cap, :], two_ref[cap:, :], two_ref[0:cap, :]], axis=0
    )
    total = first.astype(F32) + dot(hot_ref[...], corr) + dot(slott_ref[...], returned)
    return total.astype(BF)


def k_lift(me_ref, first_ref, hot_ref, slott_ref, corr_ref, one_ref, two_ref, pick_ref,
           lift_ref, msg_ref):
    lifted = spread_back(first_ref[...], hot_ref, slott_ref, corr_ref[...], one_ref, two_ref)
    lift_ref[...] = lifted
    rim = msg_ref.shape[0]
    at = pl.multiple_of(me_ref[1] * rim, rim)
    msg_ref[...] = dot(pick_ref[pl.ds(at, rim), :], lifted).astype(BF)


def rim_grads(sub, pg, wa_ref, inv_ref, adjt_ref, scaled_ref, msg_ref):
    n = pg.shape[0]
    rim = msg_ref.shape[0]
    scaled = (dot(pg, wa_ref[...]) * wide(inv_ref[...], wa_ref.shape[1])).astype(BF)
    scaled_ref[...] = scaled
    at = pl.multiple_of(n + (1 - sub) * rim, rim)
    msg_ref[...] = dot(adjt_ref[pl.ds(at, rim), :], scaled).astype(BF)


def k_second(me_ref, lift_ref, rim_ref, adj_ref, adjt_ref, inv_ref, wx_ref, wa_ref, wo_ref, hg_ref,
             agg_ref, hid_ref, new_ref, pg_ref, scaled_ref, msg_ref, src):
    n = lift_ref.shape[0]
    lifted = lift_ref[...]
    src[0:n, :] = lifted
    src[n:, :] = rim_ref[...]
    agg, pre, hid, out = forward(lifted, src[...], adj_ref, inv_ref, wx_ref, wa_ref, wo_ref)
    agg_ref[...] = agg
    hid_ref[...] = hid
    new_ref[...] = out
    pg = (hg_ref[...] * slope_of(pre)).astype(BF)
    pg_ref[...] = pg
    rim_grads(me_ref[1], pg, wa_ref, inv_ref, adjt_ref, scaled_ref, msg_ref)


def combine(g, pg, wx_ref, scaled, adjt_ref):
    n = g.shape[0]
    return g.astype(F32) + dot(pg, wx_ref[...]) + dot(adjt_ref[0:n, :], scaled)


def k_combine(g_ref, pg_ref, wx_ref, scaled_ref, adjt_ref, comb_ref):
    comb_ref[...] = combine(g_ref[...], pg_ref[...], wx_ref, scaled_ref[...], adjt_ref)


def k_newt(me_ref, new_ref, out_ref):
    half = out_ref.shape[0]
    at = pl.multiple_of(me_ref[1] * half, half)
    out_ref[...] = new_ref[:, pl.ds(at, half)].T


def k_grads(scale, me_ref, pg_ref, h_ref, agg_ref, g_ref, hid_ref, gin_ref, gout_ref):
    half = gin_ref.shape[0]
    width = h_ref.shape[1]
    at = pl.multiple_of(me_ref[1] * half, half)
    pgt = pg_ref[:, pl.ds(at, half)].T
    gin_ref[:, 0:width] = dot(pgt, h_ref[...]) * scale
    gin_ref[:, width:] = dot(pgt, agg_ref[...]) * scale
    gt = g_ref[:, pl.ds(at, half)].T
    gout_ref[...] = dot(gt, hid_ref[...]) * scale


def k_packed(scale, order, me_ref, pg_ref, h_ref, agg_ref, g_ref, hid_ref, *rest):
    out_ref = rest[-1]
    extra_ref = rest[0] if len(rest) > 1 else None
    parts = out_ref.shape[0]
    width = h_ref.shape[1]
    hidden = hid_ref.shape[1]
    half = width // 2
    at = pl.multiple_of(me_ref[1] * half, half)
    pgt = pg_ref[:, pl.ds(at, half)].T
    lo = (dot(pgt, h_ref[...]) * scale).astype(BF)
    hi = (dot(pgt, agg_ref[...]) * scale).astype(BF)
    gt = g_ref[:, pl.ds(at, half)].T
    go = (dot(gt, hid_ref[...]) * scale).astype(BF)
    piece = 2 * width // parts
    small = hidden // parts
    for d in range(parts):
        row = order[d]
        src, c = (lo, d * piece) if d * piece < width else (hi, d * piece - width)
        out_ref[row, 0:half, :] = src[:, c:c + piece]
        mine = go[:, d * small:(d + 1) * small]
        if extra_ref is None:
            quarter = half // 2
            out_ref[row, half:half + quarter, :] = jnp.concatenate([mine[:quarter], mine[quarter:]], axis=1)
        else:
            other = extra_ref[:, d * small:(d + 1) * small].astype(BF)
            out_ref[row, half:2 * half, :] = jnp.concatenate([mine, other], axis=1)


def k_lgrad(me_ref, comb_ref, rim_ref, place_ref, slot_ref, lg_ref, one_ref, two_ref):
    rim = rim_ref.shape[0] // 2
    lg = comb_ref[...] + dot(place_ref[:, 0:rim], rim_ref[rim:, :]) + dot(place_ref[:, rim:], rim_ref[0:rim, :])
    lg = lg.astype(BF)
    lg_ref[...] = lg
    send_slots(me_ref[1], lg, slot_ref, one_ref, two_ref)


def k_cgrad(me_ref, pool_ref, one_ref, two_ref, hits_ref, icount_ref, cpre_ref, cw_ref,
            pgrad_ref, spread_ref, out1_ref, out2_ref):
    cap = out1_ref.shape[0]
    hits = hits_ref[...]
    total = pool_ref[...] + dot(hits.astype(BF), arrived_of(one_ref, two_ref, cap, cap))
    pgrad = (total * slope_of(cpre_ref[...])).astype(BF)
    pgrad_ref[...] = pgrad
    spread = (dot(pgrad, cw_ref[...]) * wide(icount_ref[...], pgrad.shape[1])).astype(BF)
    spread_ref[...] = spread
    ans = dot(hits.T.astype(BF), spread).astype(BF)
    sub = me_ref[1]
    out1_ref[...] = jnp.where(sub == 0, ans[cap:2 * cap], ans[0:cap])
    out2_ref[...] = jnp.where(sub == 0, ans[3 * cap:], ans[2 * cap:3 * cap])


def k_cweight(scale, me_ref, pgrad_ref, coarse_ref, out_ref):
    half = out_ref.shape[0]
    at = pl.multiple_of(me_ref[1] * half, half)
    out_ref[...] = dot(pgrad_ref[:, pl.ds(at, half)].T, coarse_ref[...]) * scale


def k_third(me_ref, lg_ref, hot_ref, slott_ref, spread_ref, one_ref, two_ref, wo_ref, slope_ref,
            wa_ref, inv_ref, adjt_ref,
            fb_ref, pg_ref, scaled_ref, before_ref, after_ref):
    fb = spread_back(lg_ref[...], hot_ref, slott_ref, spread_ref[...], one_ref, two_ref)
    fb_ref[...] = fb
    pg = (dot(fb, wo_ref[...]) * slope_ref[...]).astype(BF)
    pg_ref[...] = pg
    n, width = fb.shape
    half = width // 2
    rim = before_ref.shape[0]
    scaled = (dot(pg, wa_ref[...]) * wide(inv_ref[...], width)).astype(BF)
    scaled_ref[...] = scaled
    at = pl.multiple_of(me_ref[1] * half, half)
    mine = scaled_ref[:, pl.ds(at, half)]
    both = dot(adjt_ref[n:, :], mine).astype(BF)
    before_ref[...] = both[0:rim]
    after_ref[...] = both[rim:]


def k_last(comb_ref, after_ref, before_ref, place_ref, out_ref):
    rim = after_ref.shape[0]
    total = comb_ref[...] + dot(place_ref[:, 0:rim], after_ref[...]) + dot(place_ref[:, rim:], before_ref[...])
    out_ref[...] = total.T


def k_halfcomb(me_ref, fb_ref, pg_ref, wx_ref, scaled_ref, adjt_ref, comb_ref):
    n, half = comb_ref.shape
    at = pl.multiple_of(me_ref[1] * half, half)
    cols = pl.ds(at, half)
    comb_ref[...] = (
        fb_ref[:, cols].astype(F32)
        + dot(pg_ref[...], wx_ref[:, cols])
        + dot(adjt_ref[0:n, :], scaled_ref[:, cols])
    )


def k_sum(early_ref, late_ref, gin_ref, gout_ref, gco_ref):
    half = gin_ref.shape[1]
    small = gout_ref.shape[2]
    e = early_ref[...].astype(F32)
    gin_ref[1] = e[0:half]
    gout_ref[1] = e[half:, 0:small]
    gco_ref[...] = e[half:, small:]
    t = late_ref[0].astype(F32)
    for d in range(1, late_ref.shape[0]):
        t = t + late_ref[d].astype(F32)
    gin_ref[0] = t[0:half]
    quarter = half // 2
    gout_ref[0, 0:quarter, :] = t[half:, 0:small]
    gout_ref[0, quarter:, :] = t[half:, small:]


def local(node_features, inward_weight, outward_weight, coarse_weight, tile_index, tile_mask,
          send_rows, parent, cotangent):
    half, n = node_features.shape
    width = 2 * half
    blocks, k_slots = tile_index.shape
    rim = tile_mask.shape[2]
    src_rows = (blocks + 2) * rim
    domains = lax.axis_size(DOM)
    cross = lax.axis_size("cross")
    curve = lax.axis_size("curve")
    cap = n // 16
    nodes = n // 4
    slots = 4 * cap
    hidden = 2 * inward_weight.shape[1]
    scale = float(n * domains) ** -0.5
    me = jnp.stack([lax.axis_index(DOM), lax.axis_index("sub")]).astype(I32)
    rows = send_rows[0]
    packed = 2 * width // domains == 128

    halo_next, halo_prev = call(
        k_halo, [sds((half, rim), BF)] * 2, [], [rows, node_features], "halo")
    before_half = shifted(halo_next, 1)
    after_half = shifted(halo_prev, -1)
    x_full = gather(node_features)
    wx = [gather(inward_weight[l, :, :width]) for l in range(2)]
    wa = [gather(inward_weight[l, :, width:]) for l in range(2)]
    wo = [gather(outward_weight[l]) for l in range(2)]
    (adj, adjt, inv, hott, hot, slot, slott, pick, place, tags, ocount) = call(
        k_prep,
        [sds((n, src_rows), BF), sds((src_rows, n), BF), sds((n, 128), F32), sds((nodes, n), BF),
         sds((n, nodes), BF), sds((slots, n), BF), sds((n, slots), BF), sds((2 * rim, n), BF),
         sds((n, 2 * rim), BF), sds((16, slots), BF), sds((nodes, 128), F32)],
        [tile_index, me],
        [tile_mask, rows, rows.T, parent[None, :], parent[:, None]], "prep")
    before = gather(before_half)
    after = gather(after_half)
    msg = sds((cap + 16, width), BF)
    plain = sds((cap, width), BF)
    cell_bf, cell_f32 = sds((n, width), BF), sds((n, width), F32)
    xc, agg0, pre0, hid0, first, one, two = call(
        k_first,
        [cell_bf, cell_bf, sds((n, hidden), F32), sds((n, hidden), BF), cell_bf, msg, msg],
        [me], [x_full, before, after, adj, inv, wx[0], wa[0], wo[0], slot, tags], "first",
        flops=2 * n * width * (src_rows + 3 * width),
        scratch=[pltpu.VMEM((src_rows, width), BF)])
    one, two = two_way(one, 1), two_way(two, 2)
    own, slope0 = call(k_own, [sds((nodes, width), F32), sds((n, hidden), F32)], [], [hott, first, pre0],
                       "own")
    ct_full = gather(cotangent)
    ctc, hg1 = call(k_cot, [cell_bf, sds((n, hidden), F32)], [], [ct_full, wo[1]], "cot")
    cw = gather(coarse_weight)
    one, two = gather(one), gather(two)
    node_bf, node_f32 = sds((nodes, width), BF), sds((nodes, width), F32)
    hits, icount, coarse, cpre, corr, one, two = call(
        k_coarse, [sds((nodes, slots), F32), sds((nodes, 128), F32), node_bf, node_f32, node_bf, plain, plain],
        [me], [own, ocount, one, two, cw], "coarse")
    one, two = gather(two_way(one, 1)), gather(two_way(two, 2))
    lifted, rims = call(
        k_lift, [cell_bf, sds((rim, width), BF)], [me],
        [first, hot, slott, corr, one, two, pick], "lift")
    rims = gather(two_way(rims, 1))
    agg1, hid1, new, pg1, scaled1, rims = call(
        k_second,
        [cell_bf, sds((n, hidden), BF), cell_bf, sds((n, hidden), BF), cell_bf, sds((rim, width), BF)],
        [me], [lifted, rims, adj, adjt, inv, wx[1], wa[1], wo[1], hg1], "second",
        scratch=[pltpu.VMEM((src_rows, width), BF)])
    rims = two_way(rims, 1)
    comb1, = call(k_combine, [cell_f32], [], [ctc, pg1, wx[1], scaled1, adjt], "combine")
    rims = gather(rims)
    lg, one, two = call(
        k_lgrad, [cell_bf, plain, plain], [me], [comb1, rims, place, slot], "lgrad")
    one, two = two_way(one, 1), two_way(two, 2)
    own_g, = call(k_pool, [node_f32], [], [hott, lg], "own_grad")
    new_t, = call(k_newt, [sds((half, n), BF)], [me], [new], "new")
    one, two = gather(one), gather(two)
    pgrad, spread, one, two = call(
        k_cgrad, [node_bf, node_bf, plain, plain], [me],
        [own_g, one, two, hits, icount, cpre, cw], "cgrad")
    one, two = two_way(one, 1), two_way(two, 2)
    gco, = call(lambda *r: k_cweight(scale, *r), [sds((half, width), F32)], [me], [pgrad, coarse], "cweight")
    one, two = gather(one), gather(two)
    fb, pg0, scaled0, to_before, to_after = call(
        k_third,
        [cell_bf, sds((n, hidden), BF), cell_bf, sds((rim, half), BF), sds((rim, half), BF)],
        [me], [lg, hot, slott, spread, one, two, wo[0], slope0, wa[0], inv, adjt], "third")
    from_after = shifted(to_before, -1)
    from_before = shifted(to_after, 1)
    comb0, = call(k_halfcomb, [sds((n, half), F32)], [me], [fb, pg0, wx[0], scaled0, adjt], "halfcomb")
    if packed:
        order = [(d % cross) * curve + d // cross for d in range(domains)]
        piece = 2 * width // domains
        early, = call(lambda *r: k_packed(scale, order, *r), [sds((domains, 2 * half, piece), BF)], [me],
                      [pg1, lifted, agg1, ctc, hid1, gco], "grads1")
        early = lax.psum_scatter(early, "cross", scatter_dimension=0, tiled=True)
        early = lax.psum_scatter(early, "curve", scatter_dimension=0, tiled=True)[0]
        late, = call(lambda *r: k_packed(scale, list(range(domains)), *r),
                     [sds((domains, half + half // 2, piece), BF)], [me],
                     [pg0, xc, agg0, fb, hid0], "grads0")
        late = lax.all_to_all(late, DOM, 0, 0, tiled=True)
        small = hidden // domains
        gin, gout, gco = call(
            k_sum, [sds((2, half, piece), F32), sds((2, half, small), F32), sds((half, small), F32)],
            [], [early, late], "sums")
    else:
        shapes = [sds((half, 2 * width), F32), sds((half, hidden), F32)]
        gi1, go1 = call(lambda *r: k_grads(scale, *r), shapes, [me], [pg1, lifted, agg1, ctc, hid1], "grads1")
        gi0, go0 = call(lambda *r: k_grads(scale, *r), shapes, [me], [pg0, xc, agg0, fb, hid0], "grads0")
        gin = lax.psum_scatter(jnp.stack([gi0, gi1]), DOM, scatter_dimension=2, tiled=True)
        gout = lax.psum_scatter(jnp.stack([go0, go1]), DOM, scatter_dimension=2, tiled=True)
        gco = lax.psum_scatter(gco, DOM, scatter_dimension=1, tiled=True)
    fgrad, = call(k_last, [sds((half, n), F32)], [], [comb0, from_after, from_before, place], "last")
    return new_t, fgrad, gin, gout, gco


def solution(mesh):
    cells = ("groups", "curve", "cross")
    in_specs = (
        P("sub", cells),
        P(None, "sub", None),
        P(None, "sub", None),
        P("sub", None),
        P(cells, None),
        P(cells, None, None, None),
        P(cells, None, None),
        P(cells),
        P("sub", cells),
    )
    out_specs = (
        P("sub", cells),
        P("sub", cells),
        P("groups", "sub", ("curve", "cross")),
        P("groups", "sub", ("curve", "cross")),
        P(("groups", "sub"), ("curve", "cross")),
    )
    return jax.shard_map(local, mesh=mesh, in_specs=in_specs, out_specs=out_specs, check_vma=False)
```

```python
import jax
import jax.numpy as jnp
from jax import lax
from jax.experimental import pallas as pl
from jax.experimental.pallas import tpu as pltpu
from jax.sharding import PartitionSpec as P

BF = jnp.bfloat16
F32 = jnp.float32
I32 = jnp.int32
DOM = ("curve", "cross")
LINE = ("curve", "cross", "sub")
NN = (((1,), (0,)), ((), ()))
NT = (((1,), (1,)), ((), ()))
TN = (((0,), (0,)), ((), ()))


def dot(a, b, dims=NN):
    return lax.dot_general(a, b, dims, preferred_element_type=F32)


def sds(shape, dtype):
    return jax.ShapeDtypeStruct(shape, dtype)


def call(body, outs, scalars, arrays, name, flops=0, scratch=()):
    scalars, arrays = list(scalars), list(arrays)
    moved = sum(a.size * a.dtype.itemsize for a in arrays) + sum(
        o.size * o.dtype.itemsize for o in outs
    )
    return pl.pallas_call(
        body,
        out_shape=tuple(outs),
        in_specs=[pl.BlockSpec(memory_space=pltpu.SMEM)] * len(scalars)
        + [pl.BlockSpec(memory_space=pltpu.VMEM)] * len(arrays),
        out_specs=tuple(pl.BlockSpec(memory_space=pltpu.VMEM) for _ in outs),
        scratch_shapes=list(scratch),
        compiler_params=pltpu.CompilerParams(vmem_limit_bytes=20 * 2**20),
        cost_estimate=pl.CostEstimate(flops=flops, bytes_accessed=moved, transcendentals=0),
        name=name,
    )(*scalars, *arrays)


def shifted(value, steps):
    count = lax.axis_size(DOM)
    first, last = (max(0, -steps), min(count, count - steps))
    return lax.ppermute(value, DOM, [(s, s + steps) for s in range(first, last)])


def two_way(value, steps):
    count = lax.axis_size(DOM)
    pairs = [(2 * p, 2 * (p + steps)) for p in range(count - steps)]
    pairs += [(2 * p + 1, 2 * (p - steps) + 1) for p in range(steps, count)]
    return lax.ppermute(value, LINE, pairs)


def gather(value):
    return lax.all_gather(value, "sub", axis=0, tiled=True)


def swap(value):
    return lax.ppermute(value, "sub", [(0, 1), (1, 0)])


def sigmoid(v):
    return 1.0 / (1.0 + jnp.exp(-v))


def slope_of(v):
    s = sigmoid(v)
    return s * (1.0 + v * (1.0 - s))


def wide(col, width):
    return jnp.concatenate([col] * (width // col.shape[1]), axis=1)


def k_halo(rows_ref, x_ref, next_ref, prev_ref):
    x = x_ref[...]
    n = x.shape[1]
    at = lax.broadcasted_iota(I32, (n, rows_ref.shape[1]), 0)
    next_ref[...] = dot(x, (at == rows_ref[0:1, :]).astype(BF)).astype(BF)
    prev_ref[...] = dot(x, (at == rows_ref[1:2, :]).astype(BF)).astype(BF)


def k_weights(me_ref, win_ref, wout_ref, win2_ref, wout2_ref, *outs):
    half = win_ref.shape[1]
    own = pl.multiple_of(me_ref[1] * half, half)
    other = pl.multiple_of((1 - me_ref[1]) * half, half)
    for layer in range(2):
        outs[layer][pl.ds(own, half), :] = win_ref[layer]
        outs[layer][pl.ds(other, half), :] = win2_ref[layer]
        outs[2 + layer][pl.ds(own, half), :] = wout_ref[layer]
        outs[2 + layer][pl.ds(other, half), :] = wout2_ref[layer]


def k_prep(tile_ref, me_ref, mask_ref, rows_ref, par_ref,
           adj_ref, adjt_ref, inv_ref, hott_ref, hot_ref, slot_ref, slott_ref,
           pick_ref, place_ref, tags_ref, ocount_ref):
    blocks, k_slots, length, _ = mask_ref.shape
    n = adj_ref.shape[0]
    nodes = hott_ref.shape[0]
    slots = slot_ref.shape[0]
    cap = slots // 4
    adj_ref[...] = jnp.zeros(adj_ref.shape, BF)
    adjt_ref[...] = jnp.zeros(adjt_ref.shape, BF)
    for b in range(blocks):
        degree = jnp.zeros((length, 1), F32)
        for k in range(k_slots):
            bits = mask_ref[b, k].astype(F32)
            start = pl.multiple_of(tile_ref[b, k] * length, length)
            adj_ref[b * length:(b + 1) * length, pl.ds(start, length)] = bits.astype(BF)
            adjt_ref[pl.ds(start, length), b * length:(b + 1) * length] = bits.T.astype(BF)
            degree = degree + jnp.sum(bits, axis=1, keepdims=True)
        inv_ref[b * length:(b + 1) * length, :] = jnp.broadcast_to(1.0 / degree, (length, 128))
    rel_row = par_ref[...] - me_ref[0] * nodes
    hott = (lax.broadcasted_iota(I32, (nodes, n), 0) == rel_row).astype(F32)
    hott_ref[...] = hott.astype(BF)
    ocount_ref[...] = jnp.broadcast_to(jnp.sum(hott, axis=1, keepdims=True), (nodes, 128))
    hot_ref[...] = hott.T.astype(BF)
    j = lax.broadcasted_iota(I32, (slots, n), 0)
    off = jnp.where(j < cap, 1, jnp.where(j < 2 * cap, -1, jnp.where(j < 3 * cap, 2, -2)))
    start = jnp.where(j < cap, 0, jnp.where(j < 2 * cap, cap, jnp.where(j < 3 * cap, 2 * cap, 3 * cap)))
    node = rel_row - off * nodes
    chosen = ((node >= 0) & (node < nodes)).astype(F32)
    before = lax.broadcasted_iota(I32, (n, n), 0) < lax.broadcasted_iota(I32, (n, n), 1)
    rank = dot(chosen.astype(BF), before.astype(F32).astype(BF))
    fits = jnp.where(rank == (j - start).astype(F32), chosen, 0.0)
    slot_ref[...] = fits.astype(BF)
    slott_ref[...] = fits.T.astype(BF)
    tags = jnp.sum(fits * (node + 1).astype(F32), axis=1, keepdims=True)
    tags_ref[...] = jnp.broadcast_to(tags, (slots, slots)).T[0:tags_ref.shape[0], :].astype(BF)
    width = rows_ref.shape[1]
    at = lax.broadcasted_iota(I32, (n, width), 0)
    for c in range(2):
        place = (at == rows_ref[c:c + 1, :]).astype(F32)
        place_ref[:, c * width:(c + 1) * width] = place.astype(BF)
        pick_ref[c * width:(c + 1) * width, :] = place.T.astype(BF)


def forward(xc, src, adj_ref, inv_ref, win_ref, wo_ref):
    width = xc.shape[1]
    agg = (dot(adj_ref[...], src) * wide(inv_ref[...], width)).astype(BF)
    pre = dot(xc, win_ref[:, 0:width], NT) + dot(agg, win_ref[:, width:], NT)
    hid = (pre * sigmoid(pre)).astype(BF)
    out = (xc.astype(F32) + dot(hid, wo_ref[...], NT)).astype(BF)
    return agg, pre, hid, out


def send_slots(sub, values, slot_ref, one_ref, two_ref):
    cap = slot_ref.shape[0] // 4
    a = pl.multiple_of(sub * cap, cap)
    one_ref[0:cap, :] = dot(slot_ref[pl.ds(a, cap), :], values).astype(BF)
    two_ref[0:cap, :] = dot(slot_ref[pl.ds(a + 2 * cap, cap), :], values).astype(BF)


def k_first(me_ref, x_ref, rims_ref, adj_ref, inv_ref, win_ref, wo_ref,
            slot_ref, tags_ref,
            xc_ref, agg_ref, pre_ref, hid_ref, first_ref, one_ref, two_ref, src):
    n = x_ref.shape[1]
    rim = rims_ref.shape[2]
    half = rims_ref.shape[1] // 2
    xc = x_ref[...].T
    xc_ref[...] = xc
    src[0:n, :] = xc
    for c in range(2):
        src[n:n + rim, c * half:(c + 1) * half] = rims_ref[c, 0:half, :].T
        src[n + rim:, c * half:(c + 1) * half] = rims_ref[c, half:, :].T
    agg, pre, hid, out = forward(xc, src[...], adj_ref, inv_ref, win_ref, wo_ref)
    agg_ref[...] = agg
    pre_ref[...] = pre
    hid_ref[...] = hid
    first_ref[...] = out
    send_slots(me_ref[1], out, slot_ref, one_ref, two_ref)
    cap = slot_ref.shape[0] // 4
    pad = wide(tags_ref[...], one_ref.shape[1])
    one_ref[cap:, :] = pad
    two_ref[cap:, :] = pad


def k_own(hott_ref, v_ref, pre_ref, pool_ref, slope_ref):
    pool_ref[...] = dot(hott_ref[...], v_ref[...])
    slope_ref[...] = slope_of(pre_ref[...])


def k_pool(hott_ref, v_ref, pool_ref):
    pool_ref[...] = dot(hott_ref[...], v_ref[...])


def k_cot(ct_ref, wo_ref, ctc_ref, hg_ref):
    ctc = ct_ref[...].T
    ctc_ref[...] = ctc
    hg_ref[...] = dot(ctc, wo_ref[...])


def arrived_of(got_ref, cap):
    rows = got_ref.shape[1] // 2
    return jnp.concatenate(
        [got_ref[0, 0:cap], got_ref[1, 0:cap], got_ref[0, rows:rows + cap], got_ref[1, rows:rows + cap]],
        axis=0,
    )


def k_coarse(me_ref, pool_ref, ocount_ref, got_ref, cw_ref,
             hits_ref, icount_ref, coarse_ref, cpre_ref, corr_ref, out1_ref, out2_ref):
    nodes, width = pool_ref.shape
    cap = out1_ref.shape[0]
    rows = got_ref.shape[1] // 2
    slots = 4 * cap
    lane = lax.broadcasted_iota(I32, (1, slots), 1)
    t = [got_ref[c, o + cap:o + cap + 1, 0:slots].astype(F32) for o in (0, rows) for c in range(2)]
    tags = jnp.where(lane < cap, t[0], jnp.where(lane < 2 * cap, t[1], jnp.where(lane < 3 * cap, t[2], t[3])))
    node = (lax.broadcasted_iota(I32, (nodes, slots), 0) + 1).astype(F32)
    hits = (node == tags).astype(F32)
    count = jnp.maximum(ocount_ref[...] + jnp.sum(hits, axis=1, keepdims=True), 1.0)
    icount = 1.0 / count
    hits_ref[...] = hits
    icount_ref[...] = icount
    hb = hits.astype(BF)
    total = pool_ref[...] + dot(hb, arrived_of(got_ref, cap))
    coarse = (total * wide(icount, width)).astype(BF)
    cpre = dot(coarse, cw_ref[...], NT)
    corr = (cpre * sigmoid(cpre)).astype(BF)
    coarse_ref[...] = coarse
    cpre_ref[...] = cpre
    corr_ref[...] = corr
    ans = dot(hits.T.astype(BF), corr).astype(BF)
    sub = me_ref[1]
    out1_ref[...] = jnp.where(sub == 0, ans[cap:2 * cap], ans[0:cap])
    out2_ref[...] = jnp.where(sub == 0, ans[3 * cap:], ans[2 * cap:3 * cap])


def spread_back(first, hot_ref, slott_ref, corr, got_ref):
    cap = got_ref.shape[1] // 2
    returned = jnp.concatenate(
        [got_ref[1, 0:cap], got_ref[0, 0:cap], got_ref[1, cap:], got_ref[0, cap:]], axis=0
    )
    total = first.astype(F32) + dot(hot_ref[...], corr) + dot(slott_ref[...], returned)
    return total.astype(BF)


def k_lift(me_ref, first_ref, hot_ref, slott_ref, corr_ref, got_ref, pick_ref,
           lift_ref, msg_ref):
    lifted = spread_back(first_ref[...], hot_ref, slott_ref, corr_ref[...], got_ref)
    lift_ref[...] = lifted
    rim = msg_ref.shape[0]
    at = pl.multiple_of(me_ref[1] * rim, rim)
    msg_ref[...] = dot(pick_ref[pl.ds(at, rim), :], lifted).astype(BF)


def rim_grads(sub, pg, win_ref, inv_ref, adjt_ref, scaled_ref, msg_ref):
    n = pg.shape[0]
    width = win_ref.shape[1] // 2
    rim = msg_ref.shape[0]
    scaled = (dot(pg, win_ref[:, width:]) * wide(inv_ref[...], width)).astype(BF)
    scaled_ref[...] = scaled
    at = pl.multiple_of(n + (1 - sub) * rim, rim)
    msg_ref[...] = dot(adjt_ref[pl.ds(at, rim), :], scaled).astype(BF)


def k_second(me_ref, lift_ref, rim_ref, adj_ref, adjt_ref, inv_ref, win_ref, wo_ref, hg_ref,
             agg_ref, hid_ref, new_ref, pg_ref, scaled_ref, msg_ref, src):
    n = lift_ref.shape[0]
    lifted = lift_ref[...]
    src[0:n, :] = lifted
    src[n:, :] = rim_ref[...]
    agg, pre, hid, out = forward(lifted, src[...], adj_ref, inv_ref, win_ref, wo_ref)
    agg_ref[...] = agg
    hid_ref[...] = hid
    new_ref[...] = out
    pg = (hg_ref[...] * slope_of(pre)).astype(BF)
    pg_ref[...] = pg
    rim_grads(me_ref[1], pg, win_ref, inv_ref, adjt_ref, scaled_ref, msg_ref)


def k_combine(g_ref, pg_ref, win_ref, scaled_ref, adjt_ref, comb_ref):
    n, width = comb_ref.shape
    comb_ref[...] = (
        g_ref[...].astype(F32)
        + dot(pg_ref[...], win_ref[:, 0:width])
        + dot(adjt_ref[0:n, :], scaled_ref[...])
    )


def k_newt(me_ref, new_ref, out_ref):
    half = out_ref.shape[0]
    at = pl.multiple_of(me_ref[1] * half, half)
    out_ref[...] = new_ref[:, pl.ds(at, half)].T


def k_grads(scale, me_ref, pg_ref, h_ref, agg_ref, g_ref, hid_ref, gin_ref, gout_ref):
    half = gin_ref.shape[0]
    width = h_ref.shape[1]
    at = pl.multiple_of(me_ref[1] * half, half)
    pgt = pg_ref[:, pl.ds(at, half)].T
    gin_ref[:, 0:width] = dot(pgt, h_ref[...]) * scale
    gin_ref[:, width:] = dot(pgt, agg_ref[...]) * scale
    gt = g_ref[:, pl.ds(at, half)].T
    gout_ref[...] = dot(gt, hid_ref[...]) * scale


def pack_grads(scale, sub, pg_ref, h_ref, agg_ref, g_ref, hid_ref, out_ref):
    parts, _, piece = out_ref.shape
    width = h_ref.shape[1]
    hidden = hid_ref.shape[1]
    half = width // 2
    at = pl.multiple_of(sub * half, half)
    pgt = pg_ref[:, pl.ds(at, half)].T
    lo = (dot(pgt, h_ref[...]) * scale).astype(BF)
    hi = (dot(pgt, agg_ref[...]) * scale).astype(BF)
    for d in range(parts):
        src, c = (lo, d * piece) if d * piece < width else (hi, d * piece - width)
        out_ref[d, 0:half, :] = src[:, c:c + piece]
    pack_small((dot(hid_ref[...].T, g_ref[:, pl.ds(at, half)]) * scale).astype(BF), out_ref, half)


def pack_small(values, out_ref, row):
    parts, _, piece = out_ref.shape
    small = values.shape[0] // parts
    for d in range(parts):
        for c in range(values.shape[1] // piece):
            start = row + c * small
            out_ref[d, start:start + small, :] = values[d * small:(d + 1) * small, c * piece:(c + 1) * piece]


def k_combine_pack(scale, me_ref, pg_ref, h_ref, agg_ref, g_ref, hid_ref, win_ref, scaled_ref, adjt_ref,
                   comb_ref, out_ref):
    k_combine(g_ref, pg_ref, win_ref, scaled_ref, adjt_ref, comb_ref)
    pack_grads(scale, me_ref[1], pg_ref, h_ref, agg_ref, g_ref, hid_ref, out_ref)


def k_cweight_pack(scale, me_ref, pgrad_ref, coarse_ref, out_ref):
    half = pgrad_ref.shape[1] // 2
    at = pl.multiple_of(me_ref[1] * half, half)
    values = (dot(coarse_ref[...].T, pgrad_ref[:, pl.ds(at, half)]) * scale).astype(BF)
    pack_small(values, out_ref, 0)


def k_lgrad(me_ref, comb_ref, rim_ref, place_ref, slot_ref, lg_ref, one_ref, two_ref):
    rim = rim_ref.shape[0] // 2
    lg = comb_ref[...] + dot(place_ref[:, 0:rim], rim_ref[rim:, :]) + dot(place_ref[:, rim:], rim_ref[0:rim, :])
    lg = lg.astype(BF)
    lg_ref[...] = lg
    send_slots(me_ref[1], lg, slot_ref, one_ref, two_ref)


def k_cgrad(me_ref, pool_ref, got_ref, hits_ref, icount_ref, cpre_ref, cw_ref,
            pgrad_ref, spread_ref, out1_ref, out2_ref):
    cap = out1_ref.shape[0]
    hits = hits_ref[...]
    total = pool_ref[...] + dot(hits.astype(BF), arrived_of(got_ref, cap))
    pgrad = (total * slope_of(cpre_ref[...])).astype(BF)
    pgrad_ref[...] = pgrad
    spread = (dot(pgrad, cw_ref[...]) * wide(icount_ref[...], pgrad.shape[1])).astype(BF)
    spread_ref[...] = spread
    ans = dot(hits.T.astype(BF), spread).astype(BF)
    sub = me_ref[1]
    out1_ref[...] = jnp.where(sub == 0, ans[cap:2 * cap], ans[0:cap])
    out2_ref[...] = jnp.where(sub == 0, ans[3 * cap:], ans[2 * cap:3 * cap])


def k_cweight(scale, me_ref, pgrad_ref, coarse_ref, out_ref):
    half = out_ref.shape[0]
    at = pl.multiple_of(me_ref[1] * half, half)
    out_ref[...] = dot(pgrad_ref[:, pl.ds(at, half)].T, coarse_ref[...]) * scale


def k_third(me_ref, lg_ref, hot_ref, slott_ref, spread_ref, got_ref, wo_ref, slope_ref,
            win_ref, inv_ref, adjt_ref, *rest, scale=None):
    fb_ref, pg_ref, scaled_ref, before_ref, after_ref = rest[-5:] if scale is None else rest[3:8]
    fb = spread_back(lg_ref[...], hot_ref, slott_ref, spread_ref[...], got_ref)
    fb_ref[...] = fb
    pg = (dot(fb, wo_ref[...]) * slope_ref[...]).astype(BF)
    pg_ref[...] = pg
    if scale is not None:
        xc_ref, agg_ref, hid_ref = rest[:3]
        pack_grads(scale, me_ref[1], pg_ref, xc_ref, agg_ref, fb_ref, hid_ref, rest[8])
    n, width = fb.shape
    half = width // 2
    rim = before_ref.shape[0]
    scaled = (dot(pg, win_ref[:, width:]) * wide(inv_ref[...], width)).astype(BF)
    scaled_ref[...] = scaled
    at = pl.multiple_of(me_ref[1] * half, half)
    both = dot(adjt_ref[n:, :], scaled_ref[:, pl.ds(at, half)]).astype(BF)
    before_ref[...] = both[0:rim]
    after_ref[...] = both[rim:]


def k_last(comb_ref, after_ref, before_ref, place_ref, out_ref):
    rim = after_ref.shape[0]
    total = comb_ref[...] + dot(place_ref[:, 0:rim], after_ref[...]) + dot(place_ref[:, rim:], before_ref[...])
    out_ref[...] = total.T


def k_halfcomb(me_ref, fb_ref, pg_ref, win_ref, scaled_ref, adjt_ref, comb_ref):
    n, half = comb_ref.shape
    at = pl.multiple_of(me_ref[1] * half, half)
    cols = pl.ds(at, half)
    comb_ref[...] = (
        fb_ref[:, cols].astype(F32)
        + dot(pg_ref[...], win_ref[:, cols])
        + dot(adjt_ref[0:n, :], scaled_ref[:, cols])
    )


def summed(ref):
    total = ref[0].astype(F32)
    for d in range(1, ref.shape[0]):
        total = total + ref[d].astype(F32)
    return total


def unpack_small(total):
    small = total.shape[0] // 2
    return jnp.concatenate([total[0:small], total[small:]], axis=1)


def k_sum(early_ref, coarse_ref, ein_ref, eout_ref, gco_ref):
    half = ein_ref.shape[0]
    total = summed(early_ref)
    ein_ref[...] = total[0:half]
    eout_ref[...] = unpack_small(total[half:])
    gco_ref[...] = unpack_small(summed(coarse_ref))


def k_sum_late(late_ref, ein_ref, eout_ref, gin_ref, gout_ref):
    half = ein_ref.shape[0]
    total = summed(late_ref)
    gin_ref[0] = total[0:half]
    gin_ref[1] = ein_ref[...]
    gout_ref[0] = unpack_small(total[half:])
    gout_ref[1] = eout_ref[...]


def local(node_features, inward_weight, outward_weight, coarse_weight, tile_index, tile_mask,
          send_rows, parent, cotangent):
    half, n = node_features.shape
    width = 2 * half
    blocks, k_slots = tile_index.shape
    rim = tile_mask.shape[2]
    src_rows = (blocks + 2) * rim
    domains = lax.axis_size(DOM)
    cross = lax.axis_size("cross")
    curve = lax.axis_size("curve")
    cap = n // 16
    nodes = n // 4
    slots = 4 * cap
    hidden = 2 * inward_weight.shape[1]
    scale = float(n * domains) ** -0.5
    me = jnp.stack([lax.axis_index(DOM), lax.axis_index("sub")]).astype(I32)
    rows = send_rows[0]
    packed = 2 * width // domains == 128

    halo_next, halo_prev = call(
        k_halo, [sds((half, rim), BF)] * 2, [], [rows, node_features], "halo")
    before_half = shifted(halo_next, 1)
    after_half = shifted(halo_prev, -1)
    win2, wout2 = swap(inward_weight), swap(outward_weight)
    x_full = gather(node_features)
    (adj, adjt, inv, hott, hot, slot, slott, pick, place, tags, ocount) = call(
        k_prep,
        [sds((n, src_rows), BF), sds((src_rows, n), BF), sds((n, 128), F32), sds((nodes, n), BF),
         sds((n, nodes), BF), sds((slots, n), BF), sds((n, slots), BF), sds((2 * rim, n), BF),
         sds((n, 2 * rim), BF), sds((16, slots), BF), sds((nodes, 128), F32)],
        [tile_index, me], [tile_mask, rows, parent[None, :]], "prep")
    win0, win1, wo0, wo1 = call(
        k_weights, [sds((hidden, 2 * width), BF)] * 2 + [sds((width, hidden), BF)] * 2,
        [me], [inward_weight, outward_weight, win2, wout2], "weights")
    rims = gather(jnp.concatenate([before_half, after_half], axis=0)).reshape(2, width, rim)
    msg = sds((cap + 16, width), BF)
    plain = sds((cap, width), BF)
    cell_bf, cell_f32 = sds((n, width), BF), sds((n, width), F32)
    hid_bf, hid_f32 = sds((n, hidden), BF), sds((n, hidden), F32)
    xc, agg0, pre0, hid0, first, one, two = call(
        k_first,
        [cell_bf, cell_bf, hid_f32, hid_bf, cell_bf, msg, msg],
        [me], [x_full, rims, adj, inv, win0, wo0, slot, tags], "first",
        flops=2 * n * width * (src_rows + 3 * width),
        scratch=[pltpu.VMEM((src_rows, width), BF)])
    one, two, cotangent, coarse_weight = lax.optimization_barrier((one, two, cotangent, coarse_weight))
    one, two = two_way(one, 1), two_way(two, 2)
    own, slope0 = call(k_own, [sds((nodes, width), F32), hid_f32], [], [hott, first, pre0], "own")
    cw = gather(coarse_weight)
    got = gather(jnp.concatenate([one, two], axis=0)).reshape(2, -1, width)
    node_bf, node_f32 = sds((nodes, width), BF), sds((nodes, width), F32)
    hits, icount, coarse, cpre, corr, one, two = call(
        k_coarse, [sds((nodes, slots), F32), sds((nodes, 128), F32), node_bf, node_f32, node_bf, plain, plain],
        [me], [own, ocount, got, cw], "coarse")
    one, two, cotangent = lax.optimization_barrier((one, two, cotangent))
    one, two = two_way(one, 1), two_way(two, 2)
    ct_full = gather(cotangent)
    ctc, hg1 = call(k_cot, [cell_bf, hid_f32], [], [ct_full, wo1], "cot")
    got = gather(jnp.concatenate([one, two], axis=0)).reshape(2, -1, width)
    lifted, rims = call(
        k_lift, [cell_bf, sds((rim, width), BF)], [me],
        [first, hot, slott, corr, got, pick], "lift")
    rims = gather(two_way(rims, 1))
    agg1, hid1, new, pg1, scaled1, rims = call(
        k_second, [cell_bf, hid_bf, cell_bf, hid_bf, cell_bf, sds((rim, width), BF)],
        [me], [lifted, rims, adj, adjt, inv, win1, wo1, hg1], "second",
        scratch=[pltpu.VMEM((src_rows, width), BF)])
    rims = two_way(rims, 1)
    piece = 2 * width // domains
    small = hidden // domains
    pack = sds((domains, half + 2 * small, piece), BF)
    if packed:
        comb1, early = call(lambda *r: k_combine_pack(scale, *r), [cell_f32, pack], [me],
                            [pg1, lifted, agg1, ctc, hid1, win1, scaled1, adjt], "combine")
    else:
        comb1, = call(k_combine, [cell_f32], [], [ctc, pg1, win1, scaled1, adjt], "combine")
    rims = gather(rims)
    lg, one, two = call(
        k_lgrad, [cell_bf, plain, plain], [me], [comb1, rims, place, slot], "lgrad")
    if packed:
        one, two, early = lax.optimization_barrier((one, two, early))
    one, two = two_way(one, 1), two_way(two, 2)
    own_g, = call(k_pool, [node_f32], [], [hott, lg], "own_grad")
    new_t, = call(k_newt, [sds((half, n), BF)], [me], [new], "new")
    got = gather(jnp.concatenate([one, two], axis=0)).reshape(2, -1, width)
    pgrad, spread, one, two = call(
        k_cgrad, [node_bf, node_bf, plain, plain], [me],
        [own_g, got, hits, icount, cpre, cw], "cgrad")
    one, two = two_way(one, 1), two_way(two, 2)
    got = gather(jnp.concatenate([one, two], axis=0)).reshape(2, -1, width)
    rim_half = sds((rim, half), BF)
    back_outs = [cell_bf, hid_bf, cell_bf, rim_half, rim_half]
    back_args = [lg, hot, slott, spread, got, wo0, slope0, win0, inv, adjt]
    if packed:
        early = lax.all_to_all(early, DOM, 0, 0, tiled=True)
        gco, = call(lambda *r: k_cweight_pack(scale, *r), [sds((domains, 2 * small, piece), BF)], [me],
                    [pgrad, coarse], "cweight")
        gco = lax.all_to_all(gco, DOM, 0, 0, tiled=True)
        fb, pg0, scaled0, to_before, to_after, late = call(
            lambda *r: k_third(*r, scale=scale), back_outs + [pack], [me], back_args + [xc, agg0, hid0], "third")
        late = lax.all_to_all(late, DOM, 0, 0, tiled=True)
    else:
        gco, = call(lambda *r: k_cweight(scale, *r), [sds((half, width), F32)], [me], [pgrad, coarse], "cweight")
        fb, pg0, scaled0, to_before, to_after = call(k_third, back_outs, [me], back_args, "third")
    from_after = shifted(to_before, -1)
    from_before = shifted(to_after, 1)
    comb0, = call(k_halfcomb, [sds((n, half), F32)], [me], [fb, pg0, win0, scaled0, adjt], "halfcomb")
    fgrad, = call(k_last, [sds((half, n), F32)], [], [comb0, from_after, from_before, place], "last")
    if packed:
        ein, eout, gco = call(
            k_sum, [sds((half, piece), F32), sds((small, half), F32), sds((small, half), F32)],
            [], [early, gco], "sums")
        gin, gout = call(
            k_sum_late, [sds((2, half, piece), F32), sds((2, small, half), F32)], [], [late, ein, eout], "late")
        gout = gout.swapaxes(1, 2)
        gco = gco.T
    else:
        shapes = [sds((half, 2 * width), F32), sds((half, hidden), F32)]
        gi1, go1 = call(lambda *r: k_grads(scale, *r), shapes, [me], [pg1, lifted, agg1, ctc, hid1], "grads1")
        gi0, go0 = call(lambda *r: k_grads(scale, *r), shapes, [me], [pg0, xc, agg0, fb, hid0], "grads0")
        gin = lax.psum_scatter(jnp.stack([gi0, gi1]), DOM, scatter_dimension=2, tiled=True)
        gout = lax.psum_scatter(jnp.stack([go0, go1]), DOM, scatter_dimension=2, tiled=True)
        gco = lax.psum_scatter(gco, DOM, scatter_dimension=1, tiled=True)
    return new_t, fgrad, gin, gout, gco


def solution(mesh):
    cells = ("groups", "curve", "cross")
    in_specs = (
        P("sub", cells),
        P(None, "sub", None),
        P(None, "sub", None),
        P("sub", None),
        P(cells, None),
        P(cells, None, None, None),
        P(cells, None, None),
        P(cells),
        P("sub", cells),
    )
    out_specs = (
        P("sub", cells),
        P("sub", cells),
        P("groups", "sub", ("curve", "cross")),
        P("groups", "sub", ("curve", "cross")),
        P(("groups", "sub"), ("curve", "cross")),
    )
    return jax.shard_map(local, mesh=mesh, in_specs=in_specs, out_specs=out_specs, check_vma=False)
```

```python
import jax
import jax.numpy as jnp
from jax import lax
from jax.experimental import pallas as pl
from jax.experimental.pallas import tpu as pltpu
from jax.sharding import PartitionSpec as P

BF = jnp.bfloat16
F32 = jnp.float32
I32 = jnp.int32
DOM = ("curve", "cross")
LINE = ("curve", "cross", "sub")
NN = (((1,), (0,)), ((), ()))
NT = (((1,), (1,)), ((), ()))
TN = (((0,), (0,)), ((), ()))


def dot(a, b, dims=NN):
    return lax.dot_general(a, b, dims, preferred_element_type=F32)


def sds(shape, dtype):
    return jax.ShapeDtypeStruct(shape, dtype)


def call(body, outs, scalars, arrays, name, flops=0, scratch=()):
    scalars, arrays = list(scalars), list(arrays)
    moved = sum(a.size * a.dtype.itemsize for a in arrays) + sum(
        o.size * o.dtype.itemsize for o in outs
    )
    return pl.pallas_call(
        body,
        out_shape=tuple(outs),
        in_specs=[pl.BlockSpec(memory_space=pltpu.SMEM)] * len(scalars)
        + [pl.BlockSpec(memory_space=pltpu.VMEM)] * len(arrays),
        out_specs=tuple(pl.BlockSpec(memory_space=pltpu.VMEM) for _ in outs),
        scratch_shapes=list(scratch),
        compiler_params=pltpu.CompilerParams(vmem_limit_bytes=20 * 2**20),
        cost_estimate=pl.CostEstimate(flops=flops, bytes_accessed=moved, transcendentals=0),
        name=name,
    )(*scalars, *arrays)


def shifted(value, steps):
    count = lax.axis_size(DOM)
    first, last = (max(0, -steps), min(count, count - steps))
    return lax.ppermute(value, DOM, [(s, s + steps) for s in range(first, last)])


def two_way(value, steps):
    count = lax.axis_size(DOM)
    pairs = [(2 * p, 2 * (p + steps)) for p in range(count - steps)]
    pairs += [(2 * p + 1, 2 * (p - steps) + 1) for p in range(steps, count)]
    return lax.ppermute(value, LINE, pairs)


def gather(value):
    return lax.all_gather(value, "sub", axis=0, tiled=True)


def swap(value):
    return lax.ppermute(value, "sub", [(0, 1), (1, 0)])


def cross_swap(value):
    return lax.ppermute(value, "cross", [(0, 1), (1, 0)])


def curve_swap(value, step):
    return lax.ppermute(value, "curve", [(z, z ^ step) for z in range(4)])


def sigmoid(v):
    return 1.0 / (1.0 + jnp.exp(-v))


def slope_of(v):
    s = sigmoid(v)
    return s * (1.0 + v * (1.0 - s))


def wide(col, width):
    return jnp.concatenate([col] * (width // col.shape[1]), axis=1)


def k_halo(rows_ref, x_ref, next_ref, prev_ref):
    x = x_ref[...]
    n = x.shape[1]
    at = lax.broadcasted_iota(I32, (n, rows_ref.shape[1]), 0)
    next_ref[...] = dot(x, (at == rows_ref[0:1, :]).astype(BF)).astype(BF)
    prev_ref[...] = dot(x, (at == rows_ref[1:2, :]).astype(BF)).astype(BF)


def k_weights(layer, me_ref, win_ref, wout_ref, win2_ref, wout2_ref, in_ref, out_ref):
    half = win_ref.shape[1]
    own = pl.multiple_of(me_ref[1] * half, half)
    other = pl.multiple_of((1 - me_ref[1]) * half, half)
    in_ref[pl.ds(own, half), :] = win_ref[layer]
    in_ref[pl.ds(other, half), :] = win2_ref[layer]
    out_ref[pl.ds(own, half), :] = wout_ref[layer]
    out_ref[pl.ds(other, half), :] = wout2_ref[layer]


def k_prep(tile_ref, me_ref, mask_ref, rows_ref, par_ref,
           adj_ref, adjt_ref, inv_ref, hott_ref, hot_ref, slot_ref, slott_ref,
           pick_ref, place_ref, tags_ref, ocount_ref):
    blocks, k_slots, length, _ = mask_ref.shape
    n = adj_ref.shape[0]
    nodes = hott_ref.shape[0]
    slots = slot_ref.shape[0]
    cap = slots // 4
    adj_ref[...] = jnp.zeros(adj_ref.shape, BF)
    adjt_ref[...] = jnp.zeros(adjt_ref.shape, BF)
    for b in range(blocks):
        degree = jnp.zeros((length, 1), F32)
        for k in range(k_slots):
            bits = mask_ref[b, k].astype(F32)
            start = pl.multiple_of(tile_ref[b, k] * length, length)
            adj_ref[b * length:(b + 1) * length, pl.ds(start, length)] = bits.astype(BF)
            adjt_ref[pl.ds(start, length), b * length:(b + 1) * length] = bits.T.astype(BF)
            degree = degree + jnp.sum(bits, axis=1, keepdims=True)
        inv_ref[b * length:(b + 1) * length, :] = jnp.broadcast_to(1.0 / degree, (length, 128))
    rel_row = par_ref[...] - me_ref[0] * nodes
    hott = (lax.broadcasted_iota(I32, (nodes, n), 0) == rel_row).astype(F32)
    hott_ref[...] = hott.astype(BF)
    ocount_ref[...] = jnp.broadcast_to(jnp.sum(hott, axis=1, keepdims=True), (nodes, 128))
    hot_ref[...] = hott.T.astype(BF)
    j = lax.broadcasted_iota(I32, (slots, n), 0)
    off = jnp.where(j < cap, 1, jnp.where(j < 2 * cap, -1, jnp.where(j < 3 * cap, 2, -2)))
    start = jnp.where(j < cap, 0, jnp.where(j < 2 * cap, cap, jnp.where(j < 3 * cap, 2 * cap, 3 * cap)))
    node = rel_row - off * nodes
    chosen = ((node >= 0) & (node < nodes)).astype(F32)
    before = lax.broadcasted_iota(I32, (n, n), 0) < lax.broadcasted_iota(I32, (n, n), 1)
    rank = dot(chosen.astype(BF), before.astype(F32).astype(BF))
    fits = jnp.where(rank == (j - start).astype(F32), chosen, 0.0)
    slot_ref[...] = fits.astype(BF)
    slott_ref[...] = fits.T.astype(BF)
    tags = jnp.sum(fits * (node + 1).astype(F32), axis=1, keepdims=True)
    tags_ref[...] = jnp.broadcast_to(tags, (slots, slots)).T[0:tags_ref.shape[0], :].astype(BF)
    width = rows_ref.shape[1]
    at = lax.broadcasted_iota(I32, (n, width), 0)
    for c in range(2):
        place = (at == rows_ref[c:c + 1, :]).astype(F32)
        place_ref[:, c * width:(c + 1) * width] = place.astype(BF)
        pick_ref[c * width:(c + 1) * width, :] = place.T.astype(BF)


def forward(xc, src, adj_ref, inv_ref, win_ref, wo_ref):
    width = xc.shape[1]
    agg = (dot(adj_ref[...], src) * wide(inv_ref[...], width)).astype(BF)
    pre = dot(xc, win_ref[:, 0:width], NT) + dot(agg, win_ref[:, width:], NT)
    hid = (pre * sigmoid(pre)).astype(BF)
    out = (xc.astype(F32) + dot(hid, wo_ref[...], NT)).astype(BF)
    return agg, pre, hid, out


def send_slots(sub, values, slot_ref, one_ref, two_ref):
    cap = slot_ref.shape[0] // 4
    a = pl.multiple_of(sub * cap, cap)
    one_ref[0:cap, :] = dot(slot_ref[pl.ds(a, cap), :], values).astype(BF)
    two_ref[0:cap, :] = dot(slot_ref[pl.ds(a + 2 * cap, cap), :], values).astype(BF)


def k_first(me_ref, x_ref, rims_ref, adj_ref, inv_ref, win_ref, wo_ref,
            slot_ref, tags_ref,
            xc_ref, agg_ref, pre_ref, hid_ref, first_ref, one_ref, two_ref, src):
    n = x_ref.shape[1]
    rim = rims_ref.shape[2]
    half = rims_ref.shape[1] // 2
    xc = x_ref[...].T
    xc_ref[...] = xc
    src[0:n, :] = xc
    for c in range(2):
        src[n:n + rim, c * half:(c + 1) * half] = rims_ref[c, 0:half, :].T
        src[n + rim:, c * half:(c + 1) * half] = rims_ref[c, half:, :].T
    agg, pre, hid, out = forward(xc, src[...], adj_ref, inv_ref, win_ref, wo_ref)
    agg_ref[...] = agg
    pre_ref[...] = pre
    hid_ref[...] = hid
    first_ref[...] = out
    send_slots(me_ref[1], out, slot_ref, one_ref, two_ref)
    cap = slot_ref.shape[0] // 4
    pad = wide(tags_ref[...], one_ref.shape[1])
    one_ref[cap:, :] = pad
    two_ref[cap:, :] = pad


def k_own(hott_ref, v_ref, pre_ref, pool_ref, slope_ref):
    pool_ref[...] = dot(hott_ref[...], v_ref[...])
    slope_ref[...] = slope_of(pre_ref[...])


def k_pool(hott_ref, v_ref, pool_ref):
    pool_ref[...] = dot(hott_ref[...], v_ref[...])


def k_cot(ct_ref, wo_ref, ctc_ref, hg_ref):
    ctc = ct_ref[...].T
    ctc_ref[...] = ctc
    hg_ref[...] = dot(ctc, wo_ref[...])


def arrived_of(got_ref, cap):
    rows = got_ref.shape[1] // 2
    return jnp.concatenate(
        [got_ref[0, 0:cap], got_ref[1, 0:cap], got_ref[0, rows:rows + cap], got_ref[1, rows:rows + cap]],
        axis=0,
    )


def k_coarse(me_ref, pool_ref, ocount_ref, got_ref, cw_ref,
             hits_ref, icount_ref, coarse_ref, cpre_ref, corr_ref, out1_ref, out2_ref):
    nodes, width = pool_ref.shape
    cap = out1_ref.shape[0]
    rows = got_ref.shape[1] // 2
    slots = 4 * cap
    lane = lax.broadcasted_iota(I32, (1, slots), 1)
    t = [got_ref[c, o + cap:o + cap + 1, 0:slots].astype(F32) for o in (0, rows) for c in range(2)]
    tags = jnp.where(lane < cap, t[0], jnp.where(lane < 2 * cap, t[1], jnp.where(lane < 3 * cap, t[2], t[3])))
    node = (lax.broadcasted_iota(I32, (nodes, slots), 0) + 1).astype(F32)
    hits = (node == tags).astype(F32)
    count = jnp.maximum(ocount_ref[...] + jnp.sum(hits, axis=1, keepdims=True), 1.0)
    icount = 1.0 / count
    hits_ref[...] = hits
    icount_ref[...] = icount
    hb = hits.astype(BF)
    total = pool_ref[...] + dot(hb, arrived_of(got_ref, cap))
    coarse = (total * wide(icount, width)).astype(BF)
    cpre = dot(coarse, cw_ref[...], NT)
    corr = (cpre * sigmoid(cpre)).astype(BF)
    coarse_ref[...] = coarse
    cpre_ref[...] = cpre
    corr_ref[...] = corr
    ans = dot(hits.T.astype(BF), corr).astype(BF)
    sub = me_ref[1]
    out1_ref[...] = jnp.where(sub == 0, ans[cap:2 * cap], ans[0:cap])
    out2_ref[...] = jnp.where(sub == 0, ans[3 * cap:], ans[2 * cap:3 * cap])


def spread_back(first, hot_ref, slott_ref, corr, got_ref):
    cap = got_ref.shape[1] // 2
    returned = jnp.concatenate(
        [got_ref[1, 0:cap], got_ref[0, 0:cap], got_ref[1, cap:], got_ref[0, cap:]], axis=0
    )
    total = first.astype(F32) + dot(hot_ref[...], corr) + dot(slott_ref[...], returned)
    return total.astype(BF)


def k_lift(me_ref, first_ref, hot_ref, slott_ref, corr_ref, got_ref, pick_ref,
           lift_ref, msg_ref):
    lifted = spread_back(first_ref[...], hot_ref, slott_ref, corr_ref[...], got_ref)
    lift_ref[...] = lifted
    rim = msg_ref.shape[0]
    at = pl.multiple_of(me_ref[1] * rim, rim)
    msg_ref[...] = dot(pick_ref[pl.ds(at, rim), :], lifted).astype(BF)


def rim_grads(sub, pg, win_ref, inv_ref, adjt_ref, scaled_ref, msg_ref):
    n = pg.shape[0]
    width = win_ref.shape[1] // 2
    rim = msg_ref.shape[0]
    scaled = (dot(pg, win_ref[:, width:]) * wide(inv_ref[...], width)).astype(BF)
    scaled_ref[...] = scaled
    at = pl.multiple_of(n + (1 - sub) * rim, rim)
    msg_ref[...] = dot(adjt_ref[pl.ds(at, rim), :], scaled).astype(BF)


def k_second(me_ref, lift_ref, rim_ref, adj_ref, adjt_ref, inv_ref, win_ref, wo_ref, hg_ref,
             agg_ref, hid_ref, new_ref, pg_ref, scaled_ref, msg_ref, src):
    n = lift_ref.shape[0]
    lifted = lift_ref[...]
    src[0:n, :] = lifted
    src[n:, :] = rim_ref[...]
    agg, pre, hid, out = forward(lifted, src[...], adj_ref, inv_ref, win_ref, wo_ref)
    agg_ref[...] = agg
    hid_ref[...] = hid
    new_ref[...] = out
    pg = (hg_ref[...] * slope_of(pre)).astype(BF)
    pg_ref[...] = pg
    rim_grads(me_ref[1], pg, win_ref, inv_ref, adjt_ref, scaled_ref, msg_ref)


def k_combine(g_ref, pg_ref, win_ref, scaled_ref, adjt_ref, comb_ref):
    n, width = comb_ref.shape
    comb_ref[...] = (
        g_ref[...].astype(F32)
        + dot(pg_ref[...], win_ref[:, 0:width])
        + dot(adjt_ref[0:n, :], scaled_ref[...])
    )


def k_newt(me_ref, new_ref, out_ref):
    half = out_ref.shape[0]
    at = pl.multiple_of(me_ref[1] * half, half)
    out_ref[...] = new_ref[:, pl.ds(at, half)].T


def k_grads(scale, me_ref, pg_ref, h_ref, agg_ref, g_ref, hid_ref, gin_ref, gout_ref):
    half = gin_ref.shape[0]
    width = h_ref.shape[1]
    at = pl.multiple_of(me_ref[1] * half, half)
    pgt = pg_ref[:, pl.ds(at, half)].T
    gin_ref[:, 0:width] = dot(pgt, h_ref[...]) * scale
    gin_ref[:, width:] = dot(pgt, agg_ref[...]) * scale
    gt = g_ref[:, pl.ds(at, half)].T
    gout_ref[...] = dot(gt, hid_ref[...]) * scale


def pack_grads(scale, me_ref, pg_ref, h_ref, agg_ref, g_ref, hid_ref, keep_ref, send_ref):
    width = h_ref.shape[1]
    half = width // 2
    piece = keep_ref.shape[2]
    at = pl.multiple_of(me_ref[1] * half, half)
    pgt = pg_ref[:, pl.ds(at, half)].T
    lo = dot(pgt, h_ref[...]) * scale
    hi = dot(pgt, agg_ref[...]) * scale
    out = dot(hid_ref[...].T, g_ref[:, pl.ds(at, half)]) * scale

    def pieces(d):
        src, c = (lo, d * piece) if d * piece < width else (hi, d * piece - width)
        return [(0, src[:, c:c + piece])] + small_pieces(out, d, piece, half)

    place_pieces(me_ref, pieces, keep_ref, send_ref)


def small_pieces(values, d, piece, row):
    small = values.shape[0] // 8
    mine = values[d * small:(d + 1) * small]
    return [
        (row + c * small, mine[:, c * piece:(c + 1) * piece]) for c in range(values.shape[1] // piece)
    ]


def place_pieces(me_ref, pieces, keep_ref, send_ref):
    for d in range(8):
        for row, value in pieces(d):
            rows = slice(row, row + value.shape[0])

            @pl.when(me_ref[2] == d % 2)
            def _():
                keep_ref[d // 2, rows, :] = value

            @pl.when(me_ref[2] != d % 2)
            def _():
                send_ref[d // 2, rows, :] = value.astype(BF)


def k_combine_pack(scale, me_ref, pg_ref, h_ref, agg_ref, g_ref, hid_ref, win_ref, scaled_ref, adjt_ref,
                   comb_ref, keep_ref, send_ref):
    k_combine(g_ref, pg_ref, win_ref, scaled_ref, adjt_ref, comb_ref)
    pack_grads(scale, me_ref, pg_ref, h_ref, agg_ref, g_ref, hid_ref, keep_ref, send_ref)


def k_cweight_pack(scale, me_ref, pgrad_ref, coarse_ref, keep_ref, send_ref):
    half = pgrad_ref.shape[1] // 2
    piece = keep_ref.shape[2]
    at = pl.multiple_of(me_ref[1] * half, half)
    values = dot(coarse_ref[...].T, pgrad_ref[:, pl.ds(at, half)]) * scale
    place_pieces(me_ref, lambda d: small_pieces(values, d, piece, 0), keep_ref, send_ref)


def k_lgrad(me_ref, comb_ref, rim_ref, place_ref, slot_ref, lg_ref, one_ref, two_ref):
    rim = rim_ref.shape[0] // 2
    lg = comb_ref[...] + dot(place_ref[:, 0:rim], rim_ref[rim:, :]) + dot(place_ref[:, rim:], rim_ref[0:rim, :])
    lg = lg.astype(BF)
    lg_ref[...] = lg
    send_slots(me_ref[1], lg, slot_ref, one_ref, two_ref)


def k_cgrad(me_ref, pool_ref, got_ref, hits_ref, icount_ref, cpre_ref, cw_ref,
            pgrad_ref, spread_ref, out1_ref, out2_ref):
    cap = out1_ref.shape[0]
    hits = hits_ref[...]
    total = pool_ref[...] + dot(hits.astype(BF), arrived_of(got_ref, cap))
    pgrad = (total * slope_of(cpre_ref[...])).astype(BF)
    pgrad_ref[...] = pgrad
    spread = (dot(pgrad, cw_ref[...]) * wide(icount_ref[...], pgrad.shape[1])).astype(BF)
    spread_ref[...] = spread
    ans = dot(hits.T.astype(BF), spread).astype(BF)
    sub = me_ref[1]
    out1_ref[...] = jnp.where(sub == 0, ans[cap:2 * cap], ans[0:cap])
    out2_ref[...] = jnp.where(sub == 0, ans[3 * cap:], ans[2 * cap:3 * cap])


def k_cweight(scale, me_ref, pgrad_ref, coarse_ref, out_ref):
    half = out_ref.shape[0]
    at = pl.multiple_of(me_ref[1] * half, half)
    out_ref[...] = dot(pgrad_ref[:, pl.ds(at, half)].T, coarse_ref[...]) * scale


def k_third(me_ref, lg_ref, hot_ref, slott_ref, spread_ref, got_ref, wo_ref, slope_ref,
            win_ref, inv_ref, adjt_ref, *rest, scale=None):
    fb_ref, pg_ref, scaled_ref, before_ref, after_ref = rest[-5:] if scale is None else rest[3:8]
    fb = spread_back(lg_ref[...], hot_ref, slott_ref, spread_ref[...], got_ref)
    fb_ref[...] = fb
    pg = (dot(fb, wo_ref[...]) * slope_ref[...]).astype(BF)
    pg_ref[...] = pg
    if scale is not None:
        xc_ref, agg_ref, hid_ref = rest[:3]
        pack_grads(scale, me_ref, pg_ref, xc_ref, agg_ref, fb_ref, hid_ref, rest[8], rest[9])
    n, width = fb.shape
    half = width // 2
    rim = before_ref.shape[0]
    scaled = (dot(pg, win_ref[:, width:]) * wide(inv_ref[...], width)).astype(BF)
    scaled_ref[...] = scaled
    at = pl.multiple_of(me_ref[1] * half, half)
    both = dot(adjt_ref[n:, :], scaled_ref[:, pl.ds(at, half)]).astype(BF)
    before_ref[...] = both[0:rim]
    after_ref[...] = both[rim:]


def k_last(comb_ref, after_ref, before_ref, place_ref, out_ref):
    rim = after_ref.shape[0]
    total = comb_ref[...] + dot(place_ref[:, 0:rim], after_ref[...]) + dot(place_ref[:, rim:], before_ref[...])
    out_ref[...] = total.T


def k_halfcomb(me_ref, fb_ref, pg_ref, win_ref, scaled_ref, adjt_ref, comb_ref):
    n, half = comb_ref.shape
    at = pl.multiple_of(me_ref[1] * half, half)
    cols = pl.ds(at, half)
    comb_ref[...] = (
        fb_ref[:, cols].astype(F32)
        + dot(pg_ref[...], win_ref[:, cols])
        + dot(adjt_ref[0:n, :], scaled_ref[:, cols])
    )


def k_stage(me_ref, *refs):
    pairs = (len(refs) - 4) // 2
    own_ref, outs = refs[2 * pairs], refs[2 * pairs + 1:]
    z = me_ref[3]
    row = 0
    for i in range(pairs):
        keep_ref, got_ref = refs[2 * i], refs[2 * i + 1]
        rows = slice(row, row + keep_ref.shape[1])
        own_ref[rows, :] = keep_ref[z] + got_ref[z].astype(F32)
        for step in (1, 2, 3):
            other = z ^ step
            outs[step - 1][rows, :] = (keep_ref[other] + got_ref[other].astype(F32)).astype(BF)
        row += keep_ref.shape[1]


def unpack_small(total):
    small = total.shape[0] // 2
    return jnp.concatenate([total[0:small], total[small:]], axis=1)


def k_sum(own_ref, a_ref, b_ref, c_ref, ein_ref, eout_ref, gco_ref):
    half = ein_ref.shape[0]
    mid = half + 2 * eout_ref.shape[0]
    total = own_ref[...] + a_ref[...].astype(F32) + b_ref[...].astype(F32) + c_ref[...].astype(F32)
    ein_ref[...] = total[0:half]
    eout_ref[...] = unpack_small(total[half:mid])
    gco_ref[...] = unpack_small(total[mid:])


def k_sum_late(own_ref, a_ref, b_ref, c_ref, ein_ref, eout_ref, gin_ref, gout_ref):
    half = ein_ref.shape[0]
    total = own_ref[...] + a_ref[...].astype(F32) + b_ref[...].astype(F32) + c_ref[...].astype(F32)
    gin_ref[0] = total[0:half]
    gin_ref[1] = ein_ref[...]
    gout_ref[0] = unpack_small(total[half:])
    gout_ref[1] = eout_ref[...]


def local(node_features, inward_weight, outward_weight, coarse_weight, tile_index, tile_mask,
          send_rows, parent, cotangent):
    half, n = node_features.shape
    width = 2 * half
    blocks, k_slots = tile_index.shape
    rim = tile_mask.shape[2]
    src_rows = (blocks + 2) * rim
    domains = lax.axis_size(DOM)
    cross = lax.axis_size("cross")
    curve = lax.axis_size("curve")
    cap = n // 16
    nodes = n // 4
    slots = 4 * cap
    hidden = 2 * inward_weight.shape[1]
    scale = float(n * domains) ** -0.5
    me = jnp.stack([lax.axis_index(a) for a in (DOM, "sub", "cross", "curve")]).astype(I32)
    rows = send_rows[0]
    packed = cross == 2 and curve == 4 and 2 * width == 1024 and hidden == width

    halo_next, halo_prev = call(
        k_halo, [sds((half, rim), BF)] * 2, [], [rows, node_features], "halo")
    before_half = shifted(halo_next, 1)
    after_half = shifted(halo_prev, -1)
    win2, wout2 = swap(inward_weight), swap(outward_weight)
    x_full = gather(node_features)
    (adj, adjt, inv, hott, hot, slot, slott, pick, place, tags, ocount) = call(
        k_prep,
        [sds((n, src_rows), BF), sds((src_rows, n), BF), sds((n, 128), F32), sds((nodes, n), BF),
         sds((n, nodes), BF), sds((slots, n), BF), sds((n, slots), BF), sds((2 * rim, n), BF),
         sds((n, 2 * rim), BF), sds((16, slots), BF), sds((nodes, 128), F32)],
        [tile_index, me], [tile_mask, rows, parent[None, :]], "prep")
    weight_outs = [sds((hidden, 2 * width), BF), sds((width, hidden), BF)]
    win0, wo0 = call(lambda *r: k_weights(0, *r), weight_outs, [me],
                     [inward_weight, outward_weight, win2, wout2], "weights0")
    rims = gather(jnp.concatenate([before_half, after_half], axis=0)).reshape(2, width, rim)
    msg = sds((cap + 16, width), BF)
    plain = sds((cap, width), BF)
    cell_bf, cell_f32 = sds((n, width), BF), sds((n, width), F32)
    hid_bf, hid_f32 = sds((n, hidden), BF), sds((n, hidden), F32)
    xc, agg0, pre0, hid0, first, one, two = call(
        k_first,
        [cell_bf, cell_bf, hid_f32, hid_bf, cell_bf, msg, msg],
        [me], [x_full, rims, adj, inv, win0, wo0, slot, tags], "first",
        flops=2 * n * width * (src_rows + 3 * width),
        scratch=[pltpu.VMEM((src_rows, width), BF)])
    one, two, win2, coarse_weight = lax.optimization_barrier((one, two, win2, coarse_weight))
    one, two = two_way(one, 1), two_way(two, 2)
    own, slope0 = call(k_own, [sds((nodes, width), F32), hid_f32], [], [hott, first, pre0], "own")
    cw = gather(coarse_weight)
    win1, wo1 = call(lambda *r: k_weights(1, *r), weight_outs, [me],
                     [inward_weight, outward_weight, win2, wout2], "weights1")
    got = gather(jnp.concatenate([one, two], axis=0)).reshape(2, -1, width)
    node_bf, node_f32 = sds((nodes, width), BF), sds((nodes, width), F32)
    hits, icount, coarse, cpre, corr, one, two = call(
        k_coarse, [sds((nodes, slots), F32), sds((nodes, 128), F32), node_bf, node_f32, node_bf, plain, plain],
        [me], [own, ocount, got, cw], "coarse")
    one, two, cotangent = lax.optimization_barrier((one, two, cotangent))
    one, two = two_way(one, 1), two_way(two, 2)
    ct_full = gather(cotangent)
    ctc, hg1 = call(k_cot, [cell_bf, hid_f32], [], [ct_full, wo1], "cot")
    got = gather(jnp.concatenate([one, two], axis=0)).reshape(2, -1, width)
    lifted, rims = call(
        k_lift, [cell_bf, sds((rim, width), BF)], [me],
        [first, hot, slott, corr, got, pick], "lift")
    rims = gather(two_way(rims, 1))
    agg1, hid1, new, pg1, scaled1, rims = call(
        k_second, [cell_bf, hid_bf, cell_bf, hid_bf, cell_bf, sds((rim, width), BF)],
        [me], [lifted, rims, adj, adjt, inv, win1, wo1, hg1], "second",
        scratch=[pltpu.VMEM((src_rows, width), BF)])
    rims = two_way(rims, 1)
    piece = 2 * width // domains
    small = hidden // domains
    layer_rows = half + 2 * small
    pack = [sds((curve, layer_rows, piece), F32), sds((curve, layer_rows, piece), BF)]
    if packed:
        comb1, keep1, send1 = call(lambda *r: k_combine_pack(scale, *r), [cell_f32] + pack, [me],
                            [pg1, lifted, agg1, ctc, hid1, win1, scaled1, adjt], "combine")
    else:
        comb1, = call(k_combine, [cell_f32], [], [ctc, pg1, win1, scaled1, adjt], "combine")
    rims = gather(rims)
    lg, one, two = call(
        k_lgrad, [cell_bf, plain, plain], [me], [comb1, rims, place, slot], "lgrad")
    if packed:
        one, two, send1 = lax.optimization_barrier((one, two, send1))
        got1 = cross_swap(send1)
    one, two = two_way(one, 1), two_way(two, 2)
    own_g, = call(k_pool, [node_f32], [], [hott, lg], "own_grad")
    new_t, = call(k_newt, [sds((half, n), BF)], [me], [new], "new")
    got = gather(jnp.concatenate([one, two], axis=0)).reshape(2, -1, width)
    pgrad, spread, one, two = call(
        k_cgrad, [node_bf, node_bf, plain, plain], [me],
        [own_g, got, hits, icount, cpre, cw], "cgrad")
    one, two = two_way(one, 1), two_way(two, 2)
    got = gather(jnp.concatenate([one, two], axis=0)).reshape(2, -1, width)
    rim_half = sds((rim, half), BF)
    back_outs = [cell_bf, hid_bf, cell_bf, rim_half, rim_half]
    back_args = [lg, hot, slott, spread, got, wo0, slope0, win0, inv, adjt]
    if packed:
        keepc, sendc = call(
            lambda *r: k_cweight_pack(scale, *r),
            [sds((curve, 2 * small, piece), F32), sds((curve, 2 * small, piece), BF)], [me],
            [pgrad, coarse], "cweight")
        gotc = cross_swap(sendc)
        fb, pg0, scaled0, to_before, to_after, keep0, send0 = call(
            lambda *r: k_third(*r, scale=scale), back_outs + pack, [me], back_args + [xc, agg0, hid0], "third")
        send0, gotc = lax.optimization_barrier((send0, gotc))
        got0 = cross_swap(send0)

        def staged(pairs, name):
            total = sum(keep.shape[1] for keep in pairs[::2])
            own, *outs = call(k_stage, [sds((total, piece), F32)] + [sds((total, piece), BF)] * 3, [me], pairs, name)
            return [own] + [curve_swap(value, step) for step, value in zip((1, 2, 3), outs)]

        early = staged([keep1, got1, keepc, gotc], "stage1")
        to_before, to_after, got0 = lax.optimization_barrier((to_before, to_after, got0))
        late = staged([keep0, got0], "stage0")
    else:
        gco, = call(lambda *r: k_cweight(scale, *r), [sds((half, width), F32)], [me], [pgrad, coarse], "cweight")
        fb, pg0, scaled0, to_before, to_after = call(k_third, back_outs, [me], back_args, "third")
    from_after = shifted(to_before, -1)
    from_before = shifted(to_after, 1)
    comb0, = call(k_halfcomb, [sds((n, half), F32)], [me], [fb, pg0, win0, scaled0, adjt], "halfcomb")
    fgrad, = call(k_last, [sds((half, n), F32)], [], [comb0, from_after, from_before, place], "last")
    if packed:
        ein, eout, gco = call(
            k_sum, [sds((half, piece), F32), sds((small, half), F32), sds((small, half), F32)],
            [], early, "sums")
        gin, gout = call(
            k_sum_late, [sds((2, half, piece), F32), sds((2, small, half), F32)], [], late + [ein, eout], "late")
        gout = gout.swapaxes(1, 2)
        gco = gco.T
    else:
        shapes = [sds((half, 2 * width), F32), sds((half, hidden), F32)]
        gi1, go1 = call(lambda *r: k_grads(scale, *r), shapes, [me], [pg1, lifted, agg1, ctc, hid1], "grads1")
        gi0, go0 = call(lambda *r: k_grads(scale, *r), shapes, [me], [pg0, xc, agg0, fb, hid0], "grads0")
        gin = lax.psum_scatter(jnp.stack([gi0, gi1]), DOM, scatter_dimension=2, tiled=True)
        gout = lax.psum_scatter(jnp.stack([go0, go1]), DOM, scatter_dimension=2, tiled=True)
        gco = lax.psum_scatter(gco, DOM, scatter_dimension=1, tiled=True)
    return new_t, fgrad, gin, gout, gco


def solution(mesh):
    cells = ("groups", "curve", "cross")
    in_specs = (
        P("sub", cells),
        P(None, "sub", None),
        P(None, "sub", None),
        P("sub", None),
        P(cells, None),
        P(cells, None, None, None),
        P(cells, None, None),
        P(cells),
        P("sub", cells),
    )
    out_specs = (
        P("sub", cells),
        P("sub", cells),
        P("groups", "sub", ("curve", "cross")),
        P("groups", "sub", ("curve", "cross")),
        P(("groups", "sub"), ("curve", "cross")),
    )
    return jax.shard_map(local, mesh=mesh, in_specs=in_specs, out_specs=out_specs, check_vma=False)
```

```python
import jax
import jax.numpy as jnp
from jax import lax
from jax.experimental import pallas as pl
from jax.experimental.pallas import tpu as pltpu
from jax.sharding import PartitionSpec as P

BF = jnp.bfloat16
F32 = jnp.float32
I32 = jnp.int32
DOM = ("curve", "cross")
LINE = ("curve", "cross", "sub")
NN = (((1,), (0,)), ((), ()))
NT = (((1,), (1,)), ((), ()))
TN = (((0,), (0,)), ((), ()))


def dot(a, b, dims=NN):
    return lax.dot_general(a, b, dims, preferred_element_type=F32)


def sds(shape, dtype):
    return jax.ShapeDtypeStruct(shape, dtype)


def call(body, outs, scalars, arrays, name, flops=0, scratch=()):
    scalars, arrays = list(scalars), list(arrays)
    moved = sum(a.size * a.dtype.itemsize for a in arrays) + sum(
        o.size * o.dtype.itemsize for o in outs
    )
    return pl.pallas_call(
        body,
        out_shape=tuple(outs),
        in_specs=[pl.BlockSpec(memory_space=pltpu.SMEM)] * len(scalars)
        + [pl.BlockSpec(memory_space=pltpu.VMEM)] * len(arrays),
        out_specs=tuple(pl.BlockSpec(memory_space=pltpu.VMEM) for _ in outs),
        scratch_shapes=list(scratch),
        compiler_params=pltpu.CompilerParams(vmem_limit_bytes=20 * 2**20),
        cost_estimate=pl.CostEstimate(flops=flops, bytes_accessed=moved, transcendentals=0),
        name=name,
    )(*scalars, *arrays)


def two_way(value, steps):
    count = lax.axis_size(DOM)
    pairs = [(2 * p, 2 * (p + steps)) for p in range(count - steps)]
    pairs += [(2 * p + 1, 2 * (p - steps) + 1) for p in range(steps, count)]
    pairs += [(2 * p, 2 * p + 1) for p in range(count - steps, count)]
    pairs += [(2 * p + 1, 2 * p) for p in range(steps)]
    return lax.ppermute(value, LINE, pairs)


def gather(value):
    return lax.all_gather(value, "sub", axis=0, tiled=True)


def swap(value):
    return lax.ppermute(value, "sub", [(0, 1), (1, 0)])


def cross_swap(value):
    return lax.ppermute(value, "cross", [(0, 1), (1, 0)])


def curve_swap(value, step):
    return lax.ppermute(value, "curve", [(z, z ^ step) for z in range(4)])


def sigmoid(v):
    return 1.0 / (1.0 + jnp.exp(-v))


def slope_of(v):
    s = sigmoid(v)
    return s * (1.0 + v * (1.0 - s))


def wide(col, width):
    return jnp.concatenate([col] * (width // col.shape[1]), axis=1)


def k_halo(me_ref, rows_ref, x_ref, xc_ref, msg_ref):
    xc = x_ref[...].T
    xc_ref[...] = xc
    row = jnp.where(me_ref[1] == 0, rows_ref[0:1, :], rows_ref[1:2, :])
    at = lax.broadcasted_iota(I32, (xc.shape[0], row.shape[1]), 0)
    pick = (at == row).astype(F32).T.astype(BF)
    msg_ref[...] = dot(pick, xc).astype(BF)


def k_weights(layer, me_ref, win_ref, wout_ref, win2_ref, wout2_ref, in_ref, out_ref):
    half = win_ref.shape[1]
    own = pl.multiple_of(me_ref[1] * half, half)
    other = pl.multiple_of((1 - me_ref[1]) * half, half)
    in_ref[pl.ds(own, half), :] = win_ref[layer]
    in_ref[pl.ds(other, half), :] = win2_ref[layer]
    out_ref[pl.ds(own, half), :] = wout_ref[layer]
    out_ref[pl.ds(other, half), :] = wout2_ref[layer]


def k_prep(tile_ref, me_ref, mask_ref, rows_ref, par_ref,
           adj_ref, adjt_ref, inv_ref, hott_ref, hot_ref, slot_ref, slott_ref,
           pick_ref, place_ref, tags_ref, ocount_ref):
    blocks, k_slots, length, _ = mask_ref.shape
    n = adj_ref.shape[0]
    nodes = hott_ref.shape[0]
    slots = slot_ref.shape[0]
    cap = slots // 4
    adj_ref[...] = jnp.zeros(adj_ref.shape, BF)
    adjt_ref[...] = jnp.zeros(adjt_ref.shape, BF)
    for b in range(blocks):
        degree = jnp.zeros((length, 1), F32)
        for k in range(k_slots):
            bits = mask_ref[b, k].astype(F32)
            start = pl.multiple_of(tile_ref[b, k] * length, length)
            adj_ref[b * length:(b + 1) * length, pl.ds(start, length)] = bits.astype(BF)
            adjt_ref[pl.ds(start, length), b * length:(b + 1) * length] = bits.T.astype(BF)
            degree = degree + jnp.sum(bits, axis=1, keepdims=True)
        inv_ref[b * length:(b + 1) * length, :] = jnp.broadcast_to(1.0 / degree, (length, 128))
    rel_row = par_ref[...] - me_ref[0] * nodes
    hott = (lax.broadcasted_iota(I32, (nodes, n), 0) == rel_row).astype(F32)
    hott_ref[...] = hott.astype(BF)
    ocount_ref[...] = jnp.broadcast_to(jnp.sum(hott, axis=1, keepdims=True), (nodes, 128))
    hot_ref[...] = hott.T.astype(BF)
    j = lax.broadcasted_iota(I32, (slots, n), 0)
    off = jnp.where(j < cap, 1, jnp.where(j < 2 * cap, -1, jnp.where(j < 3 * cap, 2, -2)))
    start = jnp.where(j < cap, 0, jnp.where(j < 2 * cap, cap, jnp.where(j < 3 * cap, 2 * cap, 3 * cap)))
    node = rel_row - off * nodes
    chosen = ((node >= 0) & (node < nodes)).astype(F32)
    before = lax.broadcasted_iota(I32, (n, n), 0) < lax.broadcasted_iota(I32, (n, n), 1)
    rank = dot(chosen.astype(BF), before.astype(F32).astype(BF))
    fits = jnp.where(rank == (j - start).astype(F32), chosen, 0.0)
    slot_ref[...] = fits.astype(BF)
    slott_ref[...] = fits.T.astype(BF)
    tags = jnp.sum(fits * (node + 1).astype(F32), axis=1, keepdims=True)
    tags_ref[...] = jnp.broadcast_to(tags, (slots, slots)).T[0:tags_ref.shape[0], :].astype(BF)
    width = rows_ref.shape[1]
    at = lax.broadcasted_iota(I32, (n, width), 0)
    for c in range(2):
        place = (at == rows_ref[c:c + 1, :]).astype(F32)
        place_ref[:, c * width:(c + 1) * width] = place.astype(BF)
        pick_ref[c * width:(c + 1) * width, :] = place.T.astype(BF)


def forward(xc, src, adj_ref, inv_ref, win_ref, wo_ref):
    width = xc.shape[1]
    agg = (dot(adj_ref[...], src) * wide(inv_ref[...], width)).astype(BF)
    pre = dot(xc, win_ref[:, 0:width], NT) + dot(agg, win_ref[:, width:], NT)
    hid = (pre * sigmoid(pre)).astype(BF)
    out = (xc.astype(F32) + dot(hid, wo_ref[...], NT)).astype(BF)
    return agg, pre, hid, out


def send_slots(sub, values, slot_ref, one_ref, two_ref):
    cap = slot_ref.shape[0] // 4
    a = pl.multiple_of(sub * cap, cap)
    one_ref[0:cap, :] = dot(slot_ref[pl.ds(a, cap), :], values).astype(BF)
    two_ref[0:cap, :] = dot(slot_ref[pl.ds(a + 2 * cap, cap), :], values).astype(BF)


def fill_sources(me_ref, xc, rims_ref, src):
    n = xc.shape[0]
    rim = rims_ref.shape[1]
    src[0:n, :] = xc
    for c in range(2):
        rows = slice(n + c * rim, n + (c + 1) * rim)
        there = me_ref[0] >= 1 if c == 0 else me_ref[0] < me_ref[4] - 1

        @pl.when(there)
        def _():
            src[rows, :] = rims_ref[c]

        @pl.when(jnp.logical_not(there))
        def _():
            src[rows, :] = jnp.zeros((rim, xc.shape[1]), BF)


def k_first(me_ref, xc_ref, rims_ref, adj_ref, inv_ref, win_ref, wo_ref,
            slot_ref, tags_ref,
            agg_ref, pre_ref, hid_ref, first_ref, one_ref, two_ref, src):
    xc = xc_ref[...]
    fill_sources(me_ref, xc, rims_ref, src)
    agg, pre, hid, out = forward(xc, src[...], adj_ref, inv_ref, win_ref, wo_ref)
    agg_ref[...] = agg
    pre_ref[...] = pre
    hid_ref[...] = hid
    first_ref[...] = out
    send_slots(me_ref[1], out, slot_ref, one_ref, two_ref)
    cap = slot_ref.shape[0] // 4
    pad = wide(tags_ref[...], one_ref.shape[1])
    one_ref[cap:, :] = pad
    two_ref[cap:, :] = pad


def k_own(hott_ref, v_ref, pre_ref, pool_ref, slope_ref):
    pool_ref[...] = dot(hott_ref[...], v_ref[...])
    slope_ref[...] = slope_of(pre_ref[...])


def k_cot(ct_ref, wo_ref, ctc_ref, hg_ref):
    ctc = ct_ref[...].T
    ctc_ref[...] = ctc
    hg_ref[...] = dot(ctc, wo_ref[...])


def arrived_of(got_ref, cap):
    rows = got_ref.shape[1] // 2
    return jnp.concatenate(
        [got_ref[0, 0:cap], got_ref[1, 0:cap], got_ref[0, rows:rows + cap], got_ref[1, rows:rows + cap]],
        axis=0,
    )


def k_coarse(me_ref, pool_ref, ocount_ref, got_ref, cw_ref,
             hits_ref, icount_ref, coarse_ref, cpre_ref, corr_ref, out1_ref, out2_ref):
    nodes, width = pool_ref.shape
    cap = out1_ref.shape[0]
    rows = got_ref.shape[1] // 2
    slots = 4 * cap
    lane = lax.broadcasted_iota(I32, (1, slots), 1)
    t = [got_ref[c, o + cap:o + cap + 1, 0:slots].astype(F32) for o in (0, rows) for c in range(2)]
    domain, count = me_ref[0], me_ref[4]
    there = (domain >= 1, domain < count - 1, domain >= 2, domain < count - 2)
    t = [jnp.where(ok, v, 0.0) for ok, v in zip(there, t)]
    tags = jnp.where(lane < cap, t[0], jnp.where(lane < 2 * cap, t[1], jnp.where(lane < 3 * cap, t[2], t[3])))
    node = (lax.broadcasted_iota(I32, (nodes, slots), 0) + 1).astype(F32)
    hits = (node == tags).astype(F32)
    count = jnp.maximum(ocount_ref[...] + jnp.sum(hits, axis=1, keepdims=True), 1.0)
    icount = 1.0 / count
    hits_ref[...] = hits
    icount_ref[...] = icount
    hb = hits.astype(BF)
    total = pool_ref[...] + dot(hb, arrived_of(got_ref, cap))
    coarse = (total * wide(icount, width)).astype(BF)
    cpre = dot(coarse, cw_ref[...], NT)
    corr = (cpre * sigmoid(cpre)).astype(BF)
    coarse_ref[...] = coarse
    cpre_ref[...] = cpre
    corr_ref[...] = corr
    ans = dot(hits.T.astype(BF), corr).astype(BF)
    sub = me_ref[1]
    out1_ref[...] = jnp.where(sub == 0, ans[cap:2 * cap], ans[0:cap])
    out2_ref[...] = jnp.where(sub == 0, ans[3 * cap:], ans[2 * cap:3 * cap])


def spread_back(first, hot_ref, slott_ref, corr, got_ref):
    cap = got_ref.shape[1] // 2
    returned = jnp.concatenate(
        [got_ref[1, 0:cap], got_ref[0, 0:cap], got_ref[1, cap:], got_ref[0, cap:]], axis=0
    )
    total = first.astype(F32) + dot(hot_ref[...], corr) + dot(slott_ref[...], returned)
    return total.astype(BF)


def k_lift(me_ref, first_ref, hot_ref, slott_ref, corr_ref, got_ref, pick_ref,
           lift_ref, msg_ref):
    lifted = spread_back(first_ref[...], hot_ref, slott_ref, corr_ref[...], got_ref)
    lift_ref[...] = lifted
    rim = msg_ref.shape[0]
    at = pl.multiple_of(me_ref[1] * rim, rim)
    msg_ref[...] = dot(pick_ref[pl.ds(at, rim), :], lifted).astype(BF)


def rim_grads(sub, pg, win_ref, inv_ref, adjt_ref, scaled_ref, msg_ref):
    n = pg.shape[0]
    width = win_ref.shape[1] // 2
    rim = msg_ref.shape[0]
    scaled = (dot(pg, win_ref[:, width:]) * wide(inv_ref[...], width)).astype(BF)
    scaled_ref[...] = scaled
    at = pl.multiple_of(n + (1 - sub) * rim, rim)
    msg_ref[...] = dot(adjt_ref[pl.ds(at, rim), :], scaled).astype(BF)


def k_second(me_ref, lift_ref, rim_ref, adj_ref, adjt_ref, inv_ref, win_ref, wo_ref, hg_ref,
             agg_ref, hid_ref, new_ref, pg_ref, scaled_ref, msg_ref, src):
    lifted = lift_ref[...]
    fill_sources(me_ref, lifted, rim_ref, src)
    agg, pre, hid, out = forward(lifted, src[...], adj_ref, inv_ref, win_ref, wo_ref)
    agg_ref[...] = agg
    hid_ref[...] = hid
    new_ref[...] = out
    pg = (hg_ref[...] * slope_of(pre)).astype(BF)
    pg_ref[...] = pg
    rim_grads(me_ref[1], pg, win_ref, inv_ref, adjt_ref, scaled_ref, msg_ref)


def k_combine(g_ref, pg_ref, win_ref, scaled_ref, adjt_ref, comb_ref):
    n, width = comb_ref.shape
    comb_ref[...] = (
        g_ref[...].astype(F32)
        + dot(pg_ref[...], win_ref[:, 0:width])
        + dot(adjt_ref[0:n, :], scaled_ref[...])
    )


def k_newt(me_ref, hott_ref, lg_ref, new_ref, pool_ref, out_ref):
    half = out_ref.shape[0]
    at = pl.multiple_of(me_ref[1] * half, half)
    out_ref[...] = new_ref[:, pl.ds(at, half)].T
    pool_ref[...] = dot(hott_ref[...], lg_ref[...])


def k_grads(scale, me_ref, pg_ref, h_ref, agg_ref, g_ref, hid_ref, gin_ref, gout_ref):
    half = gin_ref.shape[0]
    width = h_ref.shape[1]
    at = pl.multiple_of(me_ref[1] * half, half)
    pgt = pg_ref[:, pl.ds(at, half)].T
    gin_ref[:, 0:width] = dot(pgt, h_ref[...]) * scale
    gin_ref[:, width:] = dot(pgt, agg_ref[...]) * scale
    gt = g_ref[:, pl.ds(at, half)].T
    gout_ref[...] = dot(gt, hid_ref[...]) * scale


def pack_grads(scale, me_ref, pg_ref, h_ref, agg_ref, g_ref, hid_ref, keep_ref, send_ref):
    width = h_ref.shape[1]
    half = width // 2
    piece = keep_ref.shape[2]
    at = pl.multiple_of(me_ref[1] * half, half)
    pgt = pg_ref[:, pl.ds(at, half)].T
    lo = dot(pgt, h_ref[...]) * scale
    hi = dot(pgt, agg_ref[...]) * scale
    out = dot(hid_ref[...].T, g_ref[:, pl.ds(at, half)]) * scale

    def pieces(d):
        src, c = (lo, d * piece) if d * piece < width else (hi, d * piece - width)
        return [(0, src[:, c:c + piece])] + small_pieces(out, d, piece, half)

    place_pieces(me_ref, pieces, keep_ref, send_ref)


def small_pieces(values, d, piece, row):
    small = values.shape[0] // 8
    mine = values[d * small:(d + 1) * small]
    return [
        (row + c * small, mine[:, c * piece:(c + 1) * piece]) for c in range(values.shape[1] // piece)
    ]


def place_pieces(me_ref, pieces, keep_ref, send_ref):
    for d in range(8):
        for row, value in pieces(d):
            rows = slice(row, row + value.shape[0])

            @pl.when(me_ref[2] == d % 2)
            def _():
                keep_ref[d // 2, rows, :] = value

            @pl.when(me_ref[2] != d % 2)
            def _():
                send_ref[d // 2, rows, :] = value.astype(BF)


def k_combine_pack(scale, me_ref, pg_ref, h_ref, agg_ref, g_ref, hid_ref, win_ref, scaled_ref, adjt_ref,
                   comb_ref, keep_ref, send_ref):
    k_combine(g_ref, pg_ref, win_ref, scaled_ref, adjt_ref, comb_ref)
    pack_grads(scale, me_ref, pg_ref, h_ref, agg_ref, g_ref, hid_ref, keep_ref, send_ref)


def k_cweight_pack(scale, me_ref, pgrad_ref, coarse_ref, keep_ref, send_ref):
    half = pgrad_ref.shape[1] // 2
    piece = keep_ref.shape[2]
    at = pl.multiple_of(me_ref[1] * half, half)
    values = dot(coarse_ref[...].T, pgrad_ref[:, pl.ds(at, half)]) * scale
    place_pieces(me_ref, lambda d: small_pieces(values, d, piece, 0), keep_ref, send_ref)


def placed(me_ref, place_ref, before, after):
    rim = before.shape[0]
    from_after = dot(place_ref[:, 0:rim], after)
    from_before = dot(place_ref[:, rim:], before)
    return jnp.where(me_ref[0] < me_ref[4] - 1, from_after, 0.0) + jnp.where(me_ref[0] >= 1, from_before, 0.0)


def k_lgrad(me_ref, comb_ref, rim_ref, place_ref, slot_ref, lg_ref, one_ref, two_ref):
    lg = (comb_ref[...] + placed(me_ref, place_ref, rim_ref[0], rim_ref[1])).astype(BF)
    lg_ref[...] = lg
    send_slots(me_ref[1], lg, slot_ref, one_ref, two_ref)


def k_cgrad(me_ref, pool_ref, got_ref, hits_ref, icount_ref, cpre_ref, cw_ref,
            pgrad_ref, spread_ref, out1_ref, out2_ref):
    cap = out1_ref.shape[0]
    hits = hits_ref[...]
    total = pool_ref[...] + dot(hits.astype(BF), arrived_of(got_ref, cap))
    pgrad = (total * slope_of(cpre_ref[...])).astype(BF)
    pgrad_ref[...] = pgrad
    spread = (dot(pgrad, cw_ref[...]) * wide(icount_ref[...], pgrad.shape[1])).astype(BF)
    spread_ref[...] = spread
    ans = dot(hits.T.astype(BF), spread).astype(BF)
    sub = me_ref[1]
    out1_ref[...] = jnp.where(sub == 0, ans[cap:2 * cap], ans[0:cap])
    out2_ref[...] = jnp.where(sub == 0, ans[3 * cap:], ans[2 * cap:3 * cap])


def k_cweight(scale, me_ref, pgrad_ref, coarse_ref, out_ref):
    half = out_ref.shape[0]
    at = pl.multiple_of(me_ref[1] * half, half)
    out_ref[...] = dot(pgrad_ref[:, pl.ds(at, half)].T, coarse_ref[...]) * scale


def k_third(me_ref, lg_ref, hot_ref, slott_ref, spread_ref, got_ref, wo_ref, slope_ref,
            win_ref, inv_ref, adjt_ref, *rest, scale=None):
    fb_ref, pg_ref, scaled_ref, msg_ref = rest[-4:] if scale is None else rest[3:7]
    fb = spread_back(lg_ref[...], hot_ref, slott_ref, spread_ref[...], got_ref)
    fb_ref[...] = fb
    pg = (dot(fb, wo_ref[...]) * slope_ref[...]).astype(BF)
    pg_ref[...] = pg
    if scale is not None:
        xc_ref, agg_ref, hid_ref = rest[:3]
        pack_grads(scale, me_ref, pg_ref, xc_ref, agg_ref, fb_ref, hid_ref, rest[7], rest[8])
    rim_grads(me_ref[1], pg, win_ref, inv_ref, adjt_ref, scaled_ref, msg_ref)


def k_last(me_ref, comb_ref, rim_ref, place_ref, *rest):
    half = comb_ref.shape[1]
    at = pl.multiple_of(me_ref[1] * half, half)
    total = comb_ref[...] + placed(
        me_ref, place_ref, rim_ref[0, :, pl.ds(at, half)], rim_ref[1, :, pl.ds(at, half)])
    if len(rest) == 1:
        rest[0][...] = total.T
    else:
        rest[4][...] = total.T
        k_sum(*rest[:4], *rest[5:])


def k_halfcomb(me_ref, fb_ref, pg_ref, win_ref, scaled_ref, adjt_ref, comb_ref):
    n, half = comb_ref.shape
    at = pl.multiple_of(me_ref[1] * half, half)
    cols = pl.ds(at, half)
    comb_ref[...] = (
        fb_ref[:, cols].astype(F32)
        + dot(pg_ref[...], win_ref[:, cols])
        + dot(adjt_ref[0:n, :], scaled_ref[:, cols])
    )


def k_stage(me_ref, *refs):
    pairs = (len(refs) - 4) // 2
    own_ref, outs = refs[2 * pairs], refs[2 * pairs + 1:]
    z = me_ref[3]
    row = 0
    for i in range(pairs):
        keep_ref, got_ref = refs[2 * i], refs[2 * i + 1]
        rows = slice(row, row + keep_ref.shape[1])
        own_ref[rows, :] = keep_ref[z] + got_ref[z].astype(F32)
        for step in (1, 2, 3):
            other = z ^ step
            outs[step - 1][rows, :] = (keep_ref[other] + got_ref[other].astype(F32)).astype(BF)
        row += keep_ref.shape[1]


def k_stage_comb(me_ref, fb_ref, pg_ref, win_ref, scaled_ref, adjt_ref, *refs):
    k_stage(me_ref, *refs[:-1])
    k_halfcomb(me_ref, fb_ref, pg_ref, win_ref, scaled_ref, adjt_ref, refs[-1])


def unpack_small(total):
    small = total.shape[0] // 2
    return jnp.concatenate([total[0:small], total[small:]], axis=1)


def k_sum(own_ref, a_ref, b_ref, c_ref, ein_ref, eout_ref, gco_ref):
    half = ein_ref.shape[0]
    mid = half + 2 * eout_ref.shape[0]
    total = own_ref[...] + a_ref[...].astype(F32) + b_ref[...].astype(F32) + c_ref[...].astype(F32)
    ein_ref[...] = total[0:half]
    eout_ref[...] = unpack_small(total[half:mid])
    gco_ref[...] = unpack_small(total[mid:])


def k_sum_late(own_ref, a_ref, b_ref, c_ref, ein_ref, eout_ref, gin_ref, gout_ref):
    half = ein_ref.shape[0]
    total = own_ref[...] + a_ref[...].astype(F32) + b_ref[...].astype(F32) + c_ref[...].astype(F32)
    gin_ref[0] = total[0:half]
    gin_ref[1] = ein_ref[...]
    gout_ref[0] = unpack_small(total[half:])
    gout_ref[1] = eout_ref[...]


def local(node_features, inward_weight, outward_weight, coarse_weight, tile_index, tile_mask,
          send_rows, parent, cotangent):
    half, n = node_features.shape
    width = 2 * half
    blocks, k_slots = tile_index.shape
    rim = tile_mask.shape[2]
    src_rows = (blocks + 2) * rim
    domains = lax.axis_size(DOM)
    cross = lax.axis_size("cross")
    curve = lax.axis_size("curve")
    cap = n // 16
    nodes = n // 4
    slots = 4 * cap
    hidden = 2 * inward_weight.shape[1]
    scale = float(n * domains) ** -0.5
    me = jnp.stack(
        [lax.axis_index(a) for a in (DOM, "sub", "cross", "curve")] + [jnp.int32(domains)]).astype(I32)
    rows = send_rows[0]
    packed = cross == 2 and curve == 4 and 2 * width == 1024 and hidden == width

    cell_bf, cell_f32 = sds((n, width), BF), sds((n, width), F32)
    win2, wout2 = swap(inward_weight), swap(outward_weight)
    x_full = gather(node_features)
    xc, rims = call(k_halo, [cell_bf, sds((rim, width), BF)], [me], [rows, x_full], "halo")
    rims = two_way(rims, 1)
    (adj, adjt, inv, hott, hot, slot, slott, pick, place, tags, ocount) = call(
        k_prep,
        [sds((n, src_rows), BF), sds((src_rows, n), BF), sds((n, 128), F32), sds((nodes, n), BF),
         sds((n, nodes), BF), sds((slots, n), BF), sds((n, slots), BF), sds((2 * rim, n), BF),
         sds((n, 2 * rim), BF), sds((16, slots), BF), sds((nodes, 128), F32)],
        [tile_index, me], [tile_mask, rows, parent[None, :]], "prep")
    weight_outs = [sds((hidden, 2 * width), BF), sds((width, hidden), BF)]
    win0, wo0 = call(lambda *r: k_weights(0, *r), weight_outs, [me],
                     [inward_weight, outward_weight, win2, wout2], "weights0")
    rims = gather(rims).reshape(2, rim, width)
    msg = sds((cap + 16, width), BF)
    plain = sds((cap, width), BF)
    hid_bf, hid_f32 = sds((n, hidden), BF), sds((n, hidden), F32)
    agg0, pre0, hid0, first, one, two = call(
        k_first,
        [cell_bf, hid_f32, hid_bf, cell_bf, msg, msg],
        [me], [xc, rims, adj, inv, win0, wo0, slot, tags], "first",
        flops=2 * n * width * (src_rows + 3 * width),
        scratch=[pltpu.VMEM((src_rows, width), BF)])
    one, two, win2, coarse_weight = lax.optimization_barrier((one, two, win2, coarse_weight))
    one, two = two_way(one, 1), two_way(two, 2)
    own, slope0 = call(k_own, [sds((nodes, width), F32), hid_f32], [], [hott, first, pre0], "own")
    cw = gather(coarse_weight)
    win1, wo1 = call(lambda *r: k_weights(1, *r), weight_outs, [me],
                     [inward_weight, outward_weight, win2, wout2], "weights1")
    got = gather(jnp.concatenate([one, two], axis=0)).reshape(2, -1, width)
    node_bf, node_f32 = sds((nodes, width), BF), sds((nodes, width), F32)
    hits, icount, coarse, cpre, corr, one, two = call(
        k_coarse, [sds((nodes, slots), F32), sds((nodes, 128), F32), node_bf, node_f32, node_bf, plain, plain],
        [me], [own, ocount, got, cw], "coarse")
    one, two, cotangent = lax.optimization_barrier((one, two, cotangent))
    one, two = two_way(one, 1), two_way(two, 2)
    ct_full = gather(cotangent)
    ctc, hg1 = call(k_cot, [cell_bf, hid_f32], [], [ct_full, wo1], "cot")
    got = gather(jnp.concatenate([one, two], axis=0)).reshape(2, -1, width)
    lifted, rims = call(
        k_lift, [cell_bf, sds((rim, width), BF)], [me],
        [first, hot, slott, corr, got, pick], "lift")
    rims = gather(two_way(rims, 1)).reshape(2, rim, width)
    agg1, hid1, new, pg1, scaled1, rims = call(
        k_second, [cell_bf, hid_bf, cell_bf, hid_bf, cell_bf, sds((rim, width), BF)],
        [me], [lifted, rims, adj, adjt, inv, win1, wo1, hg1], "second",
        scratch=[pltpu.VMEM((src_rows, width), BF)])
    rims = two_way(rims, 1)
    piece = 2 * width // domains
    small = hidden // domains
    layer_rows = half + 2 * small
    pack = [sds((curve, layer_rows, piece), F32), sds((curve, layer_rows, piece), BF)]
    if packed:
        comb1, keep1, send1 = call(lambda *r: k_combine_pack(scale, *r), [cell_f32] + pack, [me],
                            [pg1, lifted, agg1, ctc, hid1, win1, scaled1, adjt], "combine")
    else:
        comb1, = call(k_combine, [cell_f32], [], [ctc, pg1, win1, scaled1, adjt], "combine")
    rims = gather(rims).reshape(2, rim, width)
    lg, one, two = call(
        k_lgrad, [cell_bf, plain, plain], [me], [comb1, rims, place, slot], "lgrad")
    if packed:
        one, two, send1 = lax.optimization_barrier((one, two, send1))
        got1 = cross_swap(send1)
    one, two = two_way(one, 1), two_way(two, 2)
    own_g, new_t = call(k_newt, [node_f32, sds((half, n), BF)], [me], [hott, lg, new], "own_grad")
    got = gather(jnp.concatenate([one, two], axis=0)).reshape(2, -1, width)
    if packed:
        got, got1 = lax.optimization_barrier((got, got1))
    pgrad, spread, one, two = call(
        k_cgrad, [node_bf, node_bf, plain, plain], [me],
        [own_g, got, hits, icount, cpre, cw], "cgrad")
    one, two = two_way(one, 1), two_way(two, 2)
    got = gather(jnp.concatenate([one, two], axis=0)).reshape(2, -1, width)
    back_outs = [cell_bf, hid_bf, cell_bf, sds((rim, width), BF)]
    back_args = [lg, hot, slott, spread, got, wo0, slope0, win0, inv, adjt]
    if packed:
        keepc, sendc = call(
            lambda *r: k_cweight_pack(scale, *r),
            [sds((curve, 2 * small, piece), F32), sds((curve, 2 * small, piece), BF)], [me],
            [pgrad, coarse], "cweight")
        gotc = cross_swap(sendc)
        fb, pg0, scaled0, rims, keep0, send0 = call(
            lambda *r: k_third(*r, scale=scale), back_outs + pack, [me], back_args + [xc, agg0, hid0], "third")
        got0 = cross_swap(send0)
        rims = two_way(rims, 1)

        def staged(body, extra, extra_outs, pairs, name):
            total = sum(keep.shape[1] for keep in pairs[::2])
            own, *outs = call(
                body, [sds((total, piece), F32)] + [sds((total, piece), BF)] * 3 + extra_outs,
                [me], extra + pairs, name)
            return [own] + [curve_swap(value, step) for step, value in zip((1, 2, 3), outs)], outs[3:]

        early, (comb0,) = staged(
            k_stage_comb, [fb, pg0, win0, scaled0, adjt], [sds((n, half), F32)],
            [keep1, got1, keepc, gotc], "stage1")
        late, _ = staged(k_stage, [], [], [keep0, got0], "stage0")
    else:
        gco, = call(lambda *r: k_cweight(scale, *r), [sds((half, width), F32)], [me], [pgrad, coarse], "cweight")
        fb, pg0, scaled0, rims = call(k_third, back_outs, [me], back_args, "third")
        rims = two_way(rims, 1)
        comb0, = call(k_halfcomb, [sds((n, half), F32)], [me], [fb, pg0, win0, scaled0, adjt], "halfcomb")
    rims = gather(rims).reshape(2, rim, width)
    if packed:
        fgrad, ein, eout, gco = call(
            k_last, [sds((half, n), F32), sds((half, piece), F32), sds((small, half), F32), sds((small, half), F32)],
            [me], [comb0, rims, place] + early, "last")
        gin, gout = call(
            k_sum_late, [sds((2, half, piece), F32), sds((2, small, half), F32)], [], late + [ein, eout], "late")
        gout = gout.swapaxes(1, 2)
        gco = gco.T
    else:
        fgrad, = call(k_last, [sds((half, n), F32)], [me], [comb0, rims, place], "last")
        shapes = [sds((half, 2 * width), F32), sds((half, hidden), F32)]
        gi1, go1 = call(lambda *r: k_grads(scale, *r), shapes, [me], [pg1, lifted, agg1, ctc, hid1], "grads1")
        gi0, go0 = call(lambda *r: k_grads(scale, *r), shapes, [me], [pg0, xc, agg0, fb, hid0], "grads0")
        gin = lax.psum_scatter(jnp.stack([gi0, gi1]), DOM, scatter_dimension=2, tiled=True)
        gout = lax.psum_scatter(jnp.stack([go0, go1]), DOM, scatter_dimension=2, tiled=True)
        gco = lax.psum_scatter(gco, DOM, scatter_dimension=1, tiled=True)
    return new_t, fgrad, gin, gout, gco


def solution(mesh):
    cells = ("groups", "curve", "cross")
    in_specs = (
        P("sub", cells),
        P(None, "sub", None),
        P(None, "sub", None),
        P("sub", None),
        P(cells, None),
        P(cells, None, None, None),
        P(cells, None, None),
        P(cells),
        P("sub", cells),
    )
    out_specs = (
        P("sub", cells),
        P("sub", cells),
        P("groups", "sub", ("curve", "cross")),
        P("groups", "sub", ("curve", "cross")),
        P(("groups", "sub"), ("curve", "cross")),
    )
    return jax.shard_map(local, mesh=mesh, in_specs=in_specs, out_specs=out_specs, check_vma=False)
```

```python
import jax
import jax.numpy as jnp
from jax import lax
from jax.experimental import pallas as pl
from jax.experimental.pallas import tpu as pltpu
from jax.sharding import PartitionSpec as P

BF = jnp.bfloat16
F32 = jnp.float32
I32 = jnp.int32
DOM = ("curve", "cross")
LINE = ("curve", "cross", "sub")
NN = (((1,), (0,)), ((), ()))
NT = (((1,), (1,)), ((), ()))
TN = (((0,), (0,)), ((), ()))


def dot(a, b, dims=NN):
    return lax.dot_general(a, b, dims, preferred_element_type=F32)


def sds(shape, dtype):
    return jax.ShapeDtypeStruct(shape, dtype)


def call(body, outs, scalars, arrays, name, flops=0, scratch=()):
    scalars, arrays = list(scalars), list(arrays)
    moved = sum(a.size * a.dtype.itemsize for a in arrays) + sum(
        o.size * o.dtype.itemsize for o in outs
    )
    return pl.pallas_call(
        body,
        out_shape=tuple(outs),
        in_specs=[pl.BlockSpec(memory_space=pltpu.SMEM)] * len(scalars)
        + [pl.BlockSpec(memory_space=pltpu.VMEM)] * len(arrays),
        out_specs=tuple(pl.BlockSpec(memory_space=pltpu.VMEM) for _ in outs),
        scratch_shapes=list(scratch),
        compiler_params=pltpu.CompilerParams(vmem_limit_bytes=20 * 2**20),
        cost_estimate=pl.CostEstimate(flops=flops, bytes_accessed=moved, transcendentals=0),
        name=name,
    )(*scalars, *arrays)


def two_way(value, steps):
    count = lax.axis_size(DOM)
    pairs = [(2 * p, 2 * (p + steps)) for p in range(count - steps)]
    pairs += [(2 * p + 1, 2 * (p - steps) + 1) for p in range(steps, count)]
    pairs += [(2 * p, 2 * p + 1) for p in range(count - steps, count)]
    pairs += [(2 * p + 1, 2 * p) for p in range(steps)]
    return lax.ppermute(value, LINE, pairs)


def gather(value):
    return lax.all_gather(value, "sub", axis=0, tiled=True)


def swap(value):
    return lax.ppermute(value, "sub", [(0, 1), (1, 0)])


def cross_swap(value):
    return lax.ppermute(value, "cross", [(0, 1), (1, 0)])


def curve_swap(value, step):
    return lax.ppermute(value, "curve", [(z, z ^ step) for z in range(4)])


def sigmoid(v):
    return 1.0 / (1.0 + jnp.exp(-v))


def slope_of(v):
    s = sigmoid(v)
    return s * (1.0 + v * (1.0 - s))


def wide(col, width):
    return jnp.concatenate([col] * (width // col.shape[1]), axis=1)


def k_halo(me_ref, rows_ref, x_ref, xc_ref, msg_ref):
    xc = x_ref[...].T
    xc_ref[...] = xc
    row = jnp.where(me_ref[1] == 0, rows_ref[0:1, :], rows_ref[1:2, :])
    at = lax.broadcasted_iota(I32, (xc.shape[0], row.shape[1]), 0)
    pick = (at == row).astype(F32).T.astype(BF)
    msg_ref[...] = dot(pick, xc).astype(BF)


def k_weights(layer, me_ref, win_ref, wout_ref, win2_ref, wout2_ref, in_ref, out_ref):
    half = win_ref.shape[1]
    own = pl.multiple_of(me_ref[1] * half, half)
    other = pl.multiple_of((1 - me_ref[1]) * half, half)
    in_ref[pl.ds(own, half), :] = win_ref[layer]
    in_ref[pl.ds(other, half), :] = win2_ref[layer]
    out_ref[pl.ds(own, half), :] = wout_ref[layer]
    out_ref[pl.ds(other, half), :] = wout2_ref[layer]


def k_prep(tile_ref, me_ref, mask_ref, rows_ref, par_ref,
           adj_ref, adjt_ref, inv_ref, hott_ref, hot_ref, slot_ref, slott_ref,
           pick_ref, place_ref, tags_ref, ocount_ref):
    blocks, k_slots, length, _ = mask_ref.shape
    n = adj_ref.shape[0]
    nodes = hott_ref.shape[0]
    slots = slot_ref.shape[0]
    cap = slots // 4
    adj_ref[...] = jnp.zeros(adj_ref.shape, BF)
    adjt_ref[...] = jnp.zeros(adjt_ref.shape, BF)
    for b in range(blocks):
        degree = jnp.zeros((length, 1), F32)
        for k in range(k_slots):
            bits = mask_ref[b, k].astype(F32)
            start = pl.multiple_of(tile_ref[b, k] * length, length)
            adj_ref[b * length:(b + 1) * length, pl.ds(start, length)] = bits.astype(BF)
            adjt_ref[pl.ds(start, length), b * length:(b + 1) * length] = bits.T.astype(BF)
            degree = degree + jnp.sum(bits, axis=1, keepdims=True)
        inv_ref[b * length:(b + 1) * length, :] = jnp.broadcast_to(1.0 / degree, (length, 128))
    rel_row = par_ref[...] - me_ref[0] * nodes
    hott = (lax.broadcasted_iota(I32, (nodes, n), 0) == rel_row).astype(F32)
    hott_ref[...] = hott.astype(BF)
    ocount_ref[...] = jnp.broadcast_to(jnp.sum(hott, axis=1, keepdims=True), (nodes, 128))
    hot_ref[...] = hott.T.astype(BF)
    j = lax.broadcasted_iota(I32, (slots, n), 0)
    off = jnp.where(j < cap, 1, jnp.where(j < 2 * cap, -1, jnp.where(j < 3 * cap, 2, -2)))
    start = jnp.where(j < cap, 0, jnp.where(j < 2 * cap, cap, jnp.where(j < 3 * cap, 2 * cap, 3 * cap)))
    node = rel_row - off * nodes
    chosen = ((node >= 0) & (node < nodes)).astype(F32)
    before = lax.broadcasted_iota(I32, (n, n), 0) < lax.broadcasted_iota(I32, (n, n), 1)
    rank = dot(chosen.astype(BF), before.astype(F32).astype(BF))
    fits = jnp.where(rank == (j - start).astype(F32), chosen, 0.0)
    slot_ref[...] = fits.astype(BF)
    slott_ref[...] = fits.T.astype(BF)
    tags = jnp.sum(fits * (node + 1).astype(F32), axis=1, keepdims=True)
    tags_ref[...] = jnp.broadcast_to(tags, (slots, slots)).T[0:tags_ref.shape[0], :].astype(BF)
    width = rows_ref.shape[1]
    at = lax.broadcasted_iota(I32, (n, width), 0)
    for c in range(2):
        place = (at == rows_ref[c:c + 1, :]).astype(F32)
        place_ref[:, c * width:(c + 1) * width] = place.astype(BF)
        pick_ref[c * width:(c + 1) * width, :] = place.T.astype(BF)


def forward(xc, src, adj_ref, inv_ref, win_ref, wo_ref):
    width = xc.shape[1]
    agg = (dot(adj_ref[...], src) * wide(inv_ref[...], width)).astype(BF)
    pre = dot(xc, win_ref[:, 0:width], NT) + dot(agg, win_ref[:, width:], NT)
    hid = (pre * sigmoid(pre)).astype(BF)
    out = (xc.astype(F32) + dot(hid, wo_ref[...], NT)).astype(BF)
    return agg, pre, hid, out


def send_slots(sub, values, slot_ref, one_ref, two_ref):
    cap = slot_ref.shape[0] // 4
    a = pl.multiple_of(sub * cap, cap)
    one_ref[0:cap, :] = dot(slot_ref[pl.ds(a, cap), :], values).astype(BF)
    two_ref[0:cap, :] = dot(slot_ref[pl.ds(a + 2 * cap, cap), :], values).astype(BF)


def fill_sources(me_ref, xc, rims_ref, src):
    n = xc.shape[0]
    rim = rims_ref.shape[1]
    src[0:n, :] = xc
    for c in range(2):
        rows = slice(n + c * rim, n + (c + 1) * rim)
        there = me_ref[0] >= 1 if c == 0 else me_ref[0] < me_ref[4] - 1

        @pl.when(there)
        def _():
            src[rows, :] = rims_ref[c]

        @pl.when(jnp.logical_not(there))
        def _():
            src[rows, :] = jnp.zeros((rim, xc.shape[1]), BF)


def k_first(me_ref, xc_ref, rims_ref, adj_ref, inv_ref, win_ref, wo_ref,
            slot_ref, tags_ref,
            agg_ref, pre_ref, hid_ref, first_ref, one_ref, two_ref, src):
    xc = xc_ref[...]
    fill_sources(me_ref, xc, rims_ref, src)
    agg, pre, hid, out = forward(xc, src[...], adj_ref, inv_ref, win_ref, wo_ref)
    agg_ref[...] = agg
    pre_ref[...] = pre
    hid_ref[...] = hid
    first_ref[...] = out
    send_slots(me_ref[1], out, slot_ref, one_ref, two_ref)
    cap = slot_ref.shape[0] // 4
    pad = wide(tags_ref[...], one_ref.shape[1])
    one_ref[cap:, :] = pad
    two_ref[cap:, :] = pad


def k_own(hott_ref, v_ref, pre_ref, pool_ref, slope_ref):
    pool_ref[...] = dot(hott_ref[...], v_ref[...])
    slope_ref[...] = slope_of(pre_ref[...])


def k_cot(ct_ref, wo_ref, ctc_ref, hg_ref):
    ctc = ct_ref[...].T
    ctc_ref[...] = ctc
    hg_ref[...] = dot(ctc, wo_ref[...])


def arrived_of(got_ref, cap):
    rows = got_ref.shape[1] // 2
    return jnp.concatenate(
        [got_ref[0, 0:cap], got_ref[1, 0:cap], got_ref[0, rows:rows + cap], got_ref[1, rows:rows + cap]],
        axis=0,
    )


def k_coarse(me_ref, pool_ref, ocount_ref, got_ref, cw_ref,
             hits_ref, icount_ref, coarse_ref, cpre_ref, corr_ref, out1_ref, out2_ref):
    nodes, width = pool_ref.shape
    cap = out1_ref.shape[0]
    rows = got_ref.shape[1] // 2
    slots = 4 * cap
    lane = lax.broadcasted_iota(I32, (1, slots), 1)
    t = [got_ref[c, o + cap:o + cap + 1, 0:slots].astype(F32) for o in (0, rows) for c in range(2)]
    domain, count = me_ref[0], me_ref[4]
    there = (domain >= 1, domain < count - 1, domain >= 2, domain < count - 2)
    t = [jnp.where(ok, v, 0.0) for ok, v in zip(there, t)]
    tags = jnp.where(lane < cap, t[0], jnp.where(lane < 2 * cap, t[1], jnp.where(lane < 3 * cap, t[2], t[3])))
    node = (lax.broadcasted_iota(I32, (nodes, slots), 0) + 1).astype(F32)
    hits = (node == tags).astype(F32)
    count = jnp.maximum(ocount_ref[...] + jnp.sum(hits, axis=1, keepdims=True), 1.0)
    icount = 1.0 / count
    hits_ref[...] = hits
    icount_ref[...] = icount
    hb = hits.astype(BF)
    total = pool_ref[...] + dot(hb, arrived_of(got_ref, cap))
    coarse = (total * wide(icount, width)).astype(BF)
    cpre = dot(coarse, cw_ref[...], NT)
    corr = (cpre * sigmoid(cpre)).astype(BF)
    coarse_ref[...] = coarse
    cpre_ref[...] = cpre
    corr_ref[...] = corr
    ans = dot(hits.T.astype(BF), corr).astype(BF)
    sub = me_ref[1]
    out1_ref[...] = jnp.where(sub == 0, ans[cap:2 * cap], ans[0:cap])
    out2_ref[...] = jnp.where(sub == 0, ans[3 * cap:], ans[2 * cap:3 * cap])


def spread_back(first, hot_ref, slott_ref, corr, got_ref):
    cap = got_ref.shape[1] // 2
    returned = jnp.concatenate(
        [got_ref[1, 0:cap], got_ref[0, 0:cap], got_ref[1, cap:], got_ref[0, cap:]], axis=0
    )
    total = first.astype(F32) + dot(hot_ref[...], corr) + dot(slott_ref[...], returned)
    return total.astype(BF)


def k_lift(me_ref, first_ref, hot_ref, slott_ref, corr_ref, got_ref, pick_ref,
           lift_ref, msg_ref):
    lifted = spread_back(first_ref[...], hot_ref, slott_ref, corr_ref[...], got_ref)
    lift_ref[...] = lifted
    rim = msg_ref.shape[0]
    at = pl.multiple_of(me_ref[1] * rim, rim)
    msg_ref[...] = dot(pick_ref[pl.ds(at, rim), :], lifted).astype(BF)


def rim_grads(sub, pg, win_ref, inv_ref, adjt_ref, scaled_ref, msg_ref):
    n = pg.shape[0]
    width = win_ref.shape[1] // 2
    rim = msg_ref.shape[0]
    scaled = (dot(pg, win_ref[:, width:]) * wide(inv_ref[...], width)).astype(BF)
    scaled_ref[...] = scaled
    at = pl.multiple_of(n + (1 - sub) * rim, rim)
    msg_ref[...] = dot(adjt_ref[pl.ds(at, rim), :], scaled).astype(BF)


def k_second(me_ref, lift_ref, rim_ref, adj_ref, adjt_ref, inv_ref, win_ref, wo_ref, hg_ref,
             agg_ref, hid_ref, new_ref, pg_ref, scaled_ref, msg_ref, src):
    lifted = lift_ref[...]
    fill_sources(me_ref, lifted, rim_ref, src)
    agg, pre, hid, out = forward(lifted, src[...], adj_ref, inv_ref, win_ref, wo_ref)
    agg_ref[...] = agg
    hid_ref[...] = hid
    new_ref[...] = out
    pg = (hg_ref[...] * slope_of(pre)).astype(BF)
    pg_ref[...] = pg
    rim_grads(me_ref[1], pg, win_ref, inv_ref, adjt_ref, scaled_ref, msg_ref)


def k_combine(g_ref, pg_ref, win_ref, scaled_ref, adjt_ref, comb_ref):
    n, width = comb_ref.shape
    comb_ref[...] = (
        g_ref[...].astype(F32)
        + dot(pg_ref[...], win_ref[:, 0:width])
        + dot(adjt_ref[0:n, :], scaled_ref[...])
    )


def k_newt(me_ref, hott_ref, lg_ref, new_ref, pool_ref, out_ref):
    half = out_ref.shape[0]
    at = pl.multiple_of(me_ref[1] * half, half)
    out_ref[...] = new_ref[:, pl.ds(at, half)].T
    pool_ref[...] = dot(hott_ref[...], lg_ref[...])


def k_grads(scale, me_ref, pg_ref, h_ref, agg_ref, g_ref, hid_ref, gin_ref, gout_ref):
    half = gin_ref.shape[0]
    width = h_ref.shape[1]
    at = pl.multiple_of(me_ref[1] * half, half)
    pgt = pg_ref[:, pl.ds(at, half)].T
    gin_ref[:, 0:width] = dot(pgt, h_ref[...]) * scale
    gin_ref[:, width:] = dot(pgt, agg_ref[...]) * scale
    gt = g_ref[:, pl.ds(at, half)].T
    gout_ref[...] = dot(gt, hid_ref[...]) * scale


def pack_grads(scale, me_ref, pg_ref, h_ref, agg_ref, g_ref, hid_ref, keep_ref, send_ref):
    width = h_ref.shape[1]
    half = width // 2
    piece = keep_ref.shape[2]
    at = pl.multiple_of(me_ref[1] * half, half)
    pgt = pg_ref[:, pl.ds(at, half)].T
    lo = dot(pgt, h_ref[...]) * scale
    hi = dot(pgt, agg_ref[...]) * scale
    out = dot(hid_ref[...].T, g_ref[:, pl.ds(at, half)]) * scale

    def pieces(d):
        src, c = (lo, d * piece) if d * piece < width else (hi, d * piece - width)
        return [(0, src[:, c:c + piece])] + small_pieces(out, d, piece, half)

    place_pieces(me_ref, pieces, keep_ref, send_ref)


def small_pieces(values, d, piece, row):
    small = values.shape[0] // 8
    mine = values[d * small:(d + 1) * small]
    return [
        (row + c * small, mine[:, c * piece:(c + 1) * piece]) for c in range(values.shape[1] // piece)
    ]


def place_pieces(me_ref, pieces, keep_ref, send_ref):
    for d in range(8):
        for row, value in pieces(d):
            rows = slice(row, row + value.shape[0])

            @pl.when(me_ref[2] == d % 2)
            def _():
                keep_ref[d // 2, rows, :] = value

            @pl.when(me_ref[2] != d % 2)
            def _():
                send_ref[d // 2, rows, :] = value.astype(BF)


def k_combine_pack(scale, me_ref, pg_ref, h_ref, agg_ref, g_ref, hid_ref, win_ref, scaled_ref, adjt_ref,
                   comb_ref, keep_ref, send_ref):
    pack_grads(scale, me_ref, pg_ref, h_ref, agg_ref, g_ref, hid_ref, keep_ref, send_ref)
    k_combine(g_ref, pg_ref, win_ref, scaled_ref, adjt_ref, comb_ref)


def k_cweight_pack(scale, me_ref, pgrad_ref, coarse_ref, keep_ref, send_ref):
    half = pgrad_ref.shape[1] // 2
    piece = keep_ref.shape[2]
    at = pl.multiple_of(me_ref[1] * half, half)
    values = dot(coarse_ref[...].T, pgrad_ref[:, pl.ds(at, half)]) * scale
    place_pieces(me_ref, lambda d: small_pieces(values, d, piece, 0), keep_ref, send_ref)


def placed(me_ref, place_ref, before, after):
    rim = before.shape[0]
    from_after = dot(place_ref[:, 0:rim], after)
    from_before = dot(place_ref[:, rim:], before)
    return jnp.where(me_ref[0] < me_ref[4] - 1, from_after, 0.0) + jnp.where(me_ref[0] >= 1, from_before, 0.0)


def k_lgrad(me_ref, comb_ref, rim_ref, place_ref, slot_ref, lg_ref, one_ref, two_ref):
    lg = (comb_ref[...] + placed(me_ref, place_ref, rim_ref[0], rim_ref[1])).astype(BF)
    lg_ref[...] = lg
    send_slots(me_ref[1], lg, slot_ref, one_ref, two_ref)


def k_cgrad(me_ref, pool_ref, got_ref, hits_ref, icount_ref, cpre_ref, cw_ref,
            pgrad_ref, spread_ref, out1_ref, out2_ref):
    cap = out1_ref.shape[0]
    hits = hits_ref[...]
    total = pool_ref[...] + dot(hits.astype(BF), arrived_of(got_ref, cap))
    pgrad = (total * slope_of(cpre_ref[...])).astype(BF)
    pgrad_ref[...] = pgrad
    spread = (dot(pgrad, cw_ref[...]) * wide(icount_ref[...], pgrad.shape[1])).astype(BF)
    spread_ref[...] = spread
    ans = dot(hits.T.astype(BF), spread).astype(BF)
    sub = me_ref[1]
    out1_ref[...] = jnp.where(sub == 0, ans[cap:2 * cap], ans[0:cap])
    out2_ref[...] = jnp.where(sub == 0, ans[3 * cap:], ans[2 * cap:3 * cap])


def k_cweight(scale, me_ref, pgrad_ref, coarse_ref, out_ref):
    half = out_ref.shape[0]
    at = pl.multiple_of(me_ref[1] * half, half)
    out_ref[...] = dot(pgrad_ref[:, pl.ds(at, half)].T, coarse_ref[...]) * scale


def k_third(me_ref, lg_ref, hot_ref, slott_ref, spread_ref, got_ref, wo_ref, slope_ref,
            win_ref, inv_ref, adjt_ref, *rest, scale=None):
    fb_ref, pg_ref, scaled_ref, msg_ref = rest[-4:] if scale is None else rest[3:7]
    fb = spread_back(lg_ref[...], hot_ref, slott_ref, spread_ref[...], got_ref)
    fb_ref[...] = fb
    pg = (dot(fb, wo_ref[...]) * slope_ref[...]).astype(BF)
    pg_ref[...] = pg
    if scale is not None:
        xc_ref, agg_ref, hid_ref = rest[:3]
        pack_grads(scale, me_ref, pg_ref, xc_ref, agg_ref, fb_ref, hid_ref, rest[7], rest[8])
    rim_grads(me_ref[1], pg, win_ref, inv_ref, adjt_ref, scaled_ref, msg_ref)


def k_last(me_ref, comb_ref, rim_ref, place_ref, *rest):
    half = comb_ref.shape[1]
    at = pl.multiple_of(me_ref[1] * half, half)
    total = comb_ref[...] + placed(
        me_ref, place_ref, rim_ref[0, :, pl.ds(at, half)], rim_ref[1, :, pl.ds(at, half)])
    if len(rest) == 1:
        rest[0][...] = total.T
    else:
        rest[4][...] = total.T
        k_sum(*rest[:4], *rest[5:])


def k_halfcomb(me_ref, fb_ref, pg_ref, win_ref, scaled_ref, adjt_ref, comb_ref):
    n, half = comb_ref.shape
    at = pl.multiple_of(me_ref[1] * half, half)
    cols = pl.ds(at, half)
    comb_ref[...] = (
        fb_ref[:, cols].astype(F32)
        + dot(pg_ref[...], win_ref[:, cols])
        + dot(adjt_ref[0:n, :], scaled_ref[:, cols])
    )


def k_stage(me_ref, *refs):
    pairs = (len(refs) - 4) // 2
    own_ref, outs = refs[2 * pairs], refs[2 * pairs + 1:]
    z = me_ref[3]
    row = 0
    for i in range(pairs):
        keep_ref, got_ref = refs[2 * i], refs[2 * i + 1]
        rows = slice(row, row + keep_ref.shape[1])
        own_ref[rows, :] = keep_ref[z] + got_ref[z].astype(F32)
        for step in (1, 2, 3):
            other = z ^ step
            outs[step - 1][rows, :] = (keep_ref[other] + got_ref[other].astype(F32)).astype(BF)
        row += keep_ref.shape[1]


def k_stage_comb(me_ref, fb_ref, pg_ref, win_ref, scaled_ref, adjt_ref, *refs):
    k_stage(me_ref, *refs[:-1])
    k_halfcomb(me_ref, fb_ref, pg_ref, win_ref, scaled_ref, adjt_ref, refs[-1])


def unpack_small(total):
    small = total.shape[0] // 2
    return jnp.concatenate([total[0:small], total[small:]], axis=1)


def k_sum(own_ref, a_ref, b_ref, c_ref, ein_ref, eout_ref, gco_ref):
    half = ein_ref.shape[0]
    mid = half + 2 * eout_ref.shape[0]
    total = own_ref[...] + a_ref[...].astype(F32) + b_ref[...].astype(F32) + c_ref[...].astype(F32)
    ein_ref[...] = total[0:half]
    eout_ref[...] = unpack_small(total[half:mid])
    gco_ref[...] = unpack_small(total[mid:])


def k_sum_late(own_ref, a_ref, b_ref, c_ref, ein_ref, eout_ref, gin_ref, gout_ref):
    half = ein_ref.shape[0]
    total = own_ref[...] + a_ref[...].astype(F32) + b_ref[...].astype(F32) + c_ref[...].astype(F32)
    gin_ref[0] = total[0:half]
    gin_ref[1] = ein_ref[...]
    gout_ref[0] = unpack_small(total[half:])
    gout_ref[1] = eout_ref[...]


def local(node_features, inward_weight, outward_weight, coarse_weight, tile_index, tile_mask,
          send_rows, parent, cotangent):
    half, n = node_features.shape
    width = 2 * half
    blocks, k_slots = tile_index.shape
    rim = tile_mask.shape[2]
    src_rows = (blocks + 2) * rim
    domains = lax.axis_size(DOM)
    cross = lax.axis_size("cross")
    curve = lax.axis_size("curve")
    cap = n // 16
    nodes = n // 4
    slots = 4 * cap
    hidden = 2 * inward_weight.shape[1]
    scale = float(n * domains) ** -0.5
    me = jnp.stack(
        [lax.axis_index(a) for a in (DOM, "sub", "cross", "curve")] + [jnp.int32(domains)]).astype(I32)
    rows = send_rows[0]
    packed = cross == 2 and curve == 4 and 2 * width == 1024 and hidden == width

    cell_bf, cell_f32 = sds((n, width), BF), sds((n, width), F32)
    win2, wout2 = swap(inward_weight), swap(outward_weight)
    x_full = gather(node_features)
    xc, rims = call(k_halo, [cell_bf, sds((rim, width), BF)], [me], [rows, x_full], "halo")
    rims = two_way(rims, 1)
    (adj, adjt, inv, hott, hot, slot, slott, pick, place, tags, ocount) = call(
        k_prep,
        [sds((n, src_rows), BF), sds((src_rows, n), BF), sds((n, 128), F32), sds((nodes, n), BF),
         sds((n, nodes), BF), sds((slots, n), BF), sds((n, slots), BF), sds((2 * rim, n), BF),
         sds((n, 2 * rim), BF), sds((16, slots), BF), sds((nodes, 128), F32)],
        [tile_index, me], [tile_mask, rows, parent[None, :]], "prep")
    weight_outs = [sds((hidden, 2 * width), BF), sds((width, hidden), BF)]
    win0, wo0 = call(lambda *r: k_weights(0, *r), weight_outs, [me],
                     [inward_weight, outward_weight, win2, wout2], "weights0")
    rims = gather(rims).reshape(2, rim, width)
    msg = sds((cap + 16, width), BF)
    plain = sds((cap, width), BF)
    hid_bf, hid_f32 = sds((n, hidden), BF), sds((n, hidden), F32)
    agg0, pre0, hid0, first, one, two = call(
        k_first,
        [cell_bf, hid_f32, hid_bf, cell_bf, msg, msg],
        [me], [xc, rims, adj, inv, win0, wo0, slot, tags], "first",
        flops=2 * n * width * (src_rows + 3 * width),
        scratch=[pltpu.VMEM((src_rows, width), BF)])
    one, two, win2, coarse_weight = lax.optimization_barrier((one, two, win2, coarse_weight))
    one, two = two_way(one, 1), two_way(two, 2)
    own, slope0 = call(k_own, [sds((nodes, width), F32), hid_f32], [], [hott, first, pre0], "own")
    cw = gather(coarse_weight)
    win1, wo1 = call(lambda *r: k_weights(1, *r), weight_outs, [me],
                     [inward_weight, outward_weight, win2, wout2], "weights1")
    got = gather(jnp.concatenate([one, two], axis=0)).reshape(2, -1, width)
    node_bf, node_f32 = sds((nodes, width), BF), sds((nodes, width), F32)
    hits, icount, coarse, cpre, corr, one, two = call(
        k_coarse, [sds((nodes, slots), F32), sds((nodes, 128), F32), node_bf, node_f32, node_bf, plain, plain],
        [me], [own, ocount, got, cw], "coarse")
    one, two, cotangent = lax.optimization_barrier((one, two, cotangent))
    one, two = two_way(one, 1), two_way(two, 2)
    ct_full = gather(cotangent)
    ctc, hg1 = call(k_cot, [cell_bf, hid_f32], [], [ct_full, wo1], "cot")
    got = gather(jnp.concatenate([one, two], axis=0)).reshape(2, -1, width)
    lifted, rims = call(
        k_lift, [cell_bf, sds((rim, width), BF)], [me],
        [first, hot, slott, corr, got, pick], "lift")
    rims = gather(two_way(rims, 1)).reshape(2, rim, width)
    agg1, hid1, new, pg1, scaled1, rims = call(
        k_second, [cell_bf, hid_bf, cell_bf, hid_bf, cell_bf, sds((rim, width), BF)],
        [me], [lifted, rims, adj, adjt, inv, win1, wo1, hg1], "second",
        scratch=[pltpu.VMEM((src_rows, width), BF)])
    rims = two_way(rims, 1)
    piece = 2 * width // domains
    small = hidden // domains
    layer_rows = half + 2 * small
    pack = [sds((curve, layer_rows, piece), F32), sds((curve, layer_rows, piece), BF)]
    if packed:
        comb1, keep1, send1 = call(
            lambda *r: k_combine_pack(scale, *r), [cell_f32] + pack, [me],
            [pg1, lifted, agg1, ctc, hid1, win1, scaled1, adjt], "combine")
        got1 = cross_swap(send1)
    else:
        comb1, = call(k_combine, [cell_f32], [], [ctc, pg1, win1, scaled1, adjt], "combine")
    rims = gather(rims).reshape(2, rim, width)
    lg, one, two = call(
        k_lgrad, [cell_bf, plain, plain], [me], [comb1, rims, place, slot], "lgrad")
    one, two = two_way(one, 1), two_way(two, 2)
    own_g, new_t = call(k_newt, [node_f32, sds((half, n), BF)], [me], [hott, lg, new], "own_grad")
    got = gather(jnp.concatenate([one, two], axis=0)).reshape(2, -1, width)
    pgrad, spread, one, two = call(
        k_cgrad, [node_bf, node_bf, plain, plain], [me],
        [own_g, got, hits, icount, cpre, cw], "cgrad")
    one, two = two_way(one, 1), two_way(two, 2)
    got = gather(jnp.concatenate([one, two], axis=0)).reshape(2, -1, width)
    back_outs = [cell_bf, hid_bf, cell_bf, sds((rim, width), BF)]
    back_args = [lg, hot, slott, spread, got, wo0, slope0, win0, inv, adjt]
    if packed:
        keepc, sendc = call(
            lambda *r: k_cweight_pack(scale, *r),
            [sds((curve, 2 * small, piece), F32), sds((curve, 2 * small, piece), BF)], [me],
            [pgrad, coarse], "cweight")
        gotc = cross_swap(sendc)
        got, got1 = lax.optimization_barrier((got, got1))
        back_args[4] = got
        fb, pg0, scaled0, rims, keep0, send0 = call(
            lambda *r: k_third(*r, scale=scale), back_outs + pack, [me], back_args + [xc, agg0, hid0], "third")
        send0, gotc = lax.optimization_barrier((send0, gotc))
        got0 = cross_swap(send0)
        rims = two_way(rims, 1)

        def staged(body, extra, extra_outs, pairs, name):
            total = sum(keep.shape[1] for keep in pairs[::2])
            own, *outs = call(
                body, [sds((total, piece), F32)] + [sds((total, piece), BF)] * 3 + extra_outs,
                [me], extra + pairs, name)
            return [own] + [curve_swap(value, step) for step, value in zip((1, 2, 3), outs)], outs[3:]

        early, (comb0,) = staged(
            k_stage_comb, [fb, pg0, win0, scaled0, adjt], [sds((n, half), F32)],
            [keep1, got1, keepc, gotc], "stage1")
        late, _ = staged(k_stage, [], [], [keep0, got0], "stage0")
    else:
        gco, = call(lambda *r: k_cweight(scale, *r), [sds((half, width), F32)], [me], [pgrad, coarse], "cweight")
        fb, pg0, scaled0, rims = call(k_third, back_outs, [me], back_args, "third")
        rims = two_way(rims, 1)
        comb0, = call(k_halfcomb, [sds((n, half), F32)], [me], [fb, pg0, win0, scaled0, adjt], "halfcomb")
    rims = gather(rims).reshape(2, rim, width)
    if packed:
        fgrad, ein, eout, gco = call(
            k_last, [sds((half, n), F32), sds((half, piece), F32), sds((small, half), F32), sds((small, half), F32)],
            [me], [comb0, rims, place] + early, "last")
        gin, gout = call(
            k_sum_late, [sds((2, half, piece), F32), sds((2, small, half), F32)], [], late + [ein, eout], "late")
        gout = gout.swapaxes(1, 2)
        gco = gco.T
    else:
        fgrad, = call(k_last, [sds((half, n), F32)], [me], [comb0, rims, place], "last")
        shapes = [sds((half, 2 * width), F32), sds((half, hidden), F32)]
        gi1, go1 = call(lambda *r: k_grads(scale, *r), shapes, [me], [pg1, lifted, agg1, ctc, hid1], "grads1")
        gi0, go0 = call(lambda *r: k_grads(scale, *r), shapes, [me], [pg0, xc, agg0, fb, hid0], "grads0")
        gin = lax.psum_scatter(jnp.stack([gi0, gi1]), DOM, scatter_dimension=2, tiled=True)
        gout = lax.psum_scatter(jnp.stack([go0, go1]), DOM, scatter_dimension=2, tiled=True)
        gco = lax.psum_scatter(gco, DOM, scatter_dimension=1, tiled=True)
    return new_t, fgrad, gin, gout, gco


def solution(mesh):
    cells = ("groups", "curve", "cross")
    in_specs = (
        P("sub", cells),
        P(None, "sub", None),
        P(None, "sub", None),
        P("sub", None),
        P(cells, None),
        P(cells, None, None, None),
        P(cells, None, None),
        P(cells),
        P("sub", cells),
    )
    out_specs = (
        P("sub", cells),
        P("sub", cells),
        P("groups", "sub", ("curve", "cross")),
        P("groups", "sub", ("curve", "cross")),
        P(("groups", "sub"), ("curve", "cross")),
    )
    return jax.shard_map(local, mesh=mesh, in_specs=in_specs, out_specs=out_specs, check_vma=False)
```

```python
import jax
import jax.numpy as jnp
from jax import lax
from jax.experimental import pallas as pl
from jax.experimental.pallas import tpu as pltpu
from jax.sharding import PartitionSpec as P

BF = jnp.bfloat16
F32 = jnp.float32
I32 = jnp.int32
DOM = ("curve", "cross")
LINE = ("curve", "cross", "sub")
NN = (((1,), (0,)), ((), ()))
NT = (((1,), (1,)), ((), ()))
TN = (((0,), (0,)), ((), ()))


def dot(a, b, dims=NN):
    return lax.dot_general(a, b, dims, preferred_element_type=F32)


def sds(shape, dtype):
    return jax.ShapeDtypeStruct(shape, dtype)


def call(body, outs, scalars, arrays, name, flops=0, scratch=()):
    scalars, arrays = list(scalars), list(arrays)
    moved = sum(a.size * a.dtype.itemsize for a in arrays) + sum(
        o.size * o.dtype.itemsize for o in outs
    )
    return pl.pallas_call(
        body,
        out_shape=tuple(outs),
        in_specs=[pl.BlockSpec(memory_space=pltpu.SMEM)] * len(scalars)
        + [pl.BlockSpec(memory_space=pltpu.VMEM)] * len(arrays),
        out_specs=tuple(pl.BlockSpec(memory_space=pltpu.VMEM) for _ in outs),
        scratch_shapes=list(scratch),
        compiler_params=pltpu.CompilerParams(vmem_limit_bytes=20 * 2**20),
        cost_estimate=pl.CostEstimate(flops=flops, bytes_accessed=moved, transcendentals=0),
        name=name,
    )(*scalars, *arrays)


def two_way(value, steps):
    count = lax.axis_size(DOM)
    pairs = [(2 * p, 2 * (p + steps)) for p in range(count - steps)]
    pairs += [(2 * p + 1, 2 * (p - steps) + 1) for p in range(steps, count)]
    pairs += [(2 * p, 2 * p + 1) for p in range(count - steps, count)]
    pairs += [(2 * p + 1, 2 * p) for p in range(steps)]
    return lax.ppermute(value, LINE, pairs)


def swap(value):
    return lax.ppermute(value, "sub", [(0, 1), (1, 0)])


def gather(value):
    return lax.all_gather(value, "sub", axis=0, tiled=False)


def shared(*values):
    return [v for value in values for v in (value, swap(value))]


def directed(sub, own_ref, other_ref, rows=slice(None)):
    own, other = own_ref[rows, :], other_ref[rows, :]
    return jnp.where(sub == 0, own, other), jnp.where(sub == 0, other, own)


def cross_swap(value):
    return lax.ppermute(value, "cross", [(0, 1), (1, 0)])


def curve_swap(value, step):
    return lax.ppermute(value, "curve", [(z, z ^ step) for z in range(4)])


def sigmoid(v):
    return 1.0 / (1.0 + jnp.exp(-v))


def slope_of(v):
    s = sigmoid(v)
    return s * (1.0 + v * (1.0 - s))


def wide(col, width):
    return jnp.concatenate([col] * (width // col.shape[1]), axis=1)


def join_halves(sub, own_ref, other_ref, out_ref):
    half = own_ref.shape[0]
    out_ref[:, pl.ds(pl.multiple_of(sub * half, half), half)] = own_ref[...].T
    out_ref[:, pl.ds(pl.multiple_of((1 - sub) * half, half), half)] = other_ref[...].T


def k_halo(me_ref, rows_ref, x_ref, xc_ref, msg_ref):
    xc = x_ref[...].T
    xc_ref[...] = xc
    row = jnp.where(me_ref[1] == 0, rows_ref[0:1, :], rows_ref[1:2, :])
    at = lax.broadcasted_iota(I32, (xc.shape[0], row.shape[1]), 0)
    pick = (at == row).astype(F32).T.astype(BF)
    msg_ref[...] = dot(pick, xc).astype(BF)


def k_weights(layer, me_ref, win_ref, wout_ref, win2_ref, wout2_ref, in_ref, out_ref):
    half = win_ref.shape[1]
    own = pl.multiple_of(me_ref[1] * half, half)
    other = pl.multiple_of((1 - me_ref[1]) * half, half)
    in_ref[pl.ds(own, half), :] = win_ref[layer]
    in_ref[pl.ds(other, half), :] = win2_ref[layer]
    out_ref[pl.ds(own, half), :] = wout_ref[layer]
    out_ref[pl.ds(other, half), :] = wout2_ref[layer]


def k_prep(tile_ref, me_ref, mask_ref, rows_ref, par_ref,
           adj_ref, adjt_ref, inv_ref, hott_ref, hot_ref, slot_ref, slott_ref,
           pick_ref, place_ref, tags_ref, ocount_ref):
    blocks, k_slots, length, _ = mask_ref.shape
    n = adj_ref.shape[0]
    nodes = hott_ref.shape[0]
    slots = slot_ref.shape[0]
    cap = slots // 4
    adj_ref[...] = jnp.zeros(adj_ref.shape, BF)
    adjt_ref[...] = jnp.zeros(adjt_ref.shape, BF)
    for b in range(blocks):
        degree = jnp.zeros((length, 1), F32)
        for k in range(k_slots):
            bits = mask_ref[b, k].astype(F32)
            start = pl.multiple_of(tile_ref[b, k] * length, length)
            adj_ref[b * length:(b + 1) * length, pl.ds(start, length)] = bits.astype(BF)
            adjt_ref[pl.ds(start, length), b * length:(b + 1) * length] = bits.T.astype(BF)
            degree = degree + jnp.sum(bits, axis=1, keepdims=True)
        inv_ref[b * length:(b + 1) * length, :] = jnp.broadcast_to(1.0 / degree, (length, 128))
    rel_row = par_ref[...] - me_ref[0] * nodes
    hott = (lax.broadcasted_iota(I32, (nodes, n), 0) == rel_row).astype(F32)
    hott_ref[...] = hott.astype(BF)
    ocount_ref[...] = jnp.broadcast_to(jnp.sum(hott, axis=1, keepdims=True), (nodes, 128))
    hot_ref[...] = hott.T.astype(BF)
    j = lax.broadcasted_iota(I32, (slots, n), 0)
    off = jnp.where(j < cap, 1, jnp.where(j < 2 * cap, -1, jnp.where(j < 3 * cap, 2, -2)))
    start = jnp.where(j < cap, 0, jnp.where(j < 2 * cap, cap, jnp.where(j < 3 * cap, 2 * cap, 3 * cap)))
    node = rel_row - off * nodes
    chosen = ((node >= 0) & (node < nodes)).astype(F32)
    before = lax.broadcasted_iota(I32, (n, n), 0) < lax.broadcasted_iota(I32, (n, n), 1)
    rank = dot(chosen.astype(BF), before.astype(F32).astype(BF))
    fits = jnp.where(rank == (j - start).astype(F32), chosen, 0.0)
    slot_ref[...] = fits.astype(BF)
    slott_ref[...] = fits.T.astype(BF)
    tags = jnp.sum(fits * (node + 1).astype(F32), axis=1, keepdims=True)
    tags_ref[...] = jnp.broadcast_to(tags, (slots, slots)).T[0:tags_ref.shape[0], :].astype(BF)
    width = rows_ref.shape[1]
    at = lax.broadcasted_iota(I32, (n, width), 0)
    for c in range(2):
        place = (at == rows_ref[c:c + 1, :]).astype(F32)
        place_ref[:, c * width:(c + 1) * width] = place.astype(BF)
        pick_ref[c * width:(c + 1) * width, :] = place.T.astype(BF)


def forward(xc, src, adj_ref, inv_ref, win_ref, wo_ref):
    width = xc.shape[1]
    agg = (dot(adj_ref[...], src) * wide(inv_ref[...], width)).astype(BF)
    pre = dot(xc, win_ref[:, 0:width], NT) + dot(agg, win_ref[:, width:], NT)
    hid = (pre * sigmoid(pre)).astype(BF)
    out = (xc.astype(F32) + dot(hid, wo_ref[...], NT)).astype(BF)
    return agg, pre, hid, out


def send_slots(sub, values, slot_ref, one_ref, two_ref):
    cap = slot_ref.shape[0] // 4
    a = pl.multiple_of(sub * cap, cap)
    one_ref[0:cap, :] = dot(slot_ref[pl.ds(a, cap), :], values).astype(BF)
    two_ref[0:cap, :] = dot(slot_ref[pl.ds(a + 2 * cap, cap), :], values).astype(BF)


def fill_sources(me_ref, xc, rims, src):
    n = xc.shape[0]
    rim = rims[0].shape[0]
    src[0:n, :] = xc
    for c in range(2):
        rows = slice(n + c * rim, n + (c + 1) * rim)
        there = me_ref[0] >= 1 if c == 0 else me_ref[0] < me_ref[4] - 1

        @pl.when(there)
        def _():
            src[rows, :] = rims[c]

        @pl.when(jnp.logical_not(there))
        def _():
            src[rows, :] = jnp.zeros((rim, xc.shape[1]), BF)


def k_first(me_ref, xc_ref, rims_ref, adj_ref, inv_ref, win_ref, wo_ref,
            slot_ref, tags_ref,
            agg_ref, pre_ref, hid_ref, first_ref, one_ref, two_ref, src):
    xc = xc_ref[...]
    fill_sources(me_ref, xc, (rims_ref[0], rims_ref[1]), src)
    agg, pre, hid, out = forward(xc, src[...], adj_ref, inv_ref, win_ref, wo_ref)
    agg_ref[...] = agg
    pre_ref[...] = pre
    hid_ref[...] = hid
    first_ref[...] = out
    send_slots(me_ref[1], out, slot_ref, one_ref, two_ref)
    cap = slot_ref.shape[0] // 4
    pad = wide(tags_ref[...], one_ref.shape[1])
    one_ref[cap:, :] = pad
    two_ref[cap:, :] = pad


def k_own(me_ref, hott_ref, v_ref, pre_ref, cw_ref, cw2_ref, pool_ref, slope_ref, cwf_ref):
    half = cw_ref.shape[0]
    pool_ref[...] = dot(hott_ref[...], v_ref[...])
    slope_ref[...] = slope_of(pre_ref[...])
    cwf_ref[pl.ds(pl.multiple_of(me_ref[1] * half, half), half), :] = cw_ref[...]
    cwf_ref[pl.ds(pl.multiple_of((1 - me_ref[1]) * half, half), half), :] = cw2_ref[...]


def k_cot(me_ref, ct_ref, ct2_ref, wo_ref, ctc_ref, hg_ref):
    join_halves(me_ref[1], ct_ref, ct2_ref, ctc_ref)
    hg_ref[...] = dot(ctc_ref[...], wo_ref[...])


def arrived_of(sub, got, cap):
    one, one2, two, two2 = got
    rows = slice(0, cap)
    return jnp.concatenate(directed(sub, one, one2, rows) + directed(sub, two, two2, rows), axis=0)


def k_coarse(me_ref, pool_ref, ocount_ref, one_ref, one2_ref, two_ref, two2_ref, cw_ref,
             hits_ref, icount_ref, coarse_ref, cpre_ref, corr_ref, out1_ref, out2_ref):
    nodes, width = pool_ref.shape
    cap = out1_ref.shape[0]
    sub = me_ref[1]
    got = (one_ref, one2_ref, two_ref, two2_ref)
    slots = 4 * cap
    lane = lax.broadcasted_iota(I32, (1, slots), 1)
    row = slice(cap, cap + 1)
    t = directed(sub, one_ref, one2_ref, row) + directed(sub, two_ref, two2_ref, row)
    t = [v[:, 0:slots].astype(F32) for v in t]
    domain, count = me_ref[0], me_ref[4]
    there = (domain >= 1, domain < count - 1, domain >= 2, domain < count - 2)
    t = [jnp.where(ok, v, 0.0) for ok, v in zip(there, t)]
    tags = jnp.where(lane < cap, t[0], jnp.where(lane < 2 * cap, t[1], jnp.where(lane < 3 * cap, t[2], t[3])))
    node = (lax.broadcasted_iota(I32, (nodes, slots), 0) + 1).astype(F32)
    hits = (node == tags).astype(F32)
    count = jnp.maximum(ocount_ref[...] + jnp.sum(hits, axis=1, keepdims=True), 1.0)
    icount = 1.0 / count
    hits_ref[...] = hits
    icount_ref[...] = icount
    hb = hits.astype(BF)
    total = pool_ref[...] + dot(hb, arrived_of(sub, got, cap))
    coarse = (total * wide(icount, width)).astype(BF)
    cpre = dot(coarse, cw_ref[...], NT)
    corr = (cpre * sigmoid(cpre)).astype(BF)
    coarse_ref[...] = coarse
    cpre_ref[...] = cpre
    corr_ref[...] = corr
    ans = dot(hits.T.astype(BF), corr).astype(BF)
    out1_ref[...] = jnp.where(sub == 0, ans[cap:2 * cap], ans[0:cap])
    out2_ref[...] = jnp.where(sub == 0, ans[3 * cap:], ans[2 * cap:3 * cap])


def spread_back(first, hot_ref, slott_ref, corr, one, two):
    returned = jnp.concatenate([one[1], one[0], two[1], two[0]], axis=0)
    total = first.astype(F32) + dot(hot_ref[...], corr) + dot(slott_ref[...], returned)
    return total.astype(BF)


def k_lift(me_ref, first_ref, hot_ref, slott_ref, corr_ref, one_ref, one2_ref, two_ref, two2_ref, pick_ref,
           lift_ref, msg_ref):
    lifted = spread_back(
        first_ref[...], hot_ref, slott_ref, corr_ref[...],
        directed(me_ref[1], one_ref, one2_ref), directed(me_ref[1], two_ref, two2_ref))
    lift_ref[...] = lifted
    rim = msg_ref.shape[0]
    at = pl.multiple_of(me_ref[1] * rim, rim)
    msg_ref[...] = dot(pick_ref[pl.ds(at, rim), :], lifted).astype(BF)


def rim_grads(sub, pg, win_ref, inv_ref, adjt_ref, scaled_ref, msg_ref):
    n = pg.shape[0]
    width = win_ref.shape[1] // 2
    rim = msg_ref.shape[0]
    scaled = (dot(pg, win_ref[:, width:]) * wide(inv_ref[...], width)).astype(BF)
    scaled_ref[...] = scaled
    at = pl.multiple_of(n + (1 - sub) * rim, rim)
    msg_ref[...] = dot(adjt_ref[pl.ds(at, rim), :], scaled).astype(BF)


def k_second(me_ref, lift_ref, rim_ref, rim2_ref, adj_ref, adjt_ref, inv_ref, win_ref, wo_ref, hg_ref,
             agg_ref, hid_ref, new_ref, pg_ref, scaled_ref, msg_ref, src):
    lifted = lift_ref[...]
    fill_sources(me_ref, lifted, directed(me_ref[1], rim_ref, rim2_ref), src)
    agg, pre, hid, out = forward(lifted, src[...], adj_ref, inv_ref, win_ref, wo_ref)
    agg_ref[...] = agg
    hid_ref[...] = hid
    new_ref[...] = out
    pg = (hg_ref[...] * slope_of(pre)).astype(BF)
    pg_ref[...] = pg
    rim_grads(me_ref[1], pg, win_ref, inv_ref, adjt_ref, scaled_ref, msg_ref)


def k_combine(g_ref, pg_ref, win_ref, scaled_ref, adjt_ref, comb_ref):
    n, width = comb_ref.shape
    comb_ref[...] = (
        g_ref[...].astype(F32)
        + dot(pg_ref[...], win_ref[:, 0:width])
        + dot(adjt_ref[0:n, :], scaled_ref[...])
    )


def k_newt(me_ref, hott_ref, lg_ref, new_ref, pool_ref, out_ref):
    half = out_ref.shape[0]
    at = pl.multiple_of(me_ref[1] * half, half)
    out_ref[...] = new_ref[:, pl.ds(at, half)].T
    pool_ref[...] = dot(hott_ref[...], lg_ref[...])


def k_grads(scale, me_ref, pg_ref, h_ref, agg_ref, g_ref, hid_ref, gin_ref, gout_ref):
    half = gin_ref.shape[0]
    width = h_ref.shape[1]
    at = pl.multiple_of(me_ref[1] * half, half)
    pgt = pg_ref[:, pl.ds(at, half)].T
    gin_ref[:, 0:width] = dot(pgt, h_ref[...]) * scale
    gin_ref[:, width:] = dot(pgt, agg_ref[...]) * scale
    gt = g_ref[:, pl.ds(at, half)].T
    gout_ref[...] = dot(gt, hid_ref[...]) * scale


def pack_grads(scale, me_ref, pg_ref, h_ref, agg_ref, g_ref, hid_ref, keep_ref, send_ref):
    width = h_ref.shape[1]
    half = width // 2
    piece = keep_ref.shape[2]
    at = pl.multiple_of(me_ref[1] * half, half)
    pgt = pg_ref[:, pl.ds(at, half)].T
    lo = dot(pgt, h_ref[...]) * scale
    hi = dot(pgt, agg_ref[...]) * scale
    out = dot(hid_ref[...].T, g_ref[:, pl.ds(at, half)]) * scale

    def pieces(d):
        src, c = (lo, d * piece) if d * piece < width else (hi, d * piece - width)
        return [(0, src[:, c:c + piece])] + small_pieces(out, d, piece, half)

    place_pieces(me_ref, pieces, keep_ref, send_ref)


def small_pieces(values, d, piece, row):
    small = values.shape[0] // 8
    mine = values[d * small:(d + 1) * small]
    return [
        (row + c * small, mine[:, c * piece:(c + 1) * piece]) for c in range(values.shape[1] // piece)
    ]


def place_pieces(me_ref, pieces, keep_ref, send_ref):
    for d in range(8):
        for row, value in pieces(d):
            rows = slice(row, row + value.shape[0])

            @pl.when(me_ref[2] == d % 2)
            def _():
                keep_ref[d // 2, rows, :] = value

            @pl.when(me_ref[2] != d % 2)
            def _():
                send_ref[d // 2, rows, :] = value.astype(BF)


def k_combine_pack(scale, me_ref, pg_ref, h_ref, agg_ref, g_ref, hid_ref, win_ref, scaled_ref, adjt_ref,
                   comb_ref, keep_ref, send_ref):
    pack_grads(scale, me_ref, pg_ref, h_ref, agg_ref, g_ref, hid_ref, keep_ref, send_ref)
    k_combine(g_ref, pg_ref, win_ref, scaled_ref, adjt_ref, comb_ref)


def k_cweight_pack(scale, me_ref, pgrad_ref, coarse_ref, keep_ref, send_ref):
    half = pgrad_ref.shape[1] // 2
    piece = keep_ref.shape[2]
    at = pl.multiple_of(me_ref[1] * half, half)
    values = dot(coarse_ref[...].T, pgrad_ref[:, pl.ds(at, half)]) * scale
    place_pieces(me_ref, lambda d: small_pieces(values, d, piece, 0), keep_ref, send_ref)


def placed(me_ref, place_ref, before, after):
    rim = before.shape[0]
    from_after = dot(place_ref[:, 0:rim], after)
    from_before = dot(place_ref[:, rim:], before)
    return jnp.where(me_ref[0] < me_ref[4] - 1, from_after, 0.0) + jnp.where(me_ref[0] >= 1, from_before, 0.0)


def k_lgrad(me_ref, comb_ref, rim_ref, rim2_ref, place_ref, slot_ref, lg_ref, one_ref, two_ref):
    lg = (comb_ref[...] + placed(me_ref, place_ref, *directed(me_ref[1], rim_ref, rim2_ref))).astype(BF)
    lg_ref[...] = lg
    send_slots(me_ref[1], lg, slot_ref, one_ref, two_ref)


def k_cgrad(me_ref, pool_ref, one_ref, one2_ref, two_ref, two2_ref, hits_ref, icount_ref, cpre_ref, cw_ref,
            pgrad_ref, spread_ref, out1_ref, out2_ref):
    cap = out1_ref.shape[0]
    sub = me_ref[1]
    hits = hits_ref[...]
    total = pool_ref[...] + dot(hits.astype(BF), arrived_of(sub, (one_ref, one2_ref, two_ref, two2_ref), cap))
    pgrad = (total * slope_of(cpre_ref[...])).astype(BF)
    pgrad_ref[...] = pgrad
    spread = (dot(pgrad, cw_ref[...]) * wide(icount_ref[...], pgrad.shape[1])).astype(BF)
    spread_ref[...] = spread
    ans = dot(hits.T.astype(BF), spread).astype(BF)
    out1_ref[...] = jnp.where(sub == 0, ans[cap:2 * cap], ans[0:cap])
    out2_ref[...] = jnp.where(sub == 0, ans[3 * cap:], ans[2 * cap:3 * cap])


def k_cweight(scale, me_ref, pgrad_ref, coarse_ref, out_ref):
    half = out_ref.shape[0]
    at = pl.multiple_of(me_ref[1] * half, half)
    out_ref[...] = dot(pgrad_ref[:, pl.ds(at, half)].T, coarse_ref[...]) * scale


def k_third(me_ref, lg_ref, hot_ref, slott_ref, spread_ref, got_ref,
            wo_ref, slope_ref, win_ref, inv_ref, adjt_ref, *rest, scale=None):
    fb_ref, pg_ref, scaled_ref, msg_ref = rest if scale is None else rest[3:7]
    cap = got_ref.shape[1] // 2
    fb = spread_back(
        lg_ref[...], hot_ref, slott_ref, spread_ref[...],
        (got_ref[0, 0:cap], got_ref[1, 0:cap]), (got_ref[0, cap:], got_ref[1, cap:]))
    fb_ref[...] = fb
    pg = (dot(fb, wo_ref[...]) * slope_ref[...]).astype(BF)
    pg_ref[...] = pg
    if scale is not None:
        xc_ref, agg_ref, hid_ref = rest[:3]
        pack_grads(scale, me_ref, pg_ref, xc_ref, agg_ref, fb_ref, hid_ref, rest[7], rest[8])
    rim_grads(me_ref[1], pg, win_ref, inv_ref, adjt_ref, scaled_ref, msg_ref)


def k_last(me_ref, comb_ref, rims_ref, place_ref, *rest):
    half = comb_ref.shape[1]
    at = pl.multiple_of(me_ref[1] * half, half)
    total = comb_ref[...] + placed(
        me_ref, place_ref, rims_ref[0, :, pl.ds(at, half)], rims_ref[1, :, pl.ds(at, half)])
    if len(rest) == 1:
        rest[0][...] = total.T
    else:
        rest[4][...] = total.T
        k_sum(*rest[:4], *rest[5:])


def k_halfcomb(me_ref, fb_ref, pg_ref, win_ref, scaled_ref, adjt_ref, comb_ref):
    n, half = comb_ref.shape
    at = pl.multiple_of(me_ref[1] * half, half)
    cols = pl.ds(at, half)
    comb_ref[...] = (
        fb_ref[:, cols].astype(F32)
        + dot(pg_ref[...], win_ref[:, cols])
        + dot(adjt_ref[0:n, :], scaled_ref[:, cols])
    )


def k_stage(me_ref, *refs):
    pairs = (len(refs) - 4) // 2
    own_ref, outs = refs[2 * pairs], refs[2 * pairs + 1:]
    z = me_ref[3]
    row = 0
    for i in range(pairs):
        keep_ref, got_ref = refs[2 * i], refs[2 * i + 1]
        rows = slice(row, row + keep_ref.shape[1])
        own_ref[rows, :] = keep_ref[z] + got_ref[z].astype(F32)
        for step in (1, 2, 3):
            other = z ^ step
            outs[step - 1][rows, :] = (keep_ref[other] + got_ref[other].astype(F32)).astype(BF)
        row += keep_ref.shape[1]


def k_stage_comb(me_ref, fb_ref, pg_ref, win_ref, scaled_ref, adjt_ref, *refs):
    k_stage(me_ref, *refs[:-1])
    k_halfcomb(me_ref, fb_ref, pg_ref, win_ref, scaled_ref, adjt_ref, refs[-1])


def unpack_small(total):
    small = total.shape[0] // 2
    return jnp.concatenate([total[0:small], total[small:]], axis=1)


def k_sum(own_ref, a_ref, b_ref, c_ref, ein_ref, eout_ref, gco_ref):
    half = ein_ref.shape[0]
    mid = half + 2 * eout_ref.shape[0]
    total = own_ref[...] + a_ref[...].astype(F32) + b_ref[...].astype(F32) + c_ref[...].astype(F32)
    ein_ref[...] = total[0:half]
    eout_ref[...] = unpack_small(total[half:mid])
    gco_ref[...] = unpack_small(total[mid:])


def k_sum_late(own_ref, a_ref, b_ref, c_ref, ein_ref, eout_ref, gin_ref, gout_ref):
    half = ein_ref.shape[0]
    total = own_ref[...] + a_ref[...].astype(F32) + b_ref[...].astype(F32) + c_ref[...].astype(F32)
    gin_ref[0] = total[0:half]
    gin_ref[1] = ein_ref[...]
    gout_ref[0] = unpack_small(total[half:])
    gout_ref[1] = eout_ref[...]


def local(node_features, inward_weight, outward_weight, coarse_weight, tile_index, tile_mask,
          send_rows, parent, cotangent):
    half, n = node_features.shape
    width = 2 * half
    blocks, k_slots = tile_index.shape
    rim = tile_mask.shape[2]
    src_rows = (blocks + 2) * rim
    domains = lax.axis_size(DOM)
    cross = lax.axis_size("cross")
    curve = lax.axis_size("curve")
    cap = n // 16
    nodes = n // 4
    slots = 4 * cap
    hidden = 2 * inward_weight.shape[1]
    scale = float(n * domains) ** -0.5
    me = jnp.stack(
        [lax.axis_index(a) for a in (DOM, "sub", "cross", "curve")] + [jnp.int32(domains)]).astype(I32)
    rows = send_rows[0]
    packed = cross == 2 and curve == 4 and 2 * width == 1024 and hidden == width

    cell_bf, cell_f32 = sds((n, width), BF), sds((n, width), F32)
    win2, wout2 = swap(inward_weight), swap(outward_weight)
    x_full = gather(node_features).reshape(width, n)
    xc, rims = call(k_halo, [cell_bf, sds((rim, width), BF)], [me], [rows, x_full], "halo")
    rims = two_way(rims, 1)
    (adj, adjt, inv, hott, hot, slot, slott, pick, place, tags, ocount) = call(
        k_prep,
        [sds((n, src_rows), BF), sds((src_rows, n), BF), sds((n, 128), F32), sds((nodes, n), BF),
         sds((n, nodes), BF), sds((slots, n), BF), sds((n, slots), BF), sds((2 * rim, n), BF),
         sds((n, 2 * rim), BF), sds((16, slots), BF), sds((nodes, 128), F32)],
        [tile_index, me], [tile_mask, rows, parent[None, :]], "prep")
    weight_outs = [sds((hidden, 2 * width), BF), sds((width, hidden), BF)]
    win0, wo0 = call(lambda *r: k_weights(0, *r), weight_outs, [me],
                     [inward_weight, outward_weight, win2, wout2], "weights0")
    rims, win0, adj = lax.optimization_barrier((rims, win0, adj))
    msg = sds((cap + 16, width), BF)
    plain = sds((cap, width), BF)
    hid_bf, hid_f32 = sds((n, hidden), BF), sds((n, hidden), F32)
    agg0, pre0, hid0, first, one, two = call(
        k_first,
        [cell_bf, hid_f32, hid_bf, cell_bf, msg, msg],
        [me], [xc, gather(rims), adj, inv, win0, wo0, slot, tags], "first",
        flops=2 * n * width * (src_rows + 3 * width),
        scratch=[pltpu.VMEM((src_rows, width), BF)])
    one, two, win2, coarse_weight = lax.optimization_barrier((one, two, win2, coarse_weight))
    one, two = two_way(one, 1), two_way(two, 2)
    own, slope0, cw = call(
        k_own, [sds((nodes, width), F32), hid_f32, sds((width, width), BF)], [me],
        [hott, first, pre0, coarse_weight, swap(coarse_weight)], "own")
    win1, wo1 = call(lambda *r: k_weights(1, *r), weight_outs, [me],
                     [inward_weight, outward_weight, win2, wout2], "weights1")
    one, two, own = lax.optimization_barrier((one, two, own))
    got = shared(one, two)
    node_bf, node_f32 = sds((nodes, width), BF), sds((nodes, width), F32)
    hits, icount, coarse, cpre, corr, one, two = call(
        k_coarse, [sds((nodes, slots), F32), sds((nodes, 128), F32), node_bf, node_f32, node_bf, plain, plain],
        [me], [own, ocount, *got, cw], "coarse")
    one, two, cotangent = lax.optimization_barrier((one, two, cotangent))
    one, two = two_way(one, 1), two_way(two, 2)
    ctc, hg1 = call(k_cot, [cell_bf, hid_f32], [me], [cotangent, swap(cotangent), wo1], "cot")
    one, two, win1 = lax.optimization_barrier((one, two, win1))
    got = shared(one, two)
    lifted, rims = call(
        k_lift, [cell_bf, sds((rim, width), BF)], [me],
        [first, hot, slott, corr, *got, pick], "lift")
    rims, hg1 = lax.optimization_barrier((two_way(rims, 1), hg1))
    rims = shared(rims)
    agg1, hid1, new, pg1, scaled1, rims = call(
        k_second, [cell_bf, hid_bf, cell_bf, hid_bf, cell_bf, sds((rim, width), BF)],
        [me], [lifted, *rims, adj, adjt, inv, win1, wo1, hg1], "second",
        scratch=[pltpu.VMEM((src_rows, width), BF)])
    rims = two_way(rims, 1)
    piece = 2 * width // domains
    small = hidden // domains
    layer_rows = half + 2 * small
    pack = [sds((curve, layer_rows, piece), F32), sds((curve, layer_rows, piece), BF)]
    if packed:
        comb1, keep1, send1 = call(
            lambda *r: k_combine_pack(scale, *r), [cell_f32] + pack, [me],
            [pg1, lifted, agg1, ctc, hid1, win1, scaled1, adjt], "combine")
        got1 = cross_swap(send1)
    else:
        comb1, = call(k_combine, [cell_f32], [], [ctc, pg1, win1, scaled1, adjt], "combine")
    rims, comb1 = lax.optimization_barrier((rims, comb1))
    rims = shared(rims)
    lg, one, two = call(
        k_lgrad, [cell_bf, plain, plain], [me], [comb1, *rims, place, slot], "lgrad")
    one, two = two_way(one, 1), two_way(two, 2)
    own_g, new_t = call(k_newt, [node_f32, sds((half, n), BF)], [me], [hott, lg, new], "own_grad")
    one, two, own_g = lax.optimization_barrier((one, two, own_g))
    got = shared(one, two)
    pgrad, spread, one, two = call(
        k_cgrad, [node_bf, node_bf, plain, plain], [me],
        [own_g, *got, hits, icount, cpre, cw], "cgrad")
    one, two = two_way(one, 1), two_way(two, 2)
    if packed:
        keepc, sendc = call(
            lambda *r: k_cweight_pack(scale, *r),
            [sds((curve, 2 * small, piece), F32), sds((curve, 2 * small, piece), BF)], [me],
            [pgrad, coarse], "cweight")
        gotc = cross_swap(sendc)
    got = gather(jnp.concatenate([one, two], axis=0))
    back_outs = [cell_bf, hid_bf, cell_bf, sds((rim, width), BF)]
    if packed:
        got, got1 = lax.optimization_barrier((got, got1))
    if packed:
        fb, pg0, scaled0, rims, keep0, send0 = call(
            lambda *r: k_third(*r, scale=scale), back_outs + pack, [me],
            [lg, hot, slott, spread, got, wo0, slope0, win0, inv, adjt, xc, agg0, hid0], "third")
        send0, gotc = lax.optimization_barrier((send0, gotc))
        got0 = cross_swap(send0)
        keepc, pg0 = lax.optimization_barrier((keepc, pg0))
        rims = two_way(rims, 1)

        def staged(body, extra, extra_outs, pairs, name):
            total = sum(keep.shape[1] for keep in pairs[::2])
            own, *outs = call(
                body, [sds((total, piece), F32)] + [sds((total, piece), BF)] * 3 + extra_outs,
                [me], extra + pairs, name)
            return [own] + [curve_swap(value, step) for step, value in zip((1, 2, 3), outs)], outs[3:]

        early, (comb0,) = staged(
            k_stage_comb, [fb, pg0, win0, scaled0, adjt], [sds((n, half), F32)],
            [keep1, got1, keepc, gotc], "stage1")
        late, _ = staged(k_stage, [], [], [keep0, got0], "stage0")
    else:
        gco, = call(lambda *r: k_cweight(scale, *r), [sds((half, width), F32)], [me], [pgrad, coarse], "cweight")
        fb, pg0, scaled0, rims = call(
            k_third, back_outs, [me], [lg, hot, slott, spread, got, wo0, slope0, win0, inv, adjt], "third")
        rims = two_way(rims, 1)
        comb0, = call(k_halfcomb, [sds((n, half), F32)], [me], [fb, pg0, win0, scaled0, adjt], "halfcomb")
    rims = gather(rims)
    if packed:
        fgrad, ein, eout, gco = call(
            k_last, [sds((half, n), F32), sds((half, piece), F32), sds((small, half), F32), sds((small, half), F32)],
            [me], [comb0, rims, place] + early, "last")
        gin, gout = call(
            k_sum_late, [sds((2, half, piece), F32), sds((2, small, half), F32)], [], late + [ein, eout], "late")
        gout = gout.swapaxes(1, 2)
        gco = gco.T
    else:
        fgrad, = call(k_last, [sds((half, n), F32)], [me], [comb0, rims, place], "last")
        shapes = [sds((half, 2 * width), F32), sds((half, hidden), F32)]
        gi1, go1 = call(lambda *r: k_grads(scale, *r), shapes, [me], [pg1, lifted, agg1, ctc, hid1], "grads1")
        gi0, go0 = call(lambda *r: k_grads(scale, *r), shapes, [me], [pg0, xc, agg0, fb, hid0], "grads0")
        gin = lax.psum_scatter(jnp.stack([gi0, gi1]), DOM, scatter_dimension=2, tiled=True)
        gout = lax.psum_scatter(jnp.stack([go0, go1]), DOM, scatter_dimension=2, tiled=True)
        gco = lax.psum_scatter(gco, DOM, scatter_dimension=1, tiled=True)
    return new_t, fgrad, gin, gout, gco


def solution(mesh):
    cells = ("groups", "curve", "cross")
    in_specs = (
        P("sub", cells),
        P(None, "sub", None),
        P(None, "sub", None),
        P("sub", None),
        P(cells, None),
        P(cells, None, None, None),
        P(cells, None, None),
        P(cells),
        P("sub", cells),
    )
    out_specs = (
        P("sub", cells),
        P("sub", cells),
        P("groups", "sub", ("curve", "cross")),
        P("groups", "sub", ("curve", "cross")),
        P(("groups", "sub"), ("curve", "cross")),
    )
    return jax.shard_map(local, mesh=mesh, in_specs=in_specs, out_specs=out_specs, check_vma=False)
```

```python
import jax
import jax.numpy as jnp
from jax import lax
from jax.experimental import pallas as pl
from jax.experimental.pallas import tpu as pltpu
from jax.sharding import PartitionSpec as P

BF = jnp.bfloat16
F32 = jnp.float32
I32 = jnp.int32
DOM = ("curve", "cross")
LINE = ("curve", "cross", "sub")
NN = (((1,), (0,)), ((), ()))
NT = (((1,), (1,)), ((), ()))
TN = (((0,), (0,)), ((), ()))


def dot(a, b, dims=NN):
    return lax.dot_general(a, b, dims, preferred_element_type=F32)


def sds(shape, dtype):
    return jax.ShapeDtypeStruct(shape, dtype)


def call(body, outs, scalars, arrays, name, flops=0, scratch=()):
    scalars, arrays = list(scalars), list(arrays)
    moved = sum(a.size * a.dtype.itemsize for a in arrays) + sum(
        o.size * o.dtype.itemsize for o in outs
    )
    return pl.pallas_call(
        body,
        out_shape=tuple(outs),
        in_specs=[pl.BlockSpec(memory_space=pltpu.SMEM)] * len(scalars)
        + [pl.BlockSpec(memory_space=pltpu.VMEM)] * len(arrays),
        out_specs=tuple(pl.BlockSpec(memory_space=pltpu.VMEM) for _ in outs),
        scratch_shapes=list(scratch),
        compiler_params=pltpu.CompilerParams(vmem_limit_bytes=20 * 2**20),
        cost_estimate=pl.CostEstimate(flops=flops, bytes_accessed=moved, transcendentals=0),
        name=name,
    )(*scalars, *arrays)


def two_way(value, steps, forward=0):
    count = lax.axis_size(DOM)
    back = 1 - forward
    pairs = [(2 * p + forward, 2 * (p + steps) + forward) for p in range(count - steps)]
    pairs += [(2 * p + back, 2 * (p - steps) + back) for p in range(steps, count)]
    pairs += [(2 * p + forward, 2 * p + back) for p in range(count - steps, count)]
    pairs += [(2 * p + back, 2 * p + forward) for p in range(steps)]
    return lax.ppermute(value, LINE, pairs)


def swap(value):
    return lax.ppermute(value, "sub", [(0, 1), (1, 0)])


def gather(value):
    return lax.all_gather(value, "sub", axis=0, tiled=False)


def shared(*values):
    return [v for value in values for v in (value, swap(value))]


def directed(sub, own_ref, other_ref, rows=slice(None)):
    own, other = own_ref[rows, :], other_ref[rows, :]
    return jnp.where(sub == 0, own, other), jnp.where(sub == 0, other, own)


def cross_swap(value):
    return lax.ppermute(value, "cross", [(0, 1), (1, 0)])


def curve_swap(value, step):
    return lax.ppermute(value, "curve", [(z, z ^ step) for z in range(4)])


def sigmoid(v):
    return 1.0 / (1.0 + jnp.exp(-v))


def slope_of(v):
    s = sigmoid(v)
    return s * (1.0 + v * (1.0 - s))


def wide(col, width):
    return jnp.concatenate([col] * (width // col.shape[1]), axis=1)


def join_halves(sub, own_ref, other_ref, out_ref):
    half = own_ref.shape[0]
    out_ref[:, pl.ds(pl.multiple_of(sub * half, half), half)] = own_ref[...].T
    out_ref[:, pl.ds(pl.multiple_of((1 - sub) * half, half), half)] = other_ref[...].T


def k_halo(me_ref, rows_ref, x_ref, a_ref, b_ref):
    half_x = x_ref[...]
    for flip, out_ref in enumerate((a_ref, b_ref)):
        row = jnp.where(me_ref[1] == flip, rows_ref[0:1, :], rows_ref[1:2, :])
        at = lax.broadcasted_iota(I32, (half_x.shape[1], row.shape[1]), 0)
        out_ref[...] = dot(half_x, (at == row).astype(F32).astype(BF)).T.astype(BF)


def k_weights(layer, me_ref, win_ref, wout_ref, win2_ref, wout2_ref, in_ref, out_ref):
    half = win_ref.shape[1]
    own = pl.multiple_of(me_ref[1] * half, half)
    other = pl.multiple_of((1 - me_ref[1]) * half, half)
    in_ref[pl.ds(own, half), :] = win_ref[layer]
    in_ref[pl.ds(other, half), :] = win2_ref[layer]
    out_ref[pl.ds(own, half), :] = wout_ref[layer]
    out_ref[pl.ds(other, half), :] = wout2_ref[layer]


def k_prep(tile_ref, me_ref, mask_ref, rows_ref, par_ref, x_ref, xc_ref,
           adj_ref, adjt_ref, inv_ref, hott_ref, hot_ref, slot_ref, slott_ref,
           pick_ref, place_ref, tags_ref, ocount_ref, rsel_ref):
    blocks, k_slots, length, _ = mask_ref.shape
    n = adj_ref.shape[0]
    nodes = hott_ref.shape[0]
    slots = slot_ref.shape[0]
    cap = slots // 4
    xc_ref[...] = x_ref[...].T
    adj_ref[...] = jnp.zeros(adj_ref.shape, BF)
    adjt_ref[...] = jnp.zeros(adjt_ref.shape, BF)
    for b in range(blocks):
        degree = jnp.zeros((length, 1), F32)
        for k in range(k_slots):
            bits = mask_ref[b, k].astype(F32)
            start = pl.multiple_of(tile_ref[b, k] * length, length)
            adj_ref[b * length:(b + 1) * length, pl.ds(start, length)] = bits.astype(BF)
            adjt_ref[pl.ds(start, length), b * length:(b + 1) * length] = bits.T.astype(BF)
            degree = degree + jnp.sum(bits, axis=1, keepdims=True)
        inv_ref[b * length:(b + 1) * length, :] = jnp.broadcast_to(1.0 / degree, (length, 128))
    rel_row = par_ref[...] - me_ref[0] * nodes
    hott = (lax.broadcasted_iota(I32, (nodes, n), 0) == rel_row).astype(F32)
    hott_ref[...] = hott.astype(BF)
    ocount_ref[...] = jnp.broadcast_to(jnp.sum(hott, axis=1, keepdims=True), (nodes, 128))
    hot_ref[...] = hott.T.astype(BF)
    j = lax.broadcasted_iota(I32, (slots, n), 0)
    off = jnp.where(j < cap, 1, jnp.where(j < 2 * cap, -1, jnp.where(j < 3 * cap, 2, -2)))
    start = jnp.where(j < cap, 0, jnp.where(j < 2 * cap, cap, jnp.where(j < 3 * cap, 2 * cap, 3 * cap)))
    node = rel_row - off * nodes
    chosen = ((node >= 0) & (node < nodes)).astype(F32)
    before = lax.broadcasted_iota(I32, (n, n), 0) < lax.broadcasted_iota(I32, (n, n), 1)
    rank = dot(chosen.astype(BF), before.astype(F32).astype(BF))
    fits = jnp.where(rank == (j - start).astype(F32), chosen, 0.0)
    slot_ref[...] = fits.astype(BF)
    slott_ref[...] = fits.T.astype(BF)
    tags = jnp.sum(fits * (node + 1).astype(F32), axis=1, keepdims=True)
    tags_ref[...] = jnp.broadcast_to(tags, (slots, slots)).T[0:tags_ref.shape[0], :].astype(BF)
    width = rows_ref.shape[1]
    at = lax.broadcasted_iota(I32, (n, width), 0)
    for c in range(2):
        place = (at == rows_ref[c:c + 1, :]).astype(F32)
        place_ref[:, c * width:(c + 1) * width] = place.astype(BF)
        pick_ref[c * width:(c + 1) * width, :] = place.T.astype(BF)
    at = pl.multiple_of(me_ref[1] * width, width)
    sent = dot(slot_ref[...], place_ref[:, pl.ds(at, width)]).astype(BF)
    for c in range(4):
        rsel_ref[:, c * width:(c + 1) * width] = sent[c * cap:(c + 1) * cap]


def forward(xc, src, adj_ref, inv_ref, win_ref, wo_ref):
    width = xc.shape[1]
    agg = (dot(adj_ref[...], src) * wide(inv_ref[...], width)).astype(BF)
    pre = dot(xc, win_ref[:, 0:width], NT) + dot(agg, win_ref[:, width:], NT)
    hid = (pre * sigmoid(pre)).astype(BF)
    out = (xc.astype(F32) + dot(hid, wo_ref[...], NT)).astype(BF)
    return agg, pre, hid, out


def send_slots(sub, values, slot_ref, one_ref, two_ref):
    cap = slot_ref.shape[0] // 4
    a = pl.multiple_of(sub * cap, cap)
    one_ref[0:cap, :] = dot(slot_ref[pl.ds(a, cap), :], values).astype(BF)
    two_ref[0:cap, :] = dot(slot_ref[pl.ds(a + 2 * cap, cap), :], values).astype(BF)


def fill_sources(me_ref, xc, rims, src):
    n = xc.shape[0]
    rim = rims[0].shape[0]
    src[0:n, :] = xc
    for c in range(2):
        rows = slice(n + c * rim, n + (c + 1) * rim)
        there = me_ref[0] >= 1 if c == 0 else me_ref[0] < me_ref[4] - 1

        @pl.when(there)
        def _():
            src[rows, :] = rims[c]

        @pl.when(jnp.logical_not(there))
        def _():
            src[rows, :] = jnp.zeros((rim, xc.shape[1]), BF)


def k_first(me_ref, xc_ref, rims_ref, adj_ref, inv_ref, win_ref, wo_ref,
            slot_ref, tags_ref, rsel_ref,
            agg_ref, pre_ref, hid_ref, first_ref, one_ref, two_ref, src):
    xc = xc_ref[...]
    rim = rims_ref.shape[1] // 2
    before = jnp.concatenate([rims_ref[0, 0:rim], rims_ref[1, rim:]], axis=1)
    after = jnp.concatenate([rims_ref[0, rim:], rims_ref[1, 0:rim]], axis=1)
    fill_sources(me_ref, xc, (before, after), src)
    agg, pre, hid, out = forward(xc, src[...], adj_ref, inv_ref, win_ref, wo_ref)
    agg_ref[...] = agg
    pre_ref[...] = pre
    hid_ref[...] = hid
    first_ref[...] = out
    send_slots(me_ref[1], out, slot_ref, one_ref, two_ref)
    cap = slot_ref.shape[0] // 4
    pad = wide(tags_ref[...], two_ref.shape[1])
    tag_rows = tags_ref.shape[0]
    one_ref[cap:cap + tag_rows, :] = pad
    one_ref[cap + tag_rows:, :] = rsel_ref[...]
    two_ref[cap:, :] = pad


def k_own(me_ref, hott_ref, v_ref, pre_ref, cw_ref, cw2_ref, pool_ref, slope_ref, cwf_ref):
    half = cw_ref.shape[0]
    pool_ref[...] = dot(hott_ref[...], v_ref[...])
    slope_ref[...] = slope_of(pre_ref[...])
    cwf_ref[pl.ds(pl.multiple_of(me_ref[1] * half, half), half), :] = cw_ref[...]
    cwf_ref[pl.ds(pl.multiple_of((1 - me_ref[1]) * half, half), half), :] = cw2_ref[...]


def k_cot(me_ref, ct_ref, ct2_ref, wo_ref, ctc_ref, hg_ref):
    join_halves(me_ref[1], ct_ref, ct2_ref, ctc_ref)
    hg_ref[...] = dot(ctc_ref[...], wo_ref[...])


def arrived_of(sub, got, cap):
    one, one2, two, two2 = got
    rows = slice(0, cap)
    return jnp.concatenate(directed(sub, one, one2, rows) + directed(sub, two, two2, rows), axis=0)


def k_coarse(me_ref, pool_ref, ocount_ref, one_ref, one2_ref, two_ref, two2_ref, cw_ref,
             hits_ref, icount_ref, coarse_ref, cpre_ref, corr_ref, out1_ref, out2_ref, rsb_ref, rsa_ref):
    nodes, width = pool_ref.shape
    cap = out1_ref.shape[0]
    sub = me_ref[1]
    got = (one_ref, one2_ref, two_ref, two2_ref)
    slots = 4 * cap
    lane = lax.broadcasted_iota(I32, (1, slots), 1)
    row = slice(cap, cap + 1)
    t = directed(sub, one_ref, one2_ref, row) + directed(sub, two_ref, two2_ref, row)
    t = [v[:, 0:slots].astype(F32) for v in t]
    domain, count = me_ref[0], me_ref[4]
    there = (domain >= 1, domain < count - 1, domain >= 2, domain < count - 2)
    t = [jnp.where(ok, v, 0.0) for ok, v in zip(there, t)]
    packed = directed(sub, one_ref, one2_ref, slice(one_ref.shape[0] - cap, one_ref.shape[0]))
    rim = width // 4
    for ok, value, ref in zip(there, packed, (rsb_ref, rsa_ref)):
        value = jnp.where(ok, value.astype(F32), 0.0).astype(BF)
        for c in range(4):
            ref[c * cap:(c + 1) * cap, :] = value[:, c * rim:(c + 1) * rim]
    tags = jnp.where(lane < cap, t[0], jnp.where(lane < 2 * cap, t[1], jnp.where(lane < 3 * cap, t[2], t[3])))
    node = (lax.broadcasted_iota(I32, (nodes, slots), 0) + 1).astype(F32)
    hits = (node == tags).astype(F32)
    count = jnp.maximum(ocount_ref[...] + jnp.sum(hits, axis=1, keepdims=True), 1.0)
    icount = 1.0 / count
    hits_ref[...] = hits
    icount_ref[...] = icount
    hb = hits.astype(BF)
    total = pool_ref[...] + dot(hb, arrived_of(sub, got, cap))
    coarse = (total * wide(icount, width)).astype(BF)
    cpre = dot(coarse, cw_ref[...], NT)
    corr = (cpre * sigmoid(cpre)).astype(BF)
    coarse_ref[...] = coarse
    cpre_ref[...] = cpre
    corr_ref[...] = corr
    ans = dot(hits.T.astype(BF), corr).astype(BF)
    out1_ref[...] = jnp.where(sub == 0, ans[cap:2 * cap], ans[0:cap])
    out2_ref[...] = jnp.where(sub == 0, ans[3 * cap:], ans[2 * cap:3 * cap])


def spread_back(first, hot_ref, slott_ref, corr, one, two):
    returned = jnp.concatenate([one[1], one[0], two[1], two[0]], axis=0)
    total = first.astype(F32) + dot(hot_ref[...], corr) + dot(slott_ref[...], returned)
    return total.astype(BF)


def k_lift(me_ref, first_ref, hot_ref, slott_ref, corr_ref, one_ref, one2_ref, two_ref, two2_ref, pick_ref,
           lift_ref, msg_ref):
    lifted = spread_back(
        first_ref[...], hot_ref, slott_ref, corr_ref[...],
        directed(me_ref[1], one_ref, one2_ref), directed(me_ref[1], two_ref, two2_ref))
    lift_ref[...] = lifted
    rim = msg_ref.shape[0]
    at = pl.multiple_of(me_ref[1] * rim, rim)
    msg_ref[...] = dot(pick_ref[pl.ds(at, rim), :], lifted).astype(BF)


def rim_grads(sub, pg, win_ref, inv_ref, adjt_ref, scaled_ref, msg_ref):
    n = pg.shape[0]
    width = win_ref.shape[1] // 2
    rim = msg_ref.shape[0]
    scaled = (dot(pg, win_ref[:, width:]) * wide(inv_ref[...], width)).astype(BF)
    scaled_ref[...] = scaled
    at = pl.multiple_of(n + (1 - sub) * rim, rim)
    msg_ref[...] = dot(adjt_ref[pl.ds(at, rim), :], scaled).astype(BF)


def k_second(me_ref, lift_ref, rim_ref, rim2_ref, adj_ref, adjt_ref, inv_ref, win_ref, wo_ref, hg_ref, g_ref,
             slot_ref, rsb_ref, rsa_ref,
             agg_ref, hid_ref, new_ref, pg_ref, comb_ref, near_ref, one_ref, two_ref, three_ref, src):
    lifted = lift_ref[...]
    n, width = lifted.shape
    fill_sources(me_ref, lifted, directed(me_ref[1], rim_ref, rim2_ref), src)
    agg, pre, hid, out = forward(lifted, src[...], adj_ref, inv_ref, win_ref, wo_ref)
    agg_ref[...] = agg
    hid_ref[...] = hid
    new_ref[...] = out
    pg = (hg_ref[...] * slope_of(pre)).astype(BF)
    pg_ref[...] = pg
    scaled = (dot(pg, win_ref[:, width:]) * wide(inv_ref[...], width)).astype(BF)
    comb = g_ref[...].astype(F32) + dot(pg, win_ref[:, 0:width]) + dot(adjt_ref[0:n, :], scaled)
    comb_ref[...] = comb
    rims = dot(adjt_ref[n:, :], scaled).astype(BF)
    rim = rims.shape[0] // 2
    before, after = rims[0:rim], rims[rim:]
    cap = slot_ref.shape[0] // 4
    own = dot(slot_ref[...], comb.astype(BF)).astype(BF)
    of_before, of_after = dot(rsb_ref[...], before), dot(rsa_ref[...], after)
    near_ref[0:cap, :] = of_before[0:cap]
    near_ref[cap:, :] = of_after[cap:2 * cap]
    of_before, of_after = of_before.astype(BF), of_after.astype(BF)

    @pl.when(me_ref[1] == 0)
    def _():
        one_ref[0:rim, :] = after
        one_ref[rim:rim + cap, :] = own[0:cap]
        one_ref[rim + cap:, :] = of_before[2 * cap:3 * cap]
        two_ref[0:cap, :] = own[2 * cap:3 * cap]
        two_ref[cap:, :] = of_after[0:cap]
        three_ref[...] = of_after[2 * cap:3 * cap]

    @pl.when(me_ref[1] == 1)
    def _():
        one_ref[0:rim, :] = before
        one_ref[rim:rim + cap, :] = own[cap:2 * cap]
        one_ref[rim + cap:, :] = of_after[3 * cap:]
        two_ref[0:cap, :] = own[3 * cap:]
        two_ref[cap:, :] = of_before[cap:2 * cap]
        three_ref[...] = of_before[3 * cap:]


def k_newt(me_ref, new_ref, out_ref):
    half = out_ref.shape[0]
    at = pl.multiple_of(me_ref[1] * half, half)
    out_ref[...] = new_ref[:, pl.ds(at, half)].T


def k_grads(scale, me_ref, pg_ref, h_ref, agg_ref, g_ref, hid_ref, gin_ref, gout_ref):
    half = gin_ref.shape[0]
    width = h_ref.shape[1]
    at = pl.multiple_of(me_ref[1] * half, half)
    pgt = pg_ref[:, pl.ds(at, half)].T
    gin_ref[:, 0:width] = dot(pgt, h_ref[...]) * scale
    gin_ref[:, width:] = dot(pgt, agg_ref[...]) * scale
    gt = g_ref[:, pl.ds(at, half)].T
    gout_ref[...] = dot(gt, hid_ref[...]) * scale


def pack_grads(scale, me_ref, pg_ref, h_ref, agg_ref, g_ref, hid_ref, keep_ref, send_ref):
    width = h_ref.shape[1]
    half = width // 2
    piece = keep_ref.shape[2]
    at = pl.multiple_of(me_ref[1] * half, half)
    pgt = pg_ref[:, pl.ds(at, half)].T
    lo = dot(pgt, h_ref[...]) * scale
    hi = dot(pgt, agg_ref[...]) * scale
    out = dot(hid_ref[...].T, g_ref[:, pl.ds(at, half)]) * scale

    def pieces(d):
        src, c = (lo, d * piece) if d * piece < width else (hi, d * piece - width)
        return [(0, src[:, c:c + piece])] + small_pieces(out, d, piece, half)

    place_pieces(me_ref, pieces, keep_ref, send_ref)


def small_pieces(values, d, piece, row):
    small = values.shape[0] // 8
    mine = values[d * small:(d + 1) * small]
    return [
        (row + c * small, mine[:, c * piece:(c + 1) * piece]) for c in range(values.shape[1] // piece)
    ]


def place_pieces(me_ref, pieces, keep_ref, send_ref):
    for d in range(8):
        for row, value in pieces(d):
            rows = slice(row, row + value.shape[0])

            @pl.when(me_ref[2] == d % 2)
            def _():
                keep_ref[d // 2, rows, :] = value

            @pl.when(me_ref[2] != d % 2)
            def _():
                send_ref[d // 2, rows, :] = value.astype(BF)


def k_newt_pack(scale, me_ref, new_ref, pg_ref, h_ref, agg_ref, g_ref, hid_ref, out_ref, keep_ref, send_ref):
    pack_grads(scale, me_ref, pg_ref, h_ref, agg_ref, g_ref, hid_ref, keep_ref, send_ref)
    k_newt(me_ref, new_ref, out_ref)


def k_cweight_pack(scale, me_ref, pgrad_ref, coarse_ref, keep_ref, send_ref):
    half = pgrad_ref.shape[1] // 2
    piece = keep_ref.shape[2]
    at = pl.multiple_of(me_ref[1] * half, half)
    values = dot(coarse_ref[...].T, pgrad_ref[:, pl.ds(at, half)]) * scale
    place_pieces(me_ref, lambda d: small_pieces(values, d, piece, 0), keep_ref, send_ref)


def placed(me_ref, place_ref, before, after):
    rim = before.shape[0]
    from_after = dot(place_ref[:, 0:rim], after)
    from_before = dot(place_ref[:, rim:], before)
    return jnp.where(me_ref[0] < me_ref[4] - 1, from_after, 0.0) + jnp.where(me_ref[0] >= 1, from_before, 0.0)


def k_cgrad(me_ref, comb_ref, place_ref, hott_ref, near_ref, one_ref, one2_ref, two_ref, two2_ref,
            three_ref, three2_ref, hits_ref, icount_ref, cpre_ref, cw_ref,
            lg_ref, pgrad_ref, spread_ref, out1_ref, out2_ref):
    cap = out1_ref.shape[0]
    rim = place_ref.shape[1] // 2
    sub, domain, count = me_ref[1], me_ref[0], me_ref[4]
    hits = hits_ref[...]
    lg = comb_ref[...] + placed(me_ref, place_ref, *directed(sub, one_ref, one2_ref, slice(0, rim)))
    lg = lg.astype(BF)
    lg_ref[...] = lg

    def pieces(own_ref, other_ref, start, there=None):
        both = directed(sub, own_ref, other_ref, slice(start, start + cap))
        both = [v.astype(F32) for v in both]
        if there is None:
            return both
        return [jnp.where(ok, v, 0.0) for ok, v in zip(there, both)]

    near = pieces(one_ref, one2_ref, rim)
    near_rim = pieces(two_ref, two2_ref, cap, (domain >= 2, domain < count - 2))
    far = pieces(two_ref, two2_ref, 0)
    far_rim = pieces(one_ref, one2_ref, rim + cap)
    far_rim3 = pieces(three_ref, three2_ref, 0, (domain >= 3, domain < count - 3))
    arrived = [near[c] + near_rim[c] + near_ref[c * cap:(c + 1) * cap, :] for c in range(2)]
    arrived += [far[c] + far_rim[c] + far_rim3[c] for c in range(2)]
    arrived = jnp.concatenate(arrived, axis=0).astype(BF)
    total = dot(hott_ref[...], lg) + dot(hits.astype(BF), arrived)
    pgrad = (total * slope_of(cpre_ref[...])).astype(BF)
    pgrad_ref[...] = pgrad
    spread = (dot(pgrad, cw_ref[...]) * wide(icount_ref[...], pgrad.shape[1])).astype(BF)
    spread_ref[...] = spread
    ans = dot(hits.T.astype(BF), spread).astype(BF)
    out1_ref[...] = jnp.where(sub == 0, ans[cap:2 * cap], ans[0:cap])
    out2_ref[...] = jnp.where(sub == 0, ans[3 * cap:], ans[2 * cap:3 * cap])


def k_cweight(scale, me_ref, pgrad_ref, coarse_ref, out_ref):
    half = out_ref.shape[0]
    at = pl.multiple_of(me_ref[1] * half, half)
    out_ref[...] = dot(pgrad_ref[:, pl.ds(at, half)].T, coarse_ref[...]) * scale


def k_third(me_ref, lg_ref, hot_ref, slott_ref, spread_ref, got_ref,
            wo_ref, slope_ref, win_ref, inv_ref, adjt_ref, *rest, scale=None):
    fb_ref, pg_ref, scaled_ref, msg_ref = rest if scale is None else rest[3:7]
    cap = got_ref.shape[1] // 2
    fb = spread_back(
        lg_ref[...], hot_ref, slott_ref, spread_ref[...],
        (got_ref[0, 0:cap], got_ref[1, 0:cap]), (got_ref[0, cap:], got_ref[1, cap:]))
    fb_ref[...] = fb
    pg = (dot(fb, wo_ref[...]) * slope_ref[...]).astype(BF)
    pg_ref[...] = pg
    if scale is not None:
        xc_ref, agg_ref, hid_ref = rest[:3]
        pack_grads(scale, me_ref, pg_ref, xc_ref, agg_ref, fb_ref, hid_ref, rest[7], rest[8])
    rim_grads(me_ref[1], pg, win_ref, inv_ref, adjt_ref, scaled_ref, msg_ref)


def k_last(me_ref, comb_ref, rims_ref, place_ref, *rest):
    half = comb_ref.shape[1]
    at = pl.multiple_of(me_ref[1] * half, half)
    total = comb_ref[...] + placed(
        me_ref, place_ref, rims_ref[0, :, pl.ds(at, half)], rims_ref[1, :, pl.ds(at, half)])
    if len(rest) == 1:
        rest[0][...] = total.T
    else:
        rest[4][...] = total.T
        k_sum(*rest[:4], *rest[5:])


def k_halfcomb(me_ref, fb_ref, pg_ref, win_ref, scaled_ref, adjt_ref, comb_ref):
    n, half = comb_ref.shape
    at = pl.multiple_of(me_ref[1] * half, half)
    cols = pl.ds(at, half)
    comb_ref[...] = (
        fb_ref[:, cols].astype(F32)
        + dot(pg_ref[...], win_ref[:, cols])
        + dot(adjt_ref[0:n, :], scaled_ref[:, cols])
    )


def k_stage(me_ref, *refs):
    pairs = (len(refs) - 4) // 2
    own_ref, outs = refs[2 * pairs], refs[2 * pairs + 1:]
    z = me_ref[3]
    row = 0
    for i in range(pairs):
        keep_ref, got_ref = refs[2 * i], refs[2 * i + 1]
        rows = slice(row, row + keep_ref.shape[1])
        own_ref[rows, :] = keep_ref[z] + got_ref[z].astype(F32)
        for step in (1, 2, 3):
            other = z ^ step
            outs[step - 1][rows, :] = (keep_ref[other] + got_ref[other].astype(F32)).astype(BF)
        row += keep_ref.shape[1]


def k_stage_comb(me_ref, fb_ref, pg_ref, win_ref, scaled_ref, adjt_ref, *refs):
    k_stage(me_ref, *refs[:-1])
    k_halfcomb(me_ref, fb_ref, pg_ref, win_ref, scaled_ref, adjt_ref, refs[-1])


def unpack_small(total):
    small = total.shape[0] // 2
    return jnp.concatenate([total[0:small], total[small:]], axis=1)


def k_sum(own_ref, a_ref, b_ref, c_ref, ein_ref, eout_ref, gco_ref):
    half = ein_ref.shape[0]
    mid = half + 2 * eout_ref.shape[0]
    total = own_ref[...] + a_ref[...].astype(F32) + b_ref[...].astype(F32) + c_ref[...].astype(F32)
    ein_ref[...] = total[0:half]
    eout_ref[...] = unpack_small(total[half:mid])
    gco_ref[...] = unpack_small(total[mid:])


def k_sum_late(own_ref, a_ref, b_ref, c_ref, ein_ref, eout_ref, gin_ref, gout_ref):
    half = ein_ref.shape[0]
    total = own_ref[...] + a_ref[...].astype(F32) + b_ref[...].astype(F32) + c_ref[...].astype(F32)
    gin_ref[0] = total[0:half]
    gin_ref[1] = ein_ref[...]
    gout_ref[0] = unpack_small(total[half:])
    gout_ref[1] = eout_ref[...]


def local(node_features, inward_weight, outward_weight, coarse_weight, tile_index, tile_mask,
          send_rows, parent, cotangent):
    half, n = node_features.shape
    width = 2 * half
    blocks, k_slots = tile_index.shape
    rim = tile_mask.shape[2]
    src_rows = (blocks + 2) * rim
    domains = lax.axis_size(DOM)
    cross = lax.axis_size("cross")
    curve = lax.axis_size("curve")
    cap = n // 16
    nodes = n // 4
    slots = 4 * cap
    hidden = 2 * inward_weight.shape[1]
    scale = float(n * domains) ** -0.5
    me = jnp.stack(
        [lax.axis_index(a) for a in (DOM, "sub", "cross", "curve")] + [jnp.int32(domains)]).astype(I32)
    rows = send_rows[0]
    packed = cross == 2 and curve == 4 and 2 * width == 1024 and hidden == width

    cell_bf, cell_f32 = sds((n, width), BF), sds((n, width), F32)
    rim_a, rim_b = call(k_halo, [sds((rim, half), BF)] * 2, [me], [rows, node_features], "halo")
    rim_a, rim_b = two_way(rim_a, 1), two_way(rim_b, 1, forward=1)
    win2, wout2 = swap(inward_weight), swap(outward_weight)
    x_full = gather(node_features).reshape(width, n)
    (xc, adj, adjt, inv, hott, hot, slot, slott, pick, place, tags, ocount, rsel) = call(
        k_prep,
        [cell_bf, sds((n, src_rows), BF), sds((src_rows, n), BF), sds((n, 128), F32), sds((nodes, n), BF),
         sds((n, nodes), BF), sds((slots, n), BF), sds((n, slots), BF), sds((2 * rim, n), BF),
         sds((n, 2 * rim), BF), sds((16, slots), BF), sds((nodes, 128), F32), sds((cap, width), BF)],
        [tile_index, me], [tile_mask, rows, parent[None, :], x_full], "prep")
    weight_outs = [sds((hidden, 2 * width), BF), sds((width, hidden), BF)]
    win0, wo0 = call(lambda *r: k_weights(0, *r), weight_outs, [me],
                     [inward_weight, outward_weight, win2, wout2], "weights0")
    rim_a, rim_b, win0, adj = lax.optimization_barrier((rim_a, rim_b, win0, adj))
    rims = gather(jnp.concatenate([rim_a, rim_b], axis=0))
    msg = sds((cap + 16, width), BF)
    plain = sds((cap, width), BF)
    hid_bf, hid_f32 = sds((n, hidden), BF), sds((n, hidden), F32)
    agg0, pre0, hid0, first, one, two = call(
        k_first,
        [cell_bf, hid_f32, hid_bf, cell_bf, sds((2 * cap + 16, width), BF), msg],
        [me], [xc, rims, adj, inv, win0, wo0, slot, tags, rsel], "first",
        flops=2 * n * width * (src_rows + 3 * width),
        scratch=[pltpu.VMEM((src_rows, width), BF)])
    one, two, win2, coarse_weight = lax.optimization_barrier((one, two, win2, coarse_weight))
    one, two = two_way(one, 1), two_way(two, 2)
    own, slope0, cw = call(
        k_own, [sds((nodes, width), F32), hid_f32, sds((width, width), BF)], [me],
        [hott, first, pre0, coarse_weight, swap(coarse_weight)], "own")
    win1, wo1 = call(lambda *r: k_weights(1, *r), weight_outs, [me],
                     [inward_weight, outward_weight, win2, wout2], "weights1")
    one, two, own = lax.optimization_barrier((one, two, own))
    got = shared(one, two)
    node_bf, node_f32 = sds((nodes, width), BF), sds((nodes, width), F32)
    hits, icount, coarse, cpre, corr, one, two, rsb, rsa = call(
        k_coarse,
        [sds((nodes, slots), F32), sds((nodes, 128), F32), node_bf, node_f32, node_bf, plain, plain]
        + [sds((slots, rim), BF)] * 2,
        [me], [own, ocount, *got, cw], "coarse")
    one, two, cotangent = lax.optimization_barrier((one, two, cotangent))
    one, two = two_way(one, 1), two_way(two, 2)
    ctc, hg1 = call(k_cot, [cell_bf, hid_f32], [me], [cotangent, swap(cotangent), wo1], "cot")
    one, two, win1 = lax.optimization_barrier((one, two, win1))
    got = shared(one, two)
    lifted, rims = call(
        k_lift, [cell_bf, sds((rim, width), BF)], [me],
        [first, hot, slott, corr, *got, pick], "lift")
    rims, hg1 = lax.optimization_barrier((two_way(rims, 1), hg1))
    rims = shared(rims)
    pair = sds((2 * cap, width), BF)
    agg1, hid1, new, pg1, comb1, near, one, two, three = call(
        k_second,
        [cell_bf, hid_bf, cell_bf, hid_bf, cell_f32, sds((2 * cap, width), F32),
         sds((rim + 2 * cap, width), BF), pair, plain],
        [me], [lifted, *rims, adj, adjt, inv, win1, wo1, hg1, ctc, slot, rsb, rsa], "second",
        scratch=[pltpu.VMEM((src_rows, width), BF)])
    one, two, three = two_way(one, 1), two_way(two, 2), two_way(three, 3)
    piece = 2 * width // domains
    small = hidden // domains
    layer_rows = half + 2 * small
    pack = [sds((curve, layer_rows, piece), F32), sds((curve, layer_rows, piece), BF)]
    if packed:
        new_t, keep1, send1 = call(
            lambda *r: k_newt_pack(scale, *r), [sds((half, n), BF)] + pack, [me],
            [new, pg1, lifted, agg1, ctc, hid1], "grads1")
        got1 = cross_swap(send1)
        one, two, three, keep1 = lax.optimization_barrier((one, two, three, keep1))
    else:
        new_t, = call(k_newt, [sds((half, n), BF)], [me], [new], "new")
    got = shared(one, two, three)
    lg, pgrad, spread, one, two = call(
        k_cgrad, [cell_bf, node_bf, node_bf, plain, plain], [me],
        [comb1, place, hott, near, *got, hits, icount, cpre, cw], "cgrad")
    one, two = two_way(one, 1), two_way(two, 2)
    if packed:
        keepc, sendc = call(
            lambda *r: k_cweight_pack(scale, *r),
            [sds((curve, 2 * small, piece), F32), sds((curve, 2 * small, piece), BF)], [me],
            [pgrad, coarse], "cweight")
        gotc = cross_swap(sendc)
    got = gather(jnp.concatenate([one, two], axis=0))
    back_outs = [cell_bf, hid_bf, cell_bf, sds((rim, width), BF)]
    if packed:
        got, got1 = lax.optimization_barrier((got, got1))
    if packed:
        fb, pg0, scaled0, rims, keep0, send0 = call(
            lambda *r: k_third(*r, scale=scale), back_outs + pack, [me],
            [lg, hot, slott, spread, got, wo0, slope0, win0, inv, adjt, xc, agg0, hid0], "third")
        send0, gotc = lax.optimization_barrier((send0, gotc))
        got0 = cross_swap(send0)
        keepc, pg0 = lax.optimization_barrier((keepc, pg0))
        rims = two_way(rims, 1)

        def staged(body, extra, extra_outs, pairs, name):
            total = sum(keep.shape[1] for keep in pairs[::2])
            own, *outs = call(
                body, [sds((total, piece), F32)] + [sds((total, piece), BF)] * 3 + extra_outs,
                [me], extra + pairs, name)
            return [own] + [curve_swap(value, step) for step, value in zip((1, 2, 3), outs)], outs[3:]

        early, (comb0,) = staged(
            k_stage_comb, [fb, pg0, win0, scaled0, adjt], [sds((n, half), F32)],
            [keep1, got1, keepc, gotc], "stage1")
        late, _ = staged(k_stage, [], [], [keep0, got0], "stage0")
    else:
        gco, = call(lambda *r: k_cweight(scale, *r), [sds((half, width), F32)], [me], [pgrad, coarse], "cweight")
        fb, pg0, scaled0, rims = call(
            k_third, back_outs, [me], [lg, hot, slott, spread, got, wo0, slope0, win0, inv, adjt], "third")
        rims = two_way(rims, 1)
        comb0, = call(k_halfcomb, [sds((n, half), F32)], [me], [fb, pg0, win0, scaled0, adjt], "halfcomb")
    rims = gather(rims)
    if packed:
        fgrad, ein, eout, gco = call(
            k_last, [sds((half, n), F32), sds((half, piece), F32), sds((small, half), F32), sds((small, half), F32)],
            [me], [comb0, rims, place] + early, "last")
        gin, gout = call(
            k_sum_late, [sds((2, half, piece), F32), sds((2, small, half), F32)], [], late + [ein, eout], "late")
        gout = gout.swapaxes(1, 2)
        gco = gco.T
    else:
        fgrad, = call(k_last, [sds((half, n), F32)], [me], [comb0, rims, place], "last")
        shapes = [sds((half, 2 * width), F32), sds((half, hidden), F32)]
        gi1, go1 = call(lambda *r: k_grads(scale, *r), shapes, [me], [pg1, lifted, agg1, ctc, hid1], "grads1")
        gi0, go0 = call(lambda *r: k_grads(scale, *r), shapes, [me], [pg0, xc, agg0, fb, hid0], "grads0")
        gin = lax.psum_scatter(jnp.stack([gi0, gi1]), DOM, scatter_dimension=2, tiled=True)
        gout = lax.psum_scatter(jnp.stack([go0, go1]), DOM, scatter_dimension=2, tiled=True)
        gco = lax.psum_scatter(gco, DOM, scatter_dimension=1, tiled=True)
    return new_t, fgrad, gin, gout, gco


def solution(mesh):
    cells = ("groups", "curve", "cross")
    in_specs = (
        P("sub", cells),
        P(None, "sub", None),
        P(None, "sub", None),
        P("sub", None),
        P(cells, None),
        P(cells, None, None, None),
        P(cells, None, None),
        P(cells),
        P("sub", cells),
    )
    out_specs = (
        P("sub", cells),
        P("sub", cells),
        P("groups", "sub", ("curve", "cross")),
        P("groups", "sub", ("curve", "cross")),
        P(("groups", "sub"), ("curve", "cross")),
    )
    return jax.shard_map(local, mesh=mesh, in_specs=in_specs, out_specs=out_specs, check_vma=False)
```

```python
import jax
import jax.numpy as jnp
from jax import lax
from jax.experimental import pallas as pl
from jax.experimental.pallas import tpu as pltpu
from jax.sharding import PartitionSpec as P

BF = jnp.bfloat16
F32 = jnp.float32
I32 = jnp.int32
DOM = ("curve", "cross")
LINE = ("curve", "cross", "sub")
NN = (((1,), (0,)), ((), ()))
NT = (((1,), (1,)), ((), ()))
TN = (((0,), (0,)), ((), ()))


def dot(a, b, dims=NN):
    return lax.dot_general(a, b, dims, preferred_element_type=F32)


def sds(shape, dtype):
    return jax.ShapeDtypeStruct(shape, dtype)


def call(body, outs, scalars, arrays, name, flops=0, scratch=()):
    scalars, arrays = list(scalars), list(arrays)
    moved = sum(a.size * a.dtype.itemsize for a in arrays) + sum(
        o.size * o.dtype.itemsize for o in outs
    )
    return pl.pallas_call(
        body,
        out_shape=tuple(outs),
        in_specs=[pl.BlockSpec(memory_space=pltpu.SMEM)] * len(scalars)
        + [pl.BlockSpec(memory_space=pltpu.VMEM)] * len(arrays),
        out_specs=tuple(pl.BlockSpec(memory_space=pltpu.VMEM) for _ in outs),
        scratch_shapes=list(scratch),
        compiler_params=pltpu.CompilerParams(vmem_limit_bytes=20 * 2**20),
        cost_estimate=pl.CostEstimate(flops=flops, bytes_accessed=moved, transcendentals=0),
        name=name,
    )(*scalars, *arrays)


def two_way(value, steps, forward=0):
    count = lax.axis_size(DOM)
    back = 1 - forward
    pairs = [(2 * p + forward, 2 * (p + steps) + forward) for p in range(count - steps)]
    pairs += [(2 * p + back, 2 * (p - steps) + back) for p in range(steps, count)]
    pairs += [(2 * p + forward, 2 * p + back) for p in range(count - steps, count)]
    pairs += [(2 * p + back, 2 * p + forward) for p in range(steps)]
    return lax.ppermute(value, LINE, pairs)


def swap(value):
    return lax.ppermute(value, "sub", [(0, 1), (1, 0)])


def gather(value):
    return lax.all_gather(value, "sub", axis=0, tiled=False)


def shared(*values):
    return [v for value in values for v in (value, swap(value))]


def directed(sub, own_ref, other_ref, rows=slice(None)):
    own, other = own_ref[rows, :], other_ref[rows, :]
    return jnp.where(sub == 0, own, other), jnp.where(sub == 0, other, own)


def cross_swap(value):
    return lax.ppermute(value, "cross", [(0, 1), (1, 0)])


def curve_swap(value, step):
    return lax.ppermute(value, "curve", [(z, z ^ step) for z in range(4)])


def sigmoid(v):
    return 1.0 / (1.0 + jnp.exp(-v))


def slope_of(v):
    s = sigmoid(v)
    return s * (1.0 + v * (1.0 - s))


def wide(col, width):
    return jnp.concatenate([col] * (width // col.shape[1]), axis=1)


def join_halves(sub, own_ref, other_ref, out_ref):
    half = own_ref.shape[0]
    out_ref[:, pl.ds(pl.multiple_of(sub * half, half), half)] = own_ref[...].T
    out_ref[:, pl.ds(pl.multiple_of((1 - sub) * half, half), half)] = other_ref[...].T


def k_halo(me_ref, rows_ref, x_ref, a_ref, b_ref):
    half_x = x_ref[...]
    for flip, out_ref in enumerate((a_ref, b_ref)):
        row = jnp.where(me_ref[1] == flip, rows_ref[0:1, :], rows_ref[1:2, :])
        at = lax.broadcasted_iota(I32, (half_x.shape[1], row.shape[1]), 0)
        out_ref[...] = dot(half_x, (at == row).astype(F32).astype(BF)).T.astype(BF)


def k_weights(layer, me_ref, win_ref, wout_ref, win2_ref, wout2_ref, in_ref, out_ref):
    half = win_ref.shape[1]
    own = pl.multiple_of(me_ref[1] * half, half)
    other = pl.multiple_of((1 - me_ref[1]) * half, half)
    in_ref[pl.ds(own, half), :] = win_ref[layer]
    in_ref[pl.ds(other, half), :] = win2_ref[layer]
    out_ref[pl.ds(own, half), :] = wout_ref[layer]
    out_ref[pl.ds(other, half), :] = wout2_ref[layer]


def k_prep(tile_ref, me_ref, mask_ref, rows_ref, par_ref, x_ref, xc_ref,
           adj_ref, adjt_ref, inv_ref, hott_ref, hot_ref, slot_ref, slott_ref,
           pick_ref, place_ref, tags_ref, ocount_ref, rsel_ref):
    blocks, k_slots, length, _ = mask_ref.shape
    n = adj_ref.shape[0]
    nodes = hott_ref.shape[0]
    slots = slot_ref.shape[0]
    cap = slots // 4
    xc_ref[...] = x_ref[...].T
    adj_ref[...] = jnp.zeros(adj_ref.shape, BF)
    adjt_ref[...] = jnp.zeros(adjt_ref.shape, BF)
    for b in range(blocks):
        degree = jnp.zeros((length, 1), F32)
        for k in range(k_slots):
            bits = mask_ref[b, k].astype(F32)
            start = pl.multiple_of(tile_ref[b, k] * length, length)
            adj_ref[b * length:(b + 1) * length, pl.ds(start, length)] = bits.astype(BF)
            adjt_ref[pl.ds(start, length), b * length:(b + 1) * length] = bits.T.astype(BF)
            degree = degree + jnp.sum(bits, axis=1, keepdims=True)
        inv_ref[b * length:(b + 1) * length, :] = jnp.broadcast_to(1.0 / degree, (length, 128))
    rel_row = par_ref[...] - me_ref[0] * nodes
    hott = (lax.broadcasted_iota(I32, (nodes, n), 0) == rel_row).astype(F32)
    hott_ref[...] = hott.astype(BF)
    ocount_ref[...] = jnp.broadcast_to(jnp.sum(hott, axis=1, keepdims=True), (nodes, 128))
    hot_ref[...] = hott.T.astype(BF)
    j = lax.broadcasted_iota(I32, (slots, n), 0)
    off = jnp.where(j < cap, 1, jnp.where(j < 2 * cap, -1, jnp.where(j < 3 * cap, 2, -2)))
    start = jnp.where(j < cap, 0, jnp.where(j < 2 * cap, cap, jnp.where(j < 3 * cap, 2 * cap, 3 * cap)))
    node = rel_row - off * nodes
    chosen = ((node >= 0) & (node < nodes)).astype(F32)
    before = lax.broadcasted_iota(I32, (n, n), 0) < lax.broadcasted_iota(I32, (n, n), 1)
    rank = dot(chosen.astype(BF), before.astype(F32).astype(BF))
    fits = jnp.where(rank == (j - start).astype(F32), chosen, 0.0)
    slot_ref[...] = fits.astype(BF)
    slott_ref[...] = fits.T.astype(BF)
    tags = jnp.sum(fits * (node + 1).astype(F32), axis=1, keepdims=True)
    tags_ref[...] = jnp.broadcast_to(tags, (slots, slots)).T[0:tags_ref.shape[0], :].astype(BF)
    width = rows_ref.shape[1]
    at = lax.broadcasted_iota(I32, (n, width), 0)
    for c in range(2):
        place = (at == rows_ref[c:c + 1, :]).astype(F32)
        place_ref[:, c * width:(c + 1) * width] = place.astype(BF)
        pick_ref[c * width:(c + 1) * width, :] = place.T.astype(BF)
    at = pl.multiple_of(me_ref[1] * width, width)
    sent = dot(slot_ref[...], place_ref[:, pl.ds(at, width)]).astype(BF)
    for c in range(4):
        rsel_ref[:, c * width:(c + 1) * width] = sent[c * cap:(c + 1) * cap]


def forward(xc, src, adj_ref, inv_ref, win_ref, wo_ref):
    width = xc.shape[1]
    agg = (dot(adj_ref[...], src) * wide(inv_ref[...], width)).astype(BF)
    pre = dot(xc, win_ref[:, 0:width], NT) + dot(agg, win_ref[:, width:], NT)
    hid = (pre * sigmoid(pre)).astype(BF)
    out = (xc.astype(F32) + dot(hid, wo_ref[...], NT)).astype(BF)
    return agg, pre, hid, out


def send_slots(sub, values, slot_ref, one_ref, two_ref):
    cap = slot_ref.shape[0] // 4
    a = pl.multiple_of(sub * cap, cap)
    one_ref[0:cap, :] = dot(slot_ref[pl.ds(a, cap), :], values).astype(BF)
    two_ref[0:cap, :] = dot(slot_ref[pl.ds(a + 2 * cap, cap), :], values).astype(BF)


def fill_sources(me_ref, xc, rims, src):
    n = xc.shape[0]
    rim = rims[0].shape[0]
    src[0:n, :] = xc
    for c in range(2):
        rows = slice(n + c * rim, n + (c + 1) * rim)
        there = me_ref[0] >= 1 if c == 0 else me_ref[0] < me_ref[4] - 1

        @pl.when(there)
        def _():
            src[rows, :] = rims[c]

        @pl.when(jnp.logical_not(there))
        def _():
            src[rows, :] = jnp.zeros((rim, xc.shape[1]), BF)


def k_first(me_ref, xc_ref, rims_ref, adj_ref, inv_ref, win_ref, wo_ref,
            slot_ref, tags_ref, rsel_ref,
            agg_ref, pre_ref, hid_ref, first_ref, one_ref, two_ref, src):
    xc = xc_ref[...]
    rim = rims_ref.shape[1] // 2
    before = jnp.concatenate([rims_ref[0, 0:rim], rims_ref[1, rim:]], axis=1)
    after = jnp.concatenate([rims_ref[0, rim:], rims_ref[1, 0:rim]], axis=1)
    fill_sources(me_ref, xc, (before, after), src)
    agg, pre, hid, out = forward(xc, src[...], adj_ref, inv_ref, win_ref, wo_ref)
    agg_ref[...] = agg
    pre_ref[...] = pre
    hid_ref[...] = hid
    first_ref[...] = out
    send_slots(me_ref[1], out, slot_ref, one_ref, two_ref)
    cap = slot_ref.shape[0] // 4
    pad = wide(tags_ref[...], two_ref.shape[1])
    tag_rows = tags_ref.shape[0]
    one_ref[cap:cap + tag_rows, :] = pad
    one_ref[cap + tag_rows:, :] = rsel_ref[...]
    two_ref[cap:, :] = pad


def k_own(me_ref, hott_ref, v_ref, pre_ref, cw_ref, cw2_ref, pick_ref, hot_ref,
          pool_ref, slope_ref, cwf_ref, rim_ref, psel_ref):
    half = cw_ref.shape[0]
    pool_ref[...] = dot(hott_ref[...], v_ref[...])
    rim = rim_ref.shape[0]
    pick = pick_ref[pl.ds(pl.multiple_of(me_ref[1] * rim, rim), rim), :]
    rim_ref[...] = dot(pick, v_ref[...]).astype(BF)
    psel_ref[...] = dot(pick, hot_ref[...]).astype(BF)
    slope_ref[...] = slope_of(pre_ref[...])
    cwf_ref[pl.ds(pl.multiple_of(me_ref[1] * half, half), half), :] = cw_ref[...]
    cwf_ref[pl.ds(pl.multiple_of((1 - me_ref[1]) * half, half), half), :] = cw2_ref[...]


def k_cot(me_ref, ct_ref, ct2_ref, wo_ref, ctc_ref, hg_ref):
    join_halves(me_ref[1], ct_ref, ct2_ref, ctc_ref)
    hg_ref[...] = dot(ctc_ref[...], wo_ref[...])


def arrived_of(sub, got, cap):
    one, one2, two, two2 = got
    rows = slice(0, cap)
    return jnp.concatenate(directed(sub, one, one2, rows) + directed(sub, two, two2, rows), axis=0)


def k_coarse(me_ref, pool_ref, ocount_ref, one_ref, one2_ref, two_ref, two2_ref, cw_ref, rim_ref, psel_ref,
             hits_ref, icount_ref, coarse_ref, cpre_ref, corr_ref, near_ref, out1_ref, out2_ref, out3_ref,
             rsb_ref, rsa_ref):
    nodes, width = pool_ref.shape
    cap = out3_ref.shape[0]
    sub = me_ref[1]
    got = (one_ref, one2_ref, two_ref, two2_ref)
    slots = 4 * cap
    lane = lax.broadcasted_iota(I32, (1, slots), 1)
    row = slice(cap, cap + 1)
    t = directed(sub, one_ref, one2_ref, row) + directed(sub, two_ref, two2_ref, row)
    t = [v[:, 0:slots].astype(F32) for v in t]
    domain, count = me_ref[0], me_ref[4]
    there = (domain >= 1, domain < count - 1, domain >= 2, domain < count - 2)
    t = [jnp.where(ok, v, 0.0) for ok, v in zip(there, t)]
    packed = directed(sub, one_ref, one2_ref, slice(one_ref.shape[0] - cap, one_ref.shape[0]))
    rim = width // 4
    for ok, value, ref in zip(there, packed, (rsb_ref, rsa_ref)):
        value = jnp.where(ok, value.astype(F32), 0.0).astype(BF)
        for c in range(4):
            ref[c * cap:(c + 1) * cap, :] = value[:, c * rim:(c + 1) * rim]
    tags = jnp.where(lane < cap, t[0], jnp.where(lane < 2 * cap, t[1], jnp.where(lane < 3 * cap, t[2], t[3])))
    node = (lax.broadcasted_iota(I32, (nodes, slots), 0) + 1).astype(F32)
    hits = (node == tags).astype(F32)
    count = jnp.maximum(ocount_ref[...] + jnp.sum(hits, axis=1, keepdims=True), 1.0)
    icount = 1.0 / count
    hits_ref[...] = hits
    icount_ref[...] = icount
    hb = hits.astype(BF)
    total = pool_ref[...] + dot(hb, arrived_of(sub, got, cap))
    coarse = (total * wide(icount, width)).astype(BF)
    cpre = dot(coarse, cw_ref[...], NT)
    corr = (cpre * sigmoid(cpre)).astype(BF)
    coarse_ref[...] = coarse
    cpre_ref[...] = cpre
    corr_ref[...] = corr
    ans = dot(hits.T.astype(BF), corr).astype(BF)
    near_ref[...] = ans[0:2 * cap]
    rims = (rim_ref[...].astype(F32) + dot(psel_ref[...], corr)).astype(BF)
    rim_rows = rims.shape[0]
    out1_ref[0:rim_rows, :] = rims
    near = jnp.where(sub == 0, ans[cap:2 * cap], ans[0:cap])
    far = jnp.where(sub == 0, ans[3 * cap:], ans[2 * cap:3 * cap])
    out1_ref[rim_rows:rim_rows + cap, :] = near
    out1_ref[rim_rows + cap:, :] = far
    out2_ref[0:cap, :] = far
    out2_ref[cap:, :] = near
    out3_ref[...] = far


def spread_back(first, hot_ref, slott_ref, corr, one, two):
    returned = jnp.concatenate([one[1], one[0], two[1], two[0]], axis=0)
    total = first.astype(F32) + dot(hot_ref[...], corr) + dot(slott_ref[...], returned)
    return total.astype(BF)


def rim_grads(sub, pg, win_ref, inv_ref, adjt_ref, scaled_ref, msg_ref):
    n = pg.shape[0]
    width = win_ref.shape[1] // 2
    rim = msg_ref.shape[0]
    scaled = (dot(pg, win_ref[:, width:]) * wide(inv_ref[...], width)).astype(BF)
    scaled_ref[...] = scaled
    at = pl.multiple_of(n + (1 - sub) * rim, rim)
    msg_ref[...] = dot(adjt_ref[pl.ds(at, rim), :], scaled).astype(BF)


def k_second(me_ref, first_ref, hot_ref, slott_ref, corr_ref, ans_ref, aone_ref, aone2_ref, atwo_ref, atwo2_ref,
             athree_ref, athree2_ref, adj_ref, adjt_ref, inv_ref, win_ref, wo_ref, hg_ref, g_ref,
             slot_ref, rsb_ref, rsa_ref,
             lift_ref, agg_ref, hid_ref, new_ref, pg_ref, comb_ref, near_ref, one_ref, two_ref, three_ref, src):
    n, width = first_ref.shape
    cap = slot_ref.shape[0] // 4
    sub = me_ref[1]
    rim = aone_ref.shape[0] - 2 * cap

    def answers(own_ref, other_ref, start):
        return directed(sub, own_ref, other_ref, slice(start, start + cap))

    near, far = answers(aone_ref, aone2_ref, rim), answers(atwo_ref, atwo2_ref, 0)
    lifted = spread_back(first_ref[...], hot_ref, slott_ref, corr_ref[...], near, far)
    lift_ref[...] = lifted
    rims = directed(sub, aone_ref, aone2_ref, slice(0, rim))
    across, near_rim = answers(aone_ref, aone2_ref, rim + cap), answers(atwo_ref, atwo2_ref, cap)
    far_rim = answers(athree_ref, athree2_ref, 0)
    of_before = jnp.concatenate([ans_ref[0:cap, :], near_rim[0], across[1], far_rim[0]], axis=0)
    of_after = jnp.concatenate([near_rim[1], ans_ref[cap:, :], far_rim[1], across[0]], axis=0)
    before = (rims[0].astype(F32) + dot(rsb_ref[...].astype(F32).T.astype(BF), of_before)).astype(BF)
    after = (rims[1].astype(F32) + dot(rsa_ref[...].astype(F32).T.astype(BF), of_after)).astype(BF)
    fill_sources(me_ref, lifted, (before, after), src)
    agg, pre, hid, out = forward(lifted, src[...], adj_ref, inv_ref, win_ref, wo_ref)
    agg_ref[...] = agg
    hid_ref[...] = hid
    new_ref[...] = out
    pg = (hg_ref[...] * slope_of(pre)).astype(BF)
    pg_ref[...] = pg
    scaled = (dot(pg, win_ref[:, width:]) * wide(inv_ref[...], width)).astype(BF)
    comb = g_ref[...].astype(F32) + dot(pg, win_ref[:, 0:width]) + dot(adjt_ref[0:n, :], scaled)
    comb_ref[...] = comb
    rims = dot(adjt_ref[n:, :], scaled).astype(BF)
    before, after = rims[0:rim], rims[rim:]
    own = dot(slot_ref[...], comb.astype(BF)).astype(BF)
    of_before, of_after = dot(rsb_ref[...], before), dot(rsa_ref[...], after)
    near_ref[0:cap, :] = of_before[0:cap]
    near_ref[cap:, :] = of_after[cap:2 * cap]
    of_before, of_after = of_before.astype(BF), of_after.astype(BF)

    @pl.when(me_ref[1] == 0)
    def _():
        one_ref[0:rim, :] = after
        one_ref[rim:rim + cap, :] = own[0:cap]
        one_ref[rim + cap:, :] = of_before[2 * cap:3 * cap]
        two_ref[0:cap, :] = own[2 * cap:3 * cap]
        two_ref[cap:, :] = of_after[0:cap]
        three_ref[...] = of_after[2 * cap:3 * cap]

    @pl.when(me_ref[1] == 1)
    def _():
        one_ref[0:rim, :] = before
        one_ref[rim:rim + cap, :] = own[cap:2 * cap]
        one_ref[rim + cap:, :] = of_after[3 * cap:]
        two_ref[0:cap, :] = own[3 * cap:]
        two_ref[cap:, :] = of_before[cap:2 * cap]
        three_ref[...] = of_before[3 * cap:]


def k_newt(me_ref, new_ref, out_ref):
    half = out_ref.shape[0]
    at = pl.multiple_of(me_ref[1] * half, half)
    out_ref[...] = new_ref[:, pl.ds(at, half)].T


def k_grads(scale, me_ref, pg_ref, h_ref, agg_ref, g_ref, hid_ref, gin_ref, gout_ref):
    half = gin_ref.shape[0]
    width = h_ref.shape[1]
    at = pl.multiple_of(me_ref[1] * half, half)
    pgt = pg_ref[:, pl.ds(at, half)].T
    gin_ref[:, 0:width] = dot(pgt, h_ref[...]) * scale
    gin_ref[:, width:] = dot(pgt, agg_ref[...]) * scale
    gt = g_ref[:, pl.ds(at, half)].T
    gout_ref[...] = dot(gt, hid_ref[...]) * scale


def pack_grads(scale, me_ref, pg_ref, h_ref, agg_ref, g_ref, hid_ref, keep_ref, send_ref):
    width = h_ref.shape[1]
    half = width // 2
    piece = keep_ref.shape[2]
    at = pl.multiple_of(me_ref[1] * half, half)
    pgt = pg_ref[:, pl.ds(at, half)].T
    lo = dot(pgt, h_ref[...]) * scale
    hi = dot(pgt, agg_ref[...]) * scale
    out = dot(hid_ref[...].T, g_ref[:, pl.ds(at, half)]) * scale

    def pieces(d):
        src, c = (lo, d * piece) if d * piece < width else (hi, d * piece - width)
        return [(0, src[:, c:c + piece])] + small_pieces(out, d, piece, half)

    place_pieces(me_ref, pieces, keep_ref, send_ref)


def small_pieces(values, d, piece, row):
    small = values.shape[0] // 8
    mine = values[d * small:(d + 1) * small]
    return [
        (row + c * small, mine[:, c * piece:(c + 1) * piece]) for c in range(values.shape[1] // piece)
    ]


def place_pieces(me_ref, pieces, keep_ref, send_ref):
    for d in range(8):
        for row, value in pieces(d):
            rows = slice(row, row + value.shape[0])

            @pl.when(me_ref[2] == d % 2)
            def _():
                keep_ref[d // 2, rows, :] = value

            @pl.when(me_ref[2] != d % 2)
            def _():
                send_ref[d // 2, rows, :] = value.astype(BF)


def k_newt_pack(scale, me_ref, new_ref, pg_ref, h_ref, agg_ref, g_ref, hid_ref, out_ref, keep_ref, send_ref):
    pack_grads(scale, me_ref, pg_ref, h_ref, agg_ref, g_ref, hid_ref, keep_ref, send_ref)
    k_newt(me_ref, new_ref, out_ref)


def k_cweight_pack(scale, me_ref, pgrad_ref, coarse_ref, keep_ref, send_ref):
    half = pgrad_ref.shape[1] // 2
    piece = keep_ref.shape[2]
    at = pl.multiple_of(me_ref[1] * half, half)
    values = dot(coarse_ref[...].T, pgrad_ref[:, pl.ds(at, half)]) * scale
    place_pieces(me_ref, lambda d: small_pieces(values, d, piece, 0), keep_ref, send_ref)


def placed(me_ref, place_ref, before, after):
    rim = before.shape[0]
    from_after = dot(place_ref[:, 0:rim], after)
    from_before = dot(place_ref[:, rim:], before)
    return jnp.where(me_ref[0] < me_ref[4] - 1, from_after, 0.0) + jnp.where(me_ref[0] >= 1, from_before, 0.0)


def k_cgrad(me_ref, comb_ref, place_ref, hott_ref, near_ref, one_ref, one2_ref, two_ref, two2_ref,
            three_ref, three2_ref, hits_ref, icount_ref, cpre_ref, cw_ref,
            lg_ref, pgrad_ref, spread_ref, out1_ref, out2_ref):
    cap = out1_ref.shape[0]
    rim = place_ref.shape[1] // 2
    sub, domain, count = me_ref[1], me_ref[0], me_ref[4]
    hits = hits_ref[...]
    lg = comb_ref[...] + placed(me_ref, place_ref, *directed(sub, one_ref, one2_ref, slice(0, rim)))
    lg = lg.astype(BF)
    lg_ref[...] = lg

    def pieces(own_ref, other_ref, start, there=None):
        both = directed(sub, own_ref, other_ref, slice(start, start + cap))
        both = [v.astype(F32) for v in both]
        if there is None:
            return both
        return [jnp.where(ok, v, 0.0) for ok, v in zip(there, both)]

    near = pieces(one_ref, one2_ref, rim)
    near_rim = pieces(two_ref, two2_ref, cap, (domain >= 2, domain < count - 2))
    far = pieces(two_ref, two2_ref, 0)
    far_rim = pieces(one_ref, one2_ref, rim + cap)
    far_rim3 = pieces(three_ref, three2_ref, 0, (domain >= 3, domain < count - 3))
    arrived = [near[c] + near_rim[c] + near_ref[c * cap:(c + 1) * cap, :] for c in range(2)]
    arrived += [far[c] + far_rim[c] + far_rim3[c] for c in range(2)]
    arrived = jnp.concatenate(arrived, axis=0).astype(BF)
    total = dot(hott_ref[...], lg) + dot(hits.astype(BF), arrived)
    pgrad = (total * slope_of(cpre_ref[...])).astype(BF)
    pgrad_ref[...] = pgrad
    spread = (dot(pgrad, cw_ref[...]) * wide(icount_ref[...], pgrad.shape[1])).astype(BF)
    spread_ref[...] = spread
    ans = dot(hits.T.astype(BF), spread).astype(BF)
    out1_ref[...] = jnp.where(sub == 0, ans[cap:2 * cap], ans[0:cap])
    out2_ref[...] = jnp.where(sub == 0, ans[3 * cap:], ans[2 * cap:3 * cap])


def k_cweight(scale, me_ref, pgrad_ref, coarse_ref, out_ref):
    half = out_ref.shape[0]
    at = pl.multiple_of(me_ref[1] * half, half)
    out_ref[...] = dot(pgrad_ref[:, pl.ds(at, half)].T, coarse_ref[...]) * scale


def k_third(me_ref, lg_ref, hot_ref, slott_ref, spread_ref, got_ref,
            wo_ref, slope_ref, win_ref, inv_ref, adjt_ref, *rest, scale=None):
    fb_ref, pg_ref, scaled_ref, msg_ref = rest if scale is None else rest[3:7]
    cap = got_ref.shape[1] // 2
    fb = spread_back(
        lg_ref[...], hot_ref, slott_ref, spread_ref[...],
        (got_ref[0, 0:cap], got_ref[1, 0:cap]), (got_ref[0, cap:], got_ref[1, cap:]))
    fb_ref[...] = fb
    pg = (dot(fb, wo_ref[...]) * slope_ref[...]).astype(BF)
    pg_ref[...] = pg
    if scale is not None:
        xc_ref, agg_ref, hid_ref = rest[:3]
        pack_grads(scale, me_ref, pg_ref, xc_ref, agg_ref, fb_ref, hid_ref, rest[7], rest[8])
    rim_grads(me_ref[1], pg, win_ref, inv_ref, adjt_ref, scaled_ref, msg_ref)


def k_last(me_ref, comb_ref, rims_ref, place_ref, *rest):
    half = comb_ref.shape[1]
    at = pl.multiple_of(me_ref[1] * half, half)
    total = comb_ref[...] + placed(
        me_ref, place_ref, rims_ref[0, :, pl.ds(at, half)], rims_ref[1, :, pl.ds(at, half)])
    if len(rest) == 1:
        rest[0][...] = total.T
    else:
        rest[4][...] = total.T
        k_sum(*rest[:4], *rest[5:])


def k_halfcomb(me_ref, fb_ref, pg_ref, win_ref, scaled_ref, adjt_ref, comb_ref):
    n, half = comb_ref.shape
    at = pl.multiple_of(me_ref[1] * half, half)
    cols = pl.ds(at, half)
    comb_ref[...] = (
        fb_ref[:, cols].astype(F32)
        + dot(pg_ref[...], win_ref[:, cols])
        + dot(adjt_ref[0:n, :], scaled_ref[:, cols])
    )


def k_stage(me_ref, *refs):
    pairs = (len(refs) - 4) // 2
    own_ref, outs = refs[2 * pairs], refs[2 * pairs + 1:]
    z = me_ref[3]
    row = 0
    for i in range(pairs):
        keep_ref, got_ref = refs[2 * i], refs[2 * i + 1]
        rows = slice(row, row + keep_ref.shape[1])
        own_ref[rows, :] = keep_ref[z] + got_ref[z].astype(F32)
        for step in (1, 2, 3):
            other = z ^ step
            outs[step - 1][rows, :] = (keep_ref[other] + got_ref[other].astype(F32)).astype(BF)
        row += keep_ref.shape[1]


def k_stage_comb(me_ref, fb_ref, pg_ref, win_ref, scaled_ref, adjt_ref, *refs):
    k_stage(me_ref, *refs[:-1])
    k_halfcomb(me_ref, fb_ref, pg_ref, win_ref, scaled_ref, adjt_ref, refs[-1])


def unpack_small(total):
    small = total.shape[0] // 2
    return jnp.concatenate([total[0:small], total[small:]], axis=1)


def k_sum(own_ref, a_ref, b_ref, c_ref, ein_ref, eout_ref, gco_ref):
    half = ein_ref.shape[0]
    mid = half + 2 * eout_ref.shape[0]
    total = own_ref[...] + a_ref[...].astype(F32) + b_ref[...].astype(F32) + c_ref[...].astype(F32)
    ein_ref[...] = total[0:half]
    eout_ref[...] = unpack_small(total[half:mid])
    gco_ref[...] = unpack_small(total[mid:])


def k_sum_late(own_ref, a_ref, b_ref, c_ref, ein_ref, eout_ref, gin_ref, gout_ref):
    half = ein_ref.shape[0]
    total = own_ref[...] + a_ref[...].astype(F32) + b_ref[...].astype(F32) + c_ref[...].astype(F32)
    gin_ref[0] = total[0:half]
    gin_ref[1] = ein_ref[...]
    gout_ref[0] = unpack_small(total[half:])
    gout_ref[1] = eout_ref[...]


def local(node_features, inward_weight, outward_weight, coarse_weight, tile_index, tile_mask,
          send_rows, parent, cotangent):
    half, n = node_features.shape
    width = 2 * half
    blocks, k_slots = tile_index.shape
    rim = tile_mask.shape[2]
    src_rows = (blocks + 2) * rim
    domains = lax.axis_size(DOM)
    cross = lax.axis_size("cross")
    curve = lax.axis_size("curve")
    cap = n // 16
    nodes = n // 4
    slots = 4 * cap
    hidden = 2 * inward_weight.shape[1]
    scale = float(n * domains) ** -0.5
    me = jnp.stack(
        [lax.axis_index(a) for a in (DOM, "sub", "cross", "curve")] + [jnp.int32(domains)]).astype(I32)
    rows = send_rows[0]
    packed = cross == 2 and curve == 4 and 2 * width == 1024 and hidden == width

    cell_bf, cell_f32 = sds((n, width), BF), sds((n, width), F32)
    rim_a, rim_b = call(k_halo, [sds((rim, half), BF)] * 2, [me], [rows, node_features], "halo")
    rim_a, rim_b = two_way(rim_a, 1), two_way(rim_b, 1, forward=1)
    win2, wout2 = swap(inward_weight), swap(outward_weight)
    x_full = gather(node_features).reshape(width, n)
    (xc, adj, adjt, inv, hott, hot, slot, slott, pick, place, tags, ocount, rsel) = call(
        k_prep,
        [cell_bf, sds((n, src_rows), BF), sds((src_rows, n), BF), sds((n, 128), F32), sds((nodes, n), BF),
         sds((n, nodes), BF), sds((slots, n), BF), sds((n, slots), BF), sds((2 * rim, n), BF),
         sds((n, 2 * rim), BF), sds((16, slots), BF), sds((nodes, 128), F32), sds((cap, width), BF)],
        [tile_index, me], [tile_mask, rows, parent[None, :], x_full], "prep")
    weight_outs = [sds((hidden, 2 * width), BF), sds((width, hidden), BF)]
    win0, wo0 = call(lambda *r: k_weights(0, *r), weight_outs, [me],
                     [inward_weight, outward_weight, win2, wout2], "weights0")
    rim_a, rim_b, win0, adj = lax.optimization_barrier((rim_a, rim_b, win0, adj))
    rims = gather(jnp.concatenate([rim_a, rim_b], axis=0))
    msg = sds((cap + 16, width), BF)
    plain = sds((cap, width), BF)
    hid_bf, hid_f32 = sds((n, hidden), BF), sds((n, hidden), F32)
    agg0, pre0, hid0, first, one, two = call(
        k_first,
        [cell_bf, hid_f32, hid_bf, cell_bf, sds((2 * cap + 16, width), BF), msg],
        [me], [xc, rims, adj, inv, win0, wo0, slot, tags, rsel], "first",
        flops=2 * n * width * (src_rows + 3 * width),
        scratch=[pltpu.VMEM((src_rows, width), BF)])
    one, two, win2, coarse_weight = lax.optimization_barrier((one, two, win2, coarse_weight))
    one, two = two_way(one, 1), two_way(two, 2)
    rim_bf = sds((rim, width), BF)
    own, slope0, cw, rims, psel = call(
        k_own, [sds((nodes, width), F32), hid_f32, sds((width, width), BF), rim_bf, sds((rim, nodes), BF)], [me],
        [hott, first, pre0, coarse_weight, swap(coarse_weight), pick, hot], "own")
    win1, wo1 = call(lambda *r: k_weights(1, *r), weight_outs, [me],
                     [inward_weight, outward_weight, win2, wout2], "weights1")
    one, two, own = lax.optimization_barrier((one, two, own))
    got = shared(one, two)
    node_bf, node_f32 = sds((nodes, width), BF), sds((nodes, width), F32)
    pair, rim_msg = sds((2 * cap, width), BF), sds((rim + 2 * cap, width), BF)
    hits, icount, coarse, cpre, corr, near, one, two, three, rsb, rsa = call(
        k_coarse,
        [sds((nodes, slots), F32), sds((nodes, 128), F32), node_bf, node_f32, node_bf, pair, rim_msg, pair, plain]
        + [sds((slots, rim), BF)] * 2,
        [me], [own, ocount, *got, cw, rims, psel], "coarse")
    one, two, three, cotangent = lax.optimization_barrier((one, two, three, cotangent))
    one, two, three = two_way(one, 1), two_way(two, 2), two_way(three, 3)
    ctc, hg1 = call(k_cot, [cell_bf, hid_f32], [me], [cotangent, swap(cotangent), wo1], "cot")
    one, two, three, win1, hg1 = lax.optimization_barrier((one, two, three, win1, hg1))
    got = shared(one, two, three)
    lifted, agg1, hid1, new, pg1, comb1, near, one, two, three = call(
        k_second,
        [cell_bf, cell_bf, hid_bf, cell_bf, hid_bf, cell_f32, sds((2 * cap, width), F32), rim_msg, pair, plain],
        [me],
        [first, hot, slott, corr, near, *got, adj, adjt, inv, win1, wo1, hg1, ctc, slot, rsb, rsa], "second",
        scratch=[pltpu.VMEM((src_rows, width), BF)])
    one, two, three = two_way(one, 1), two_way(two, 2), two_way(three, 3)
    piece = 2 * width // domains
    small = hidden // domains
    layer_rows = half + 2 * small
    pack = [sds((curve, layer_rows, piece), F32), sds((curve, layer_rows, piece), BF)]
    if packed:
        new_t, keep1, send1 = call(
            lambda *r: k_newt_pack(scale, *r), [sds((half, n), BF)] + pack, [me],
            [new, pg1, lifted, agg1, ctc, hid1], "grads1")
        got1 = cross_swap(send1)
        one, two, three, keep1 = lax.optimization_barrier((one, two, three, keep1))
    else:
        new_t, = call(k_newt, [sds((half, n), BF)], [me], [new], "new")
    got = shared(one, two, three)
    lg, pgrad, spread, one, two = call(
        k_cgrad, [cell_bf, node_bf, node_bf, plain, plain], [me],
        [comb1, place, hott, near, *got, hits, icount, cpre, cw], "cgrad")
    one, two = two_way(one, 1), two_way(two, 2)
    if packed:
        keepc, sendc = call(
            lambda *r: k_cweight_pack(scale, *r),
            [sds((curve, 2 * small, piece), F32), sds((curve, 2 * small, piece), BF)], [me],
            [pgrad, coarse], "cweight")
        gotc = cross_swap(sendc)
    got = gather(jnp.concatenate([one, two], axis=0))
    back_outs = [cell_bf, hid_bf, cell_bf, sds((rim, width), BF)]
    if packed:
        got, got1 = lax.optimization_barrier((got, got1))
    if packed:
        fb, pg0, scaled0, rims, keep0, send0 = call(
            lambda *r: k_third(*r, scale=scale), back_outs + pack, [me],
            [lg, hot, slott, spread, got, wo0, slope0, win0, inv, adjt, xc, agg0, hid0], "third")
        send0, gotc = lax.optimization_barrier((send0, gotc))
        got0 = cross_swap(send0)
        keepc, pg0 = lax.optimization_barrier((keepc, pg0))
        rims = two_way(rims, 1)

        def staged(body, extra, extra_outs, pairs, name):
            total = sum(keep.shape[1] for keep in pairs[::2])
            own, *outs = call(
                body, [sds((total, piece), F32)] + [sds((total, piece), BF)] * 3 + extra_outs,
                [me], extra + pairs, name)
            return [own] + [curve_swap(value, step) for step, value in zip((1, 2, 3), outs)], outs[3:]

        early, (comb0,) = staged(
            k_stage_comb, [fb, pg0, win0, scaled0, adjt], [sds((n, half), F32)],
            [keep1, got1, keepc, gotc], "stage1")
        late, _ = staged(k_stage, [], [], [keep0, got0], "stage0")
    else:
        gco, = call(lambda *r: k_cweight(scale, *r), [sds((half, width), F32)], [me], [pgrad, coarse], "cweight")
        fb, pg0, scaled0, rims = call(
            k_third, back_outs, [me], [lg, hot, slott, spread, got, wo0, slope0, win0, inv, adjt], "third")
        rims = two_way(rims, 1)
        comb0, = call(k_halfcomb, [sds((n, half), F32)], [me], [fb, pg0, win0, scaled0, adjt], "halfcomb")
    rims = gather(rims)
    if packed:
        fgrad, ein, eout, gco = call(
            k_last, [sds((half, n), F32), sds((half, piece), F32), sds((small, half), F32), sds((small, half), F32)],
            [me], [comb0, rims, place] + early, "last")
        gin, gout = call(
            k_sum_late, [sds((2, half, piece), F32), sds((2, small, half), F32)], [], late + [ein, eout], "late")
        gout = gout.swapaxes(1, 2)
        gco = gco.T
    else:
        fgrad, = call(k_last, [sds((half, n), F32)], [me], [comb0, rims, place], "last")
        shapes = [sds((half, 2 * width), F32), sds((half, hidden), F32)]
        gi1, go1 = call(lambda *r: k_grads(scale, *r), shapes, [me], [pg1, lifted, agg1, ctc, hid1], "grads1")
        gi0, go0 = call(lambda *r: k_grads(scale, *r), shapes, [me], [pg0, xc, agg0, fb, hid0], "grads0")
        gin = lax.psum_scatter(jnp.stack([gi0, gi1]), DOM, scatter_dimension=2, tiled=True)
        gout = lax.psum_scatter(jnp.stack([go0, go1]), DOM, scatter_dimension=2, tiled=True)
        gco = lax.psum_scatter(gco, DOM, scatter_dimension=1, tiled=True)
    return new_t, fgrad, gin, gout, gco


def solution(mesh):
    cells = ("groups", "curve", "cross")
    in_specs = (
        P("sub", cells),
        P(None, "sub", None),
        P(None, "sub", None),
        P("sub", None),
        P(cells, None),
        P(cells, None, None, None),
        P(cells, None, None),
        P(cells),
        P("sub", cells),
    )
    out_specs = (
        P("sub", cells),
        P("sub", cells),
        P("groups", "sub", ("curve", "cross")),
        P("groups", "sub", ("curve", "cross")),
        P(("groups", "sub"), ("curve", "cross")),
    )
    return jax.shard_map(local, mesh=mesh, in_specs=in_specs, out_specs=out_specs, check_vma=False)
```

```python
import jax
import jax.numpy as jnp
from jax import lax
from jax.experimental import pallas as pl
from jax.experimental.pallas import tpu as pltpu
from jax.sharding import PartitionSpec as P

BF = jnp.bfloat16
F32 = jnp.float32
I32 = jnp.int32
DOM = ("curve", "cross")
LINE = ("curve", "cross", "sub")
NN = (((1,), (0,)), ((), ()))
NT = (((1,), (1,)), ((), ()))
TN = (((0,), (0,)), ((), ()))


def dot(a, b, dims=NN):
    return lax.dot_general(a, b, dims, preferred_element_type=F32)


def sds(shape, dtype):
    return jax.ShapeDtypeStruct(shape, dtype)


def call(body, outs, scalars, arrays, name, flops=0, scratch=()):
    scalars, arrays = list(scalars), list(arrays)
    moved = sum(a.size * a.dtype.itemsize for a in arrays) + sum(
        o.size * o.dtype.itemsize for o in outs
    )
    return pl.pallas_call(
        body,
        out_shape=tuple(outs),
        in_specs=[pl.BlockSpec(memory_space=pltpu.SMEM)] * len(scalars)
        + [pl.BlockSpec(memory_space=pltpu.VMEM)] * len(arrays),
        out_specs=tuple(pl.BlockSpec(memory_space=pltpu.VMEM) for _ in outs),
        scratch_shapes=list(scratch),
        compiler_params=pltpu.CompilerParams(vmem_limit_bytes=20 * 2**20),
        cost_estimate=pl.CostEstimate(flops=flops, bytes_accessed=moved, transcendentals=0),
        name=name,
    )(*scalars, *arrays)


def two_way(value, steps, forward=0):
    count = lax.axis_size(DOM)
    back = 1 - forward
    pairs = [(2 * p + forward, 2 * (p + steps) + forward) for p in range(count - steps)]
    pairs += [(2 * p + back, 2 * (p - steps) + back) for p in range(steps, count)]
    pairs += [(2 * p + forward, 2 * p + back) for p in range(count - steps, count)]
    pairs += [(2 * p + back, 2 * p + forward) for p in range(steps)]
    return lax.ppermute(value, LINE, pairs)


def swap(value):
    return lax.ppermute(value, "sub", [(0, 1), (1, 0)])


def gather(value):
    return lax.all_gather(value, "sub", axis=0, tiled=False)


def shared(*values):
    return [v for value in values for v in (value, swap(value))]


def directed(sub, own_ref, other_ref, rows=slice(None)):
    own, other = own_ref[rows, :], other_ref[rows, :]
    return jnp.where(sub == 0, own, other), jnp.where(sub == 0, other, own)


def cross_swap(value):
    return lax.ppermute(value, "cross", [(0, 1), (1, 0)])


def curve_swap(value, step):
    return lax.ppermute(value, "curve", [(z, z ^ step) for z in range(4)])


def sigmoid(v):
    return 1.0 / (1.0 + jnp.exp(-v))


def slope_of(v):
    s = sigmoid(v)
    return s * (1.0 + v * (1.0 - s))


def wide(col, width):
    return jnp.concatenate([col] * (width // col.shape[1]), axis=1)


def join_halves(sub, own_ref, other_ref, out_ref):
    half = own_ref.shape[0]
    out_ref[:, pl.ds(pl.multiple_of(sub * half, half), half)] = own_ref[...].T
    out_ref[:, pl.ds(pl.multiple_of((1 - sub) * half, half), half)] = other_ref[...].T


def k_halo(me_ref, rows_ref, x_ref, a_ref, b_ref):
    half_x = x_ref[...]
    for flip, out_ref in enumerate((a_ref, b_ref)):
        row = jnp.where(me_ref[1] == flip, rows_ref[0:1, :], rows_ref[1:2, :])
        at = lax.broadcasted_iota(I32, (half_x.shape[1], row.shape[1]), 0)
        out_ref[...] = dot(half_x, (at == row).astype(F32).astype(BF)).T.astype(BF)


def k_weights(layer, me_ref, win_ref, wout_ref, win2_ref, wout2_ref, in_ref, out_ref):
    half = win_ref.shape[1]
    own = pl.multiple_of(me_ref[1] * half, half)
    other = pl.multiple_of((1 - me_ref[1]) * half, half)
    in_ref[pl.ds(own, half), :] = win_ref[layer]
    in_ref[pl.ds(other, half), :] = win2_ref[layer]
    out_ref[pl.ds(own, half), :] = wout_ref[layer]
    out_ref[pl.ds(other, half), :] = wout2_ref[layer]


def k_prep(tile_ref, me_ref, mask_ref, rows_ref, par_ref, x_ref, xc_ref,
           adj_ref, adjt_ref, inv_ref, hott_ref, hot_ref, slot_ref, slott_ref,
           pick_ref, place_ref, tags_ref, ocount_ref, rsel_ref):
    blocks, k_slots, length, _ = mask_ref.shape
    n = adj_ref.shape[0]
    nodes = hott_ref.shape[0]
    slots = slot_ref.shape[0]
    cap = slots // 4
    xc_ref[...] = x_ref[...].T
    adj_ref[...] = jnp.zeros(adj_ref.shape, BF)
    adjt_ref[...] = jnp.zeros(adjt_ref.shape, BF)
    for b in range(blocks):
        degree = jnp.zeros((length, 1), F32)
        for k in range(k_slots):
            bits = mask_ref[b, k].astype(F32)
            start = pl.multiple_of(tile_ref[b, k] * length, length)
            adj_ref[b * length:(b + 1) * length, pl.ds(start, length)] = bits.astype(BF)
            adjt_ref[pl.ds(start, length), b * length:(b + 1) * length] = bits.T.astype(BF)
            degree = degree + jnp.sum(bits, axis=1, keepdims=True)
        inv_ref[b * length:(b + 1) * length, :] = jnp.broadcast_to(1.0 / degree, (length, 128))
    rel_row = par_ref[...] - me_ref[0] * nodes
    hott = (lax.broadcasted_iota(I32, (nodes, n), 0) == rel_row).astype(F32)
    hott_ref[...] = hott.astype(BF)
    ocount_ref[...] = jnp.broadcast_to(jnp.sum(hott, axis=1, keepdims=True), (nodes, 128))
    hot_ref[...] = hott.T.astype(BF)
    j = lax.broadcasted_iota(I32, (slots, n), 0)
    off = jnp.where(j < cap, 1, jnp.where(j < 2 * cap, -1, jnp.where(j < 3 * cap, 2, -2)))
    start = jnp.where(j < cap, 0, jnp.where(j < 2 * cap, cap, jnp.where(j < 3 * cap, 2 * cap, 3 * cap)))
    node = rel_row - off * nodes
    chosen = ((node >= 0) & (node < nodes)).astype(F32)
    before = lax.broadcasted_iota(I32, (n, n), 0) < lax.broadcasted_iota(I32, (n, n), 1)
    rank = dot(chosen.astype(BF), before.astype(F32).astype(BF))
    fits = jnp.where(rank == (j - start).astype(F32), chosen, 0.0)
    slot_ref[...] = fits.astype(BF)
    slott_ref[...] = fits.T.astype(BF)
    tags = jnp.sum(fits * (node + 1).astype(F32), axis=1, keepdims=True)
    tags_ref[...] = jnp.broadcast_to(tags, (slots, slots)).T[0:tags_ref.shape[0], :].astype(BF)
    width = rows_ref.shape[1]
    at = lax.broadcasted_iota(I32, (n, width), 0)
    for c in range(2):
        place = (at == rows_ref[c:c + 1, :]).astype(F32)
        place_ref[:, c * width:(c + 1) * width] = place.astype(BF)
        pick_ref[c * width:(c + 1) * width, :] = place.T.astype(BF)
    at = pl.multiple_of(me_ref[1] * width, width)
    sent = dot(slot_ref[...], place_ref[:, pl.ds(at, width)]).astype(BF)
    for c in range(4):
        rsel_ref[:, c * width:(c + 1) * width] = sent[c * cap:(c + 1) * cap]


def forward(xc, src, adj_ref, inv_ref, win_ref, wo_ref):
    width = xc.shape[1]
    agg = (dot(adj_ref[...], src) * wide(inv_ref[...], width)).astype(BF)
    pre = dot(xc, win_ref[:, 0:width], NT) + dot(agg, win_ref[:, width:], NT)
    hid = (pre * sigmoid(pre)).astype(BF)
    out = (xc.astype(F32) + dot(hid, wo_ref[...], NT)).astype(BF)
    return agg, pre, hid, out


def send_slots(sub, values, slot_ref, one_ref, two_ref):
    cap = slot_ref.shape[0] // 4
    a = pl.multiple_of(sub * cap, cap)
    one_ref[0:cap, :] = dot(slot_ref[pl.ds(a, cap), :], values).astype(BF)
    two_ref[0:cap, :] = dot(slot_ref[pl.ds(a + 2 * cap, cap), :], values).astype(BF)


def fill_sources(me_ref, xc, rims, src):
    n = xc.shape[0]
    rim = rims[0].shape[0]
    src[0:n, :] = xc
    for c in range(2):
        rows = slice(n + c * rim, n + (c + 1) * rim)
        there = me_ref[0] >= 1 if c == 0 else me_ref[0] < me_ref[4] - 1

        @pl.when(there)
        def _():
            src[rows, :] = rims[c]

        @pl.when(jnp.logical_not(there))
        def _():
            src[rows, :] = jnp.zeros((rim, xc.shape[1]), BF)


def k_first(me_ref, xc_ref, a_ref, a2_ref, b_ref, b2_ref, adj_ref, inv_ref, win_ref, wo_ref,
            slot_ref, tags_ref, rsel_ref,
            agg_ref, pre_ref, hid_ref, first_ref, one_ref, two_ref, src):
    xc = xc_ref[...]
    (before0, after1), (after0, before1) = directed(me_ref[1], a_ref, a2_ref), directed(me_ref[1], b_ref, b2_ref)
    before = jnp.concatenate([before0, before1], axis=1)
    after = jnp.concatenate([after0, after1], axis=1)
    fill_sources(me_ref, xc, (before, after), src)
    agg, pre, hid, out = forward(xc, src[...], adj_ref, inv_ref, win_ref, wo_ref)
    agg_ref[...] = agg
    pre_ref[...] = pre
    hid_ref[...] = hid
    first_ref[...] = out
    send_slots(me_ref[1], out, slot_ref, one_ref, two_ref)
    cap = slot_ref.shape[0] // 4
    pad = wide(tags_ref[...], two_ref.shape[1])
    tag_rows = tags_ref.shape[0]
    one_ref[cap:cap + tag_rows, :] = pad
    one_ref[cap + tag_rows:, :] = rsel_ref[...]
    two_ref[cap:, :] = pad


def k_own(me_ref, hott_ref, v_ref, pre_ref, cw_ref, cw2_ref, pick_ref, hot_ref,
          pool_ref, slope_ref, cwf_ref, rim_ref, psel_ref):
    half = cw_ref.shape[0]
    pool_ref[...] = dot(hott_ref[...], v_ref[...])
    rim = rim_ref.shape[0]
    pick = pick_ref[pl.ds(pl.multiple_of(me_ref[1] * rim, rim), rim), :]
    rim_ref[...] = dot(pick, v_ref[...]).astype(BF)
    psel_ref[...] = dot(pick, hot_ref[...]).astype(BF)
    slope_ref[...] = slope_of(pre_ref[...])
    cwf_ref[pl.ds(pl.multiple_of(me_ref[1] * half, half), half), :] = cw_ref[...]
    cwf_ref[pl.ds(pl.multiple_of((1 - me_ref[1]) * half, half), half), :] = cw2_ref[...]


def k_cot(me_ref, ct_ref, ct2_ref, wo_ref, ctc_ref, hg_ref):
    join_halves(me_ref[1], ct_ref, ct2_ref, ctc_ref)
    hg_ref[...] = dot(ctc_ref[...], wo_ref[...])


def arrived_of(sub, got, cap):
    one, one2, two, two2 = got
    rows = slice(0, cap)
    return jnp.concatenate(directed(sub, one, one2, rows) + directed(sub, two, two2, rows), axis=0)


def k_coarse(me_ref, pool_ref, ocount_ref, one_ref, one2_ref, two_ref, two2_ref, cw_ref, rim_ref, psel_ref,
             hits_ref, icount_ref, coarse_ref, cpre_ref, corr_ref, near_ref, out1_ref, out2_ref, out3_ref,
             rsb_ref, rsa_ref):
    nodes, width = pool_ref.shape
    cap = out3_ref.shape[0]
    sub = me_ref[1]
    got = (one_ref, one2_ref, two_ref, two2_ref)
    slots = 4 * cap
    lane = lax.broadcasted_iota(I32, (1, slots), 1)
    row = slice(cap, cap + 1)
    t = directed(sub, one_ref, one2_ref, row) + directed(sub, two_ref, two2_ref, row)
    t = [v[:, 0:slots].astype(F32) for v in t]
    domain, count = me_ref[0], me_ref[4]
    there = (domain >= 1, domain < count - 1, domain >= 2, domain < count - 2)
    t = [jnp.where(ok, v, 0.0) for ok, v in zip(there, t)]
    packed = directed(sub, one_ref, one2_ref, slice(one_ref.shape[0] - cap, one_ref.shape[0]))
    rim = width // 4
    for ok, value, ref in zip(there, packed, (rsb_ref, rsa_ref)):
        value = jnp.where(ok, value.astype(F32), 0.0).astype(BF)
        for c in range(4):
            ref[c * cap:(c + 1) * cap, :] = value[:, c * rim:(c + 1) * rim]
    tags = jnp.where(lane < cap, t[0], jnp.where(lane < 2 * cap, t[1], jnp.where(lane < 3 * cap, t[2], t[3])))
    node = (lax.broadcasted_iota(I32, (nodes, slots), 0) + 1).astype(F32)
    hits = (node == tags).astype(F32)
    count = jnp.maximum(ocount_ref[...] + jnp.sum(hits, axis=1, keepdims=True), 1.0)
    icount = 1.0 / count
    hits_ref[...] = hits
    icount_ref[...] = icount
    hb = hits.astype(BF)
    total = pool_ref[...] + dot(hb, arrived_of(sub, got, cap))
    coarse = (total * wide(icount, width)).astype(BF)
    cpre = dot(coarse, cw_ref[...], NT)
    corr = (cpre * sigmoid(cpre)).astype(BF)
    coarse_ref[...] = coarse
    cpre_ref[...] = cpre
    corr_ref[...] = corr
    ans = dot(hits.T.astype(BF), corr).astype(BF)
    near_ref[...] = ans[0:2 * cap]
    rims = (rim_ref[...].astype(F32) + dot(psel_ref[...], corr)).astype(BF)
    rim_rows = rims.shape[0]
    out1_ref[0:rim_rows, :] = rims
    near = jnp.where(sub == 0, ans[cap:2 * cap], ans[0:cap])
    far = jnp.where(sub == 0, ans[3 * cap:], ans[2 * cap:3 * cap])
    out1_ref[rim_rows:rim_rows + cap, :] = near
    out1_ref[rim_rows + cap:, :] = far
    out2_ref[0:cap, :] = far
    out2_ref[cap:, :] = near
    out3_ref[...] = far


def spread_back(first, hot_ref, slott_ref, corr, one, two):
    returned = jnp.concatenate([one[1], one[0], two[1], two[0]], axis=0)
    total = first.astype(F32) + dot(hot_ref[...], corr) + dot(slott_ref[...], returned)
    return total.astype(BF)


def rim_grads(sub, pg, win_ref, inv_ref, adjt_ref, scaled_ref, msg_ref):
    n = pg.shape[0]
    width = win_ref.shape[1] // 2
    rim = msg_ref.shape[0]
    scaled = (dot(pg, win_ref[:, width:]) * wide(inv_ref[...], width)).astype(BF)
    scaled_ref[...] = scaled
    at = pl.multiple_of(n + (1 - sub) * rim, rim)
    msg_ref[...] = dot(adjt_ref[pl.ds(at, rim), :], scaled).astype(BF)


def k_second(me_ref, first_ref, hot_ref, slott_ref, corr_ref, ans_ref, aone_ref, aone2_ref, atwo_ref, atwo2_ref,
             athree_ref, athree2_ref, adj_ref, adjt_ref, inv_ref, win_ref, wo_ref, hg_ref, g_ref,
             slot_ref, rsb_ref, rsa_ref,
             lift_ref, agg_ref, hid_ref, new_ref, pg_ref, comb_ref, near_ref, one_ref, two_ref, three_ref, src):
    n, width = first_ref.shape
    cap = slot_ref.shape[0] // 4
    sub = me_ref[1]
    rim = aone_ref.shape[0] - 2 * cap

    def answers(own_ref, other_ref, start):
        return directed(sub, own_ref, other_ref, slice(start, start + cap))

    near, far = answers(aone_ref, aone2_ref, rim), answers(atwo_ref, atwo2_ref, 0)
    lifted = spread_back(first_ref[...], hot_ref, slott_ref, corr_ref[...], near, far)
    lift_ref[...] = lifted
    rims = directed(sub, aone_ref, aone2_ref, slice(0, rim))
    across, near_rim = answers(aone_ref, aone2_ref, rim + cap), answers(atwo_ref, atwo2_ref, cap)
    far_rim = answers(athree_ref, athree2_ref, 0)
    of_before = jnp.concatenate([ans_ref[0:cap, :], near_rim[0], across[1], far_rim[0]], axis=0)
    of_after = jnp.concatenate([near_rim[1], ans_ref[cap:, :], far_rim[1], across[0]], axis=0)
    before = (rims[0].astype(F32) + dot(rsb_ref[...].astype(F32).T.astype(BF), of_before)).astype(BF)
    after = (rims[1].astype(F32) + dot(rsa_ref[...].astype(F32).T.astype(BF), of_after)).astype(BF)
    fill_sources(me_ref, lifted, (before, after), src)
    agg, pre, hid, out = forward(lifted, src[...], adj_ref, inv_ref, win_ref, wo_ref)
    agg_ref[...] = agg
    hid_ref[...] = hid
    new_ref[...] = out
    pg = (hg_ref[...] * slope_of(pre)).astype(BF)
    pg_ref[...] = pg
    scaled = (dot(pg, win_ref[:, width:]) * wide(inv_ref[...], width)).astype(BF)
    comb = g_ref[...].astype(F32) + dot(pg, win_ref[:, 0:width]) + dot(adjt_ref[0:n, :], scaled)
    comb_ref[...] = comb
    rims = dot(adjt_ref[n:, :], scaled).astype(BF)
    before, after = rims[0:rim], rims[rim:]
    own = dot(slot_ref[...], comb.astype(BF)).astype(BF)
    of_before, of_after = dot(rsb_ref[...], before), dot(rsa_ref[...], after)
    near_ref[0:cap, :] = of_before[0:cap]
    near_ref[cap:, :] = of_after[cap:2 * cap]
    of_before, of_after = of_before.astype(BF), of_after.astype(BF)

    @pl.when(me_ref[1] == 0)
    def _():
        one_ref[0:rim, :] = after
        one_ref[rim:rim + cap, :] = own[0:cap]
        one_ref[rim + cap:, :] = of_before[2 * cap:3 * cap]
        two_ref[0:cap, :] = own[2 * cap:3 * cap]
        two_ref[cap:, :] = of_after[0:cap]
        three_ref[...] = of_after[2 * cap:3 * cap]

    @pl.when(me_ref[1] == 1)
    def _():
        one_ref[0:rim, :] = before
        one_ref[rim:rim + cap, :] = own[cap:2 * cap]
        one_ref[rim + cap:, :] = of_after[3 * cap:]
        two_ref[0:cap, :] = own[3 * cap:]
        two_ref[cap:, :] = of_before[cap:2 * cap]
        three_ref[...] = of_before[3 * cap:]


def k_grads(scale, me_ref, pg_ref, h_ref, agg_ref, g_ref, hid_ref, gin_ref, gout_ref):
    half = gin_ref.shape[0]
    width = h_ref.shape[1]
    at = pl.multiple_of(me_ref[1] * half, half)
    pgt = pg_ref[:, pl.ds(at, half)].T
    gin_ref[:, 0:width] = dot(pgt, h_ref[...]) * scale
    gin_ref[:, width:] = dot(pgt, agg_ref[...]) * scale
    gt = g_ref[:, pl.ds(at, half)].T
    gout_ref[...] = dot(gt, hid_ref[...]) * scale


def pack_grads(scale, me_ref, pg_ref, h_ref, agg_ref, g_ref, hid_ref, keep_ref, send_ref):
    width = h_ref.shape[1]
    half = width // 2
    piece = keep_ref.shape[2]
    at = pl.multiple_of(me_ref[1] * half, half)
    pgt = pg_ref[:, pl.ds(at, half)].T
    lo = dot(pgt, h_ref[...]) * scale
    hi = dot(pgt, agg_ref[...]) * scale
    out = dot(hid_ref[...].T, g_ref[:, pl.ds(at, half)]) * scale

    def pieces(d):
        src, c = (lo, d * piece) if d * piece < width else (hi, d * piece - width)
        return [(0, src[:, c:c + piece])] + small_pieces(out, d, piece, half)

    place_pieces(me_ref, pieces, keep_ref, send_ref)


def small_pieces(values, d, piece, row):
    small = values.shape[0] // 8
    mine = values[d * small:(d + 1) * small]
    return [
        (row + c * small, mine[:, c * piece:(c + 1) * piece]) for c in range(values.shape[1] // piece)
    ]


def place_pieces(me_ref, pieces, keep_ref, send_ref):
    for d in range(8):
        for row, value in pieces(d):
            rows = slice(row, row + value.shape[0])

            @pl.when(me_ref[2] == d % 2)
            def _():
                keep_ref[d // 2, rows, :] = value

            @pl.when(me_ref[2] != d % 2)
            def _():
                send_ref[d // 2, rows, :] = value.astype(BF)


def k_cweight_pack(scale, me_ref, pgrad_ref, coarse_ref, keep_ref, send_ref):
    half = pgrad_ref.shape[1] // 2
    piece = keep_ref.shape[2]
    at = pl.multiple_of(me_ref[1] * half, half)
    values = dot(coarse_ref[...].T, pgrad_ref[:, pl.ds(at, half)]) * scale
    place_pieces(me_ref, lambda d: small_pieces(values, d, piece, 0), keep_ref, send_ref)


def placed(me_ref, place_ref, before, after):
    rim = before.shape[0]
    from_after = dot(place_ref[:, 0:rim], after)
    from_before = dot(place_ref[:, rim:], before)
    return jnp.where(me_ref[0] < me_ref[4] - 1, from_after, 0.0) + jnp.where(me_ref[0] >= 1, from_before, 0.0)


def k_cgrad(me_ref, comb_ref, place_ref, hott_ref, near_ref, one_ref, one2_ref, two_ref, two2_ref,
            three_ref, three2_ref, hits_ref, icount_ref, cpre_ref, cw_ref,
            lg_ref, pgrad_ref, spread_ref, out1_ref, out2_ref):
    cap = out1_ref.shape[0]
    rim = place_ref.shape[1] // 2
    sub, domain, count = me_ref[1], me_ref[0], me_ref[4]
    hits = hits_ref[...]
    lg = comb_ref[...] + placed(me_ref, place_ref, *directed(sub, one_ref, one2_ref, slice(0, rim)))
    lg = lg.astype(BF)
    lg_ref[...] = lg

    def pieces(own_ref, other_ref, start, there=None):
        both = directed(sub, own_ref, other_ref, slice(start, start + cap))
        both = [v.astype(F32) for v in both]
        if there is None:
            return both
        return [jnp.where(ok, v, 0.0) for ok, v in zip(there, both)]

    near = pieces(one_ref, one2_ref, rim)
    near_rim = pieces(two_ref, two2_ref, cap, (domain >= 2, domain < count - 2))
    far = pieces(two_ref, two2_ref, 0)
    far_rim = pieces(one_ref, one2_ref, rim + cap)
    far_rim3 = pieces(three_ref, three2_ref, 0, (domain >= 3, domain < count - 3))
    arrived = [near[c] + near_rim[c] + near_ref[c * cap:(c + 1) * cap, :] for c in range(2)]
    arrived += [far[c] + far_rim[c] + far_rim3[c] for c in range(2)]
    arrived = jnp.concatenate(arrived, axis=0).astype(BF)
    total = dot(hott_ref[...], lg) + dot(hits.astype(BF), arrived)
    pgrad = (total * slope_of(cpre_ref[...])).astype(BF)
    pgrad_ref[...] = pgrad
    spread = (dot(pgrad, cw_ref[...]) * wide(icount_ref[...], pgrad.shape[1])).astype(BF)
    spread_ref[...] = spread
    ans = dot(hits.T.astype(BF), spread).astype(BF)
    out1_ref[...] = jnp.where(sub == 0, ans[cap:2 * cap], ans[0:cap])
    out2_ref[...] = jnp.where(sub == 0, ans[3 * cap:], ans[2 * cap:3 * cap])


def k_cweight(scale, me_ref, pgrad_ref, coarse_ref, out_ref):
    half = out_ref.shape[0]
    at = pl.multiple_of(me_ref[1] * half, half)
    out_ref[...] = dot(pgrad_ref[:, pl.ds(at, half)].T, coarse_ref[...]) * scale


def k_third(me_ref, lg_ref, hot_ref, slott_ref, spread_ref, got_ref,
            wo_ref, slope_ref, win_ref, inv_ref, adjt_ref, *rest, scale=None):
    fb_ref, pg_ref, scaled_ref, msg_ref = rest if scale is None else rest[3:7]
    cap = got_ref.shape[1] // 2
    fb = spread_back(
        lg_ref[...], hot_ref, slott_ref, spread_ref[...],
        (got_ref[0, 0:cap], got_ref[1, 0:cap]), (got_ref[0, cap:], got_ref[1, cap:]))
    fb_ref[...] = fb
    pg = (dot(fb, wo_ref[...]) * slope_ref[...]).astype(BF)
    pg_ref[...] = pg
    if scale is not None:
        xc_ref, agg_ref, hid_ref = rest[:3]
        pack_grads(scale, me_ref, pg_ref, xc_ref, agg_ref, fb_ref, hid_ref, rest[7], rest[8])
    rim_grads(me_ref[1], pg, win_ref, inv_ref, adjt_ref, scaled_ref, msg_ref)


def k_last(me_ref, fb_ref, pg_ref, win_ref, scaled_ref, adjt_ref, rims_ref, place_ref, new_ref, *rest):
    n, width = fb_ref.shape
    half = width // 2
    cols = pl.ds(pl.multiple_of(me_ref[1] * half, half), half)
    grad_ref, out_ref = rest[-2:]
    total = (
        fb_ref[:, cols].astype(F32)
        + dot(pg_ref[...], win_ref[:, cols])
        + dot(adjt_ref[0:n, :], scaled_ref[:, cols])
        + placed(me_ref, place_ref, rims_ref[0, :, cols], rims_ref[1, :, cols])
    )
    grad_ref[...] = total.T
    out_ref[...] = new_ref[:, cols].T
    if len(rest) > 2:
        k_sum(*rest[:-2])


def k_stage(me_ref, *refs):
    pairs = (len(refs) - 4) // 2
    own_ref, outs = refs[2 * pairs], refs[2 * pairs + 1:]
    z = me_ref[3]
    row = 0
    for i in range(pairs):
        keep_ref, got_ref = refs[2 * i], refs[2 * i + 1]
        rows = slice(row, row + keep_ref.shape[1])
        own_ref[rows, :] = keep_ref[z] + got_ref[z].astype(F32)
        for step in (1, 2, 3):
            other = z ^ step
            outs[step - 1][rows, :] = (keep_ref[other] + got_ref[other].astype(F32)).astype(BF)
        row += keep_ref.shape[1]


def unpack_small(total):
    small = total.shape[0] // 2
    return jnp.concatenate([total[0:small], total[small:]], axis=1)


def k_sum(own_ref, a_ref, b_ref, c_ref, ein_ref, eout_ref, gco_ref):
    half = ein_ref.shape[0]
    mid = half + 2 * eout_ref.shape[0]
    total = own_ref[...] + a_ref[...].astype(F32) + b_ref[...].astype(F32) + c_ref[...].astype(F32)
    ein_ref[...] = total[0:half]
    eout_ref[...] = unpack_small(total[half:mid])
    gco_ref[...] = unpack_small(total[mid:])


def k_sum_late(own_ref, a_ref, b_ref, c_ref, ein_ref, eout_ref, gin_ref, gout_ref):
    half = ein_ref.shape[0]
    total = own_ref[...] + a_ref[...].astype(F32) + b_ref[...].astype(F32) + c_ref[...].astype(F32)
    gin_ref[0] = total[0:half]
    gin_ref[1] = ein_ref[...]
    gout_ref[0] = unpack_small(total[half:])
    gout_ref[1] = eout_ref[...]


def local(node_features, inward_weight, outward_weight, coarse_weight, tile_index, tile_mask,
          send_rows, parent, cotangent):
    half, n = node_features.shape
    width = 2 * half
    blocks, k_slots = tile_index.shape
    rim = tile_mask.shape[2]
    src_rows = (blocks + 2) * rim
    domains = lax.axis_size(DOM)
    cross = lax.axis_size("cross")
    curve = lax.axis_size("curve")
    cap = n // 16
    nodes = n // 4
    slots = 4 * cap
    hidden = 2 * inward_weight.shape[1]
    scale = float(n * domains) ** -0.5
    me = jnp.stack(
        [lax.axis_index(a) for a in (DOM, "sub", "cross", "curve")] + [jnp.int32(domains)]).astype(I32)
    rows = send_rows[0]
    packed = cross == 2 and curve == 4 and 2 * width == 1024 and hidden == width

    cell_bf, cell_f32 = sds((n, width), BF), sds((n, width), F32)
    rim_a, rim_b = call(k_halo, [sds((rim, half), BF)] * 2, [me], [rows, node_features], "halo")
    rim_a, rim_b = two_way(rim_a, 1), two_way(rim_b, 1, forward=1)
    win2, wout2 = swap(inward_weight), swap(outward_weight)
    x_full = gather(node_features).reshape(width, n)
    (xc, adj, adjt, inv, hott, hot, slot, slott, pick, place, tags, ocount, rsel) = call(
        k_prep,
        [cell_bf, sds((n, src_rows), BF), sds((src_rows, n), BF), sds((n, 128), F32), sds((nodes, n), BF),
         sds((n, nodes), BF), sds((slots, n), BF), sds((n, slots), BF), sds((2 * rim, n), BF),
         sds((n, 2 * rim), BF), sds((16, slots), BF), sds((nodes, 128), F32), sds((cap, width), BF)],
        [tile_index, me], [tile_mask, rows, parent[None, :], x_full], "prep")
    weight_outs = [sds((hidden, 2 * width), BF), sds((width, hidden), BF)]
    win0, wo0 = call(lambda *r: k_weights(0, *r), weight_outs, [me],
                     [inward_weight, outward_weight, win2, wout2], "weights0")
    rim_a, rim_b, win0, adj = lax.optimization_barrier((rim_a, rim_b, win0, adj))
    msg = sds((cap + 16, width), BF)
    plain = sds((cap, width), BF)
    hid_bf, hid_f32 = sds((n, hidden), BF), sds((n, hidden), F32)
    agg0, pre0, hid0, first, one, two = call(
        k_first,
        [cell_bf, hid_f32, hid_bf, cell_bf, sds((2 * cap + 16, width), BF), msg],
        [me], [xc, *shared(rim_a, rim_b), adj, inv, win0, wo0, slot, tags, rsel], "first",
        flops=2 * n * width * (src_rows + 3 * width),
        scratch=[pltpu.VMEM((src_rows, width), BF)])
    one, two, win2, coarse_weight = lax.optimization_barrier((one, two, win2, coarse_weight))
    one, two = two_way(one, 1), two_way(two, 2)
    rim_bf = sds((rim, width), BF)
    own, slope0, cw, rims, psel = call(
        k_own, [sds((nodes, width), F32), hid_f32, sds((width, width), BF), rim_bf, sds((rim, nodes), BF)], [me],
        [hott, first, pre0, coarse_weight, swap(coarse_weight), pick, hot], "own")
    win1, wo1 = call(lambda *r: k_weights(1, *r), weight_outs, [me],
                     [inward_weight, outward_weight, win2, wout2], "weights1")
    one, two, own = lax.optimization_barrier((one, two, own))
    got = shared(one, two)
    node_bf, node_f32 = sds((nodes, width), BF), sds((nodes, width), F32)
    pair, rim_msg = sds((2 * cap, width), BF), sds((rim + 2 * cap, width), BF)
    hits, icount, coarse, cpre, corr, near, one, two, three, rsb, rsa = call(
        k_coarse,
        [sds((nodes, slots), F32), sds((nodes, 128), F32), node_bf, node_f32, node_bf, pair, rim_msg, pair, plain]
        + [sds((slots, rim), BF)] * 2,
        [me], [own, ocount, *got, cw, rims, psel], "coarse")
    one, two, three, cotangent = lax.optimization_barrier((one, two, three, cotangent))
    one, two, three = two_way(one, 1), two_way(two, 2), two_way(three, 3)
    ctc, hg1 = call(k_cot, [cell_bf, hid_f32], [me], [cotangent, swap(cotangent), wo1], "cot")
    one, two, three, win1, hg1 = lax.optimization_barrier((one, two, three, win1, hg1))
    got = shared(one, two, three)
    lifted, agg1, hid1, new, pg1, comb1, near, one, two, three = call(
        k_second,
        [cell_bf, cell_bf, hid_bf, cell_bf, hid_bf, cell_f32, sds((2 * cap, width), F32), rim_msg, pair, plain],
        [me],
        [first, hot, slott, corr, near, *got, adj, adjt, inv, win1, wo1, hg1, ctc, slot, rsb, rsa], "second",
        scratch=[pltpu.VMEM((src_rows, width), BF)])
    one, two, three = two_way(one, 1), two_way(two, 2), two_way(three, 3)
    piece = 2 * width // domains
    small = hidden // domains
    layer_rows = half + 2 * small
    pack = [sds((curve, layer_rows, piece), F32), sds((curve, layer_rows, piece), BF)]
    if packed:
        keep1, send1 = call(
            lambda *r: pack_grads(scale, *r), pack, [me], [pg1, lifted, agg1, ctc, hid1], "grads1")
        got1 = cross_swap(send1)
        one, two, three, keep1 = lax.optimization_barrier((one, two, three, keep1))
    got = shared(one, two, three)
    lg, pgrad, spread, one, two = call(
        k_cgrad, [cell_bf, node_bf, node_bf, plain, plain], [me],
        [comb1, place, hott, near, *got, hits, icount, cpre, cw], "cgrad")
    one, two = two_way(one, 1), two_way(two, 2)
    if packed:
        keepc, sendc = call(
            lambda *r: k_cweight_pack(scale, *r),
            [sds((curve, 2 * small, piece), F32), sds((curve, 2 * small, piece), BF)], [me],
            [pgrad, coarse], "cweight")
        gotc = cross_swap(sendc)
    got = gather(jnp.concatenate([one, two], axis=0))
    back_outs = [cell_bf, hid_bf, cell_bf, sds((rim, width), BF)]
    if packed:
        got, got1 = lax.optimization_barrier((got, got1))
    if packed:
        fb, pg0, scaled0, rims, keep0, send0 = call(
            lambda *r: k_third(*r, scale=scale), back_outs + pack, [me],
            [lg, hot, slott, spread, got, wo0, slope0, win0, inv, adjt, xc, agg0, hid0], "third")
        send0, gotc = lax.optimization_barrier((send0, gotc))
        got0 = cross_swap(send0)
        keepc, pg0 = lax.optimization_barrier((keepc, pg0))
        rims = two_way(rims, 1)

        def staged(pairs, name):
            total = sum(keep.shape[1] for keep in pairs[::2])
            own, *outs = call(
                k_stage, [sds((total, piece), F32)] + [sds((total, piece), BF)] * 3, [me], pairs, name)
            return [own] + [curve_swap(value, step) for step, value in zip((1, 2, 3), outs)]

        early = staged([keep1, got1, keepc, gotc], "stage1")
        late = staged([keep0, got0], "stage0")
    else:
        gco, = call(lambda *r: k_cweight(scale, *r), [sds((half, width), F32)], [me], [pgrad, coarse], "cweight")
        fb, pg0, scaled0, rims = call(
            k_third, back_outs, [me], [lg, hot, slott, spread, got, wo0, slope0, win0, inv, adjt], "third")
        rims = two_way(rims, 1)
    last_args = [fb, pg0, win0, scaled0, adjt, gather(rims), place, new]
    last_outs = [sds((half, n), F32), sds((half, n), BF)]
    if packed:
        ein, eout, gco, fgrad, new_t = call(
            k_last, [sds((half, piece), F32), sds((small, half), F32), sds((small, half), F32)] + last_outs,
            [me], last_args + early, "last")
        gin, gout = call(
            k_sum_late, [sds((2, half, piece), F32), sds((2, small, half), F32)], [], late + [ein, eout], "late")
        gout = gout.swapaxes(1, 2)
        gco = gco.T
    else:
        fgrad, new_t = call(k_last, last_outs, [me], last_args, "last")
        shapes = [sds((half, 2 * width), F32), sds((half, hidden), F32)]
        gi1, go1 = call(lambda *r: k_grads(scale, *r), shapes, [me], [pg1, lifted, agg1, ctc, hid1], "grads1")
        gi0, go0 = call(lambda *r: k_grads(scale, *r), shapes, [me], [pg0, xc, agg0, fb, hid0], "grads0")
        gin = lax.psum_scatter(jnp.stack([gi0, gi1]), DOM, scatter_dimension=2, tiled=True)
        gout = lax.psum_scatter(jnp.stack([go0, go1]), DOM, scatter_dimension=2, tiled=True)
        gco = lax.psum_scatter(gco, DOM, scatter_dimension=1, tiled=True)
    return new_t, fgrad, gin, gout, gco


def solution(mesh):
    cells = ("groups", "curve", "cross")
    in_specs = (
        P("sub", cells),
        P(None, "sub", None),
        P(None, "sub", None),
        P("sub", None),
        P(cells, None),
        P(cells, None, None, None),
        P(cells, None, None),
        P(cells),
        P("sub", cells),
    )
    out_specs = (
        P("sub", cells),
        P("sub", cells),
        P("groups", "sub", ("curve", "cross")),
        P("groups", "sub", ("curve", "cross")),
        P(("groups", "sub"), ("curve", "cross")),
    )
    return jax.shard_map(local, mesh=mesh, in_specs=in_specs, out_specs=out_specs, check_vma=False)
```
